128 devices in a mesh: freq: 4 (over x), tile: 32 (over y, z, core).
Axes of the slice: x: 4, y: 4, z: 4, core: 2. Of those that a mesh axis runs over, the one named last changes fastest.
Arguments:
- voltages: bfloat16 [4096, 98688], P(('freq', 'tile')), may hold values from -16 to 16, as said below
- channel_ids: int32 [12], replicated, may hold values from 1 to 63
- start_basis: float32 [2, 8, 4096], replicated, may hold values from -0.0625 to 0.0625
Outputs:
- cleaned: float32 [2, 12, 768, 4096], P(None, 'freq', 'tile')
The draws below stay inside these ranges and needn't reach their ends.
Inputs may be any that keep to these rules, and one draw needn't show every extreme that they name: `voltages`: real samples of each input over the whole window.
All inputs are finite; a program needn't handle non-finite values.
Results may differ from the reference program's by a relative error of at most 0.0048.
Values may be sent and summed in bfloat16 or wider, within the bound.
No kernel may reach another device: no remote copies, remote signals or barrier semaphores. Data moves between devices by JAX's collectives and lax.ppermute only.
A program may use at most 128 MiB of HBM per device.

```python
import math
import jax
import jax.numpy as jnp
from jax import lax

INPUTS = 4096
TAPS = 4
P_SIZE = 128
KDIM = 8
ITERS = 3
CHANNELS = 12
SPECTRA = 768
SAMPLES = 98688


highest = lax.Precision.HIGHEST


def draw_voltages(key, part):
    key_gain = jax.random.fold_in(key, 11)
    key_signal = jax.random.fold_in(key, 12)
    key_power = jax.random.fold_in(key, 13)
    key_noise = jax.random.fold_in(key, 14)
    sources = KDIM + 2
    powers = jnp.exp(jax.random.uniform(key_power, (sources,), jnp.float32, math.log(0.001), math.log(0.2)))
    time_frac = jnp.arange(SAMPLES, dtype=jnp.float32) / SAMPLES
    envelope = 0.6 + 1.2 * time_frac
    signals = jax.random.normal(key_signal, (sources, SAMPLES), jnp.float32) * jnp.sqrt(powers)[:, None] * envelope[None, :]
    gain_table = jax.random.normal(key_gain, (INPUTS, sources), jnp.float32)
    block_rows = min(INPUTS, 128)
    block_count = INPUTS // block_rows

    def one_block(block_at):
        first_row = block_at * block_rows
        gain_rows = lax.dynamic_slice_in_dim(gain_table, first_row, block_rows, 0)
        fraction = (first_row + jnp.arange(block_rows, dtype=jnp.int32)).astype(jnp.float32) / INPUTS
        noise_key = jax.random.fold_in(key_noise, block_at)
        noise_draw = jax.random.normal(noise_key, (block_rows, SAMPLES), jnp.float32)
        amplitude = 0.5 + fraction
        combined = amplitude[:, None] * (noise_draw + jnp.dot(gain_rows, signals, precision=highest))
        return jnp.clip(combined, -16.0, 16.0).astype(jnp.bfloat16)
    blocks = lax.map(one_block, jnp.arange(block_count, dtype=jnp.int32))
    return blocks.reshape(INPUTS, SAMPLES)


def place_ends(drawn, rng, low, top_value):
    longest = drawn.shape.index(max(drawn.shape))
    spots = []
    for shift in (0, 1):
        where = [jax.random.randint(jax.random.fold_in(rng, axis), (), 0, length) for axis, length in enumerate(drawn.shape)]
        where[longest] = (where[longest] + shift) % drawn.shape[longest]
        spots.append(tuple(where))
    return drawn.at[spots[0]].set(low).at[spots[1]].set(top_value)


def centred(rng, shape, spread, limit, kind=jnp.bfloat16):
    values = jax.random.normal(rng, shape, jnp.float32) * spread
    return jnp.minimum(jnp.maximum(values, -limit), limit).astype(kind)


def setup_inputs(seed: int = 0) -> dict:
    seeds = jax.random.split(jax.random.key(seed), 4)
    voltages = draw_voltages(jax.random.fold_in(seeds[3], 71), 0)
    channel_ids = place_ends(jax.random.randint(seeds[1], (CHANNELS,), 1, P_SIZE // 2), jax.random.fold_in(seeds[1], 1), 1, (P_SIZE // 2) - 1).astype(jnp.int32)
    start_basis = centred(seeds[2], (2, KDIM, INPUTS), (2 * INPUTS) ** -0.5, 0.0625, jnp.float32)
    return dict(voltages=voltages, channel_ids=channel_ids, start_basis=start_basis)


loading = 0.5
highest = lax.Precision.HIGHEST

def make_table(channel_ids, taps_count, points):
    length = taps_count * points
    offsets = jnp.arange(length, dtype=jnp.float32)
    shifted = (offsets + 0.5 - length / 2.0) / points
    window = jnp.sinc(shifted) * (0.5 - 0.5 * jnp.cos(2.0 * math.pi * (offsets + 0.5) / length))
    window = window / jnp.sqrt(jnp.sum(window * window))
    window = window.reshape(taps_count, points)
    phases = channel_ids[:, None] * jnp.arange(points, dtype=jnp.int32)[None, :] % points
    angles = 2.0 * math.pi / points * phases.astype(jnp.float32)
    rotors = jnp.stack([jnp.cos(angles), -jnp.sin(angles)])
    return (window[:, None, None, :] * rotors[None]).astype(jnp.bfloat16)

def channelize(voltages, coeffs):
    block_rows = min(INPUTS, 128)
    block_count = INPUTS // block_rows
    filter_table = coeffs.astype(jnp.float32)

    def one_block(first_row):
        chosen = lax.dynamic_slice_in_dim(voltages, first_row, block_rows, 0)
        frames = chosen.reshape(block_rows, SPECTRA + TAPS - 1, P_SIZE).astype(jnp.float32)
        summed = jnp.zeros((2, CHANNELS, SPECTRA, block_rows), jnp.float32)
        for offset in range(TAPS):
            summed = summed + jnp.einsum('rcp,isp->rcsi', filter_table[offset], frames[:, offset:offset + SPECTRA, :], precision=highest)
        return summed.astype(jnp.bfloat16)
    starts = (jnp.arange(block_count) * block_rows).astype(jnp.int32)
    stacked = lax.map(one_block, starts)
    return jnp.transpose(stacked, (1, 2, 3, 0, 4)).reshape(2, CHANNELS, SPECTRA, INPUTS)

def contract(form, left, right):
    return jnp.einsum(form, left, right, precision=highest)

def image_of(values, basis):
    real_v, imag_v = (values[0], values[1])
    real_q, imag_q = (basis[0], basis[1])
    weight_re = contract('csi,cki->csk', real_v, real_q) + contract('csi,cki->csk', imag_v, imag_q)
    weight_im = contract('csi,cki->csk', real_v, imag_q) - contract('csi,cki->csk', imag_v, real_q)
    image_re = contract('csi,csk->cki', real_v, weight_re) - contract('csi,csk->cki', imag_v, weight_im)
    image_im = contract('csi,csk->cki', real_v, weight_im) + contract('csi,csk->cki', imag_v, weight_re)
    return jnp.stack([image_re, image_im])

def gram_parts(image):
    real_z, imag_z = (image[0], image[1])
    gram_re = contract('cki,cji->ckj', real_z, real_z) + contract('cki,cji->ckj', imag_z, imag_z)
    gram_im = contract('cki,cji->ckj', real_z, imag_z) - contract('cki,cji->ckj', imag_z, real_z)
    return (gram_re, gram_im)

def lower_factor(gram_re, gram_im):
    basis_width = gram_re.shape[-1]
    lower_re = {}
    lower_im = {}
    pivots = []
    for column in range(basis_width):
        pivot_square = gram_re[:, column, column]
        for earlier in range(column):
            pivot_square = pivot_square - lower_re[column, earlier] ** 2 - lower_im[column, earlier] ** 2
        pivot_value = jnp.sqrt(pivot_square)
        pivots.append(pivot_value)
        for row_at in range(column + 1, basis_width):
            value_re = gram_re[:, row_at, column]
            value_im = gram_im[:, row_at, column]
            for earlier in range(column):
                left_re, left_im = (lower_re[row_at, earlier], lower_im[row_at, earlier])
                right_re, right_im = (lower_re[column, earlier], lower_im[column, earlier])
                value_re = value_re - (left_re * right_re + left_im * right_im)
                value_im = value_im - (left_im * right_re - left_re * right_im)
            lower_re[row_at, column] = value_re / pivot_value
            lower_im[row_at, column] = value_im / pivot_value
    return (lower_re, lower_im, pivots)

def apply_factor(image, lower_re, lower_im, pivots):
    basis_width = image.shape[2]
    result_re = []
    result_im = []
    for column in range(basis_width):
        value_re = image[0, :, column, :]
        value_im = image[1, :, column, :]
        for earlier in range(column):
            left_re, left_im = (result_re[earlier], result_im[earlier])
            right_re = lower_re[column, earlier][:, None]
            right_im = lower_im[column, earlier][:, None]
            value_re = value_re - (left_re * right_re + left_im * right_im)
            value_im = value_im - (left_im * right_re - left_re * right_im)
        divisor = pivots[column][:, None]
        result_re.append(value_re / divisor)
        result_im.append(value_im / divisor)
    return jnp.stack([jnp.stack(result_re, axis=1), jnp.stack(result_im, axis=1)])

def remove_subspace(values, basis):
    real_v, imag_v = (values[0], values[1])
    real_q, imag_q = (basis[0], basis[1])
    coord_re = contract('cki,csi->cks', real_q, real_v) + contract('cki,csi->cks', imag_q, imag_v)
    coord_im = contract('cki,csi->cks', real_q, imag_v) - contract('cki,csi->cks', imag_q, real_v)
    fitted_re = contract('cki,cks->csi', real_q, coord_re) - contract('cki,cks->csi', imag_q, coord_im)
    fitted_im = contract('cki,cks->csi', real_q, coord_im) + contract('cki,cks->csi', imag_q, coord_re)
    return values - jnp.stack([fitted_re, fitted_im])

def reference(voltages, channel_ids, start_basis):
    coeffs = make_table(channel_ids, TAPS, P_SIZE)
    spectra = channelize(voltages, coeffs)
    values = spectra.astype(jnp.float32)
    basis = jnp.broadcast_to(start_basis[:, None], (2, CHANNELS, KDIM, INPUTS))
    for step_at in range(ITERS):
        image = image_of(values, basis) / SPECTRA + loading * basis
        gram_re, gram_im = gram_parts(image)
        lower_re, lower_im, pivots = lower_factor(gram_re, gram_im)
        basis = apply_factor(image, lower_re, lower_im, pivots)
    return remove_subspace(values, basis)
```

```python
import functools
import math

import jax
import jax.numpy as jnp
from jax import lax
from jax.experimental import pallas as pl
from jax.experimental.pallas import tpu as pltpu
from jax.sharding import Mesh, PartitionSpec as P

TAPS = 4
P_SIZE = 128
INPUTS = 4096
KDIM = 8
CHANNELS = 12
SPECTRA = 768
LOADING = 0.5

NX, NY, NZ, NC = 4, 4, 4, 2
LOCAL = INPUTS // (NX * NY * NZ * NC)
GROUP = CHANNELS // NX
HELD = LOCAL * NX * NZ
PHASES = 6
ROWS = SPECTRA // PHASES
SPAN = (PHASES + TAPS - 1) * P_SIZE
SHARE = SPECTRA // (NY * NZ * NC)
RC = 2 * CHANNELS

F32, BF16 = jnp.float32, jnp.bfloat16
VMEM_LIMIT = 56 * 1024 * 1024
params = pltpu.CompilerParams(vmem_limit_bytes=VMEM_LIMIT)
in_vmem = pl.BlockSpec(memory_space=pltpu.VMEM)


def dot_nn(a, b):
    return lax.dot_general(a, b, (((1,), (0,)), ((), ())), preferred_element_type=F32)


def dot_nt(a, b):
    return lax.dot_general(a, b, (((1,), (1,)), ((), ())), preferred_element_type=F32)


def dot_tn(a, b, precision=None):
    return lax.dot_general(
        a, b, (((0,), (0,)), ((), ())), preferred_element_type=F32, precision=precision
    )


def split3(x):
    hi = x.astype(BF16)
    rest = x - hi.astype(F32)
    mid = rest.astype(BF16)
    lo = (rest - mid.astype(F32)).astype(BF16)
    return jnp.concatenate([hi, mid, lo], axis=0)


def sum3(x):
    n = x.shape[0] // 3
    return x[:n] + (x[n : 2 * n] + x[2 * n :])


def make_table(channel_ids):
    length = TAPS * P_SIZE
    offsets = jnp.arange(length, dtype=F32)
    shifted = (offsets + 0.5 - length / 2.0) / P_SIZE
    window = jnp.sinc(shifted) * (0.5 - 0.5 * jnp.cos(2.0 * math.pi * (offsets + 0.5) / length))
    window = window / jnp.sqrt(jnp.sum(window * window))
    window = window.reshape(TAPS, P_SIZE)
    phases = channel_ids[:, None] * jnp.arange(P_SIZE, dtype=jnp.int32)[None, :] % P_SIZE
    angles = 2.0 * math.pi / P_SIZE * phases.astype(F32)
    rotors = jnp.stack([jnp.cos(angles), -jnp.sin(angles)])
    return (window[:, None, None, :] * rotors[None]).astype(BF16)


def banded_table(channel_ids):
    columns = jnp.transpose(make_table(channel_ids), (0, 3, 1, 2)).reshape(TAPS * P_SIZE, RC)
    parts = [
        jnp.pad(columns, ((q * P_SIZE, (PHASES - 1 - q) * P_SIZE), (0, 0))) for q in range(PHASES)
    ]
    parts.append(jnp.zeros((SPAN, 256 - PHASES * RC), BF16))
    return jnp.concatenate(parts, axis=1)


STEP_ROWS = 8


def channelize_kernel(x_ref, c_ref, o_ref, wide, tall):
    def filter_rows(at, carry):
        rows = []
        for k in range(STEP_ROWS):
            start = pl.multiple_of((at * STEP_ROWS + k) * (PHASES * P_SIZE), 128)
            rows.append(x_ref[:, pl.ds(start, SPAN)])
        got = dot_nn(jnp.concatenate(rows, axis=0), c_ref[...])
        wide[pl.ds(at * STEP_ROWS, STEP_ROWS)] = got.reshape(STEP_ROWS, LOCAL, 256)
        return carry

    lax.fori_loop(0, ROWS // STEP_ROWS, filter_rows, 0)

    for n in range(LOCAL):
        turned = jnp.concatenate(
            [wide[:, n, 0:128].T, wide[:, n, 128:256].T[0 : PHASES * RC - 128]], axis=0
        )
        for q in range(PHASES):
            tall[:, n, q * 128 : (q + 1) * 128] = turned[q * RC : (q + 1) * RC]

    for x in range(NX):
        for z in range(NZ):
            for r in range(2):
                if z < GROUP:
                    o_ref[x * NZ + z, r] = tall[r * CHANNELS + x * GROUP + z].astype(BF16)
                else:
                    o_ref[x * NZ + z, r] = jnp.zeros((LOCAL, SPECTRA), BF16)


def channelize(x, table):
    return pl.pallas_call(
        channelize_kernel,
        out_shape=jax.ShapeDtypeStruct((NX * NZ, 2, LOCAL, SPECTRA), BF16),
        in_specs=[in_vmem] * 2,
        out_specs=in_vmem,
        scratch_shapes=[
            pltpu.VMEM((ROWS, LOCAL, 256), F32),
            pltpu.VMEM((RC, LOCAL, SPECTRA), F32),
        ],
        compiler_params=params,
    )(x, table)


def halves(v_ref):
    return v_ref[:, 0].reshape(HELD, SPECTRA), v_ref[:, 1].reshape(HELD, SPECTRA)


def turn_kernel(v_ref, o_ref):
    row = lax.broadcasted_iota(jnp.int32, (SPECTRA, SPECTRA), 0)
    col = lax.broadcasted_iota(jnp.int32, (SPECTRA, SPECTRA), 1)
    pick = jnp.where(row == (col % ROWS) * PHASES + col // ROWS, 1.0, 0.0).astype(BF16)
    real_v, imag_v = halves(v_ref)
    real_t, imag_t = dot_nt(pick, real_v), dot_nt(pick, imag_v)
    for t in range(NY * NZ * NC):
        rows = slice(t * SHARE, (t + 1) * SHARE)
        o_ref[t] = jnp.concatenate([real_t[rows], imag_t[rows]], axis=0).astype(BF16)


def turn(v):
    return pl.pallas_call(
        turn_kernel,
        out_shape=jax.ShapeDtypeStruct((NY * NZ * NC, 2 * SHARE, HELD), BF16),
        in_specs=[in_vmem],
        out_specs=in_vmem,
        compiler_params=params,
    )(v)


def project(v_halves, pieces):
    a, b = sum3(dot_nn(pieces, v_halves[0])), sum3(dot_nn(pieces, v_halves[1]))
    return a[0:KDIM] + b[KDIM:], a[KDIM:] - b[0:KDIM]


def expand(v_halves, pieces):
    a, b = sum3(dot_nt(pieces, v_halves[0])), sum3(dot_nt(pieces, v_halves[1]))
    return a[0:KDIM] - b[KDIM:], a[KDIM:] + b[0:KDIM]


def gram_from(products):
    p0, p1, p2 = products[0:16], products[16:32], products[32:48]
    m = (p0 + (p1 + p2)) + pltpu.roll(p0 + p1, 112, 1) + pltpu.roll(p0, 96, 1)
    up, down = m[0:KDIM], m[KDIM:]
    return up + pltpu.roll(down, 120, 1), down - pltpu.roll(up, 120, 1)


def eliminate(gram, others):
    row_id = lax.broadcasted_iota(jnp.int32, (KDIM, 1), 0)
    gram_re, gram_im = gram
    pairs = [(gram_re, gram_im)] + list(others)
    for j in range(KDIM):
        gram_re, gram_im = pairs[0]
        scale = 1.0 / jnp.sqrt(gram_re[j : j + 1, j : j + 1])
        below = jnp.where(row_id > j, scale, 0.0)
        m_re, m_im = gram_re[:, j : j + 1] * below, gram_im[:, j : j + 1] * below
        done = []
        for re, im in pairs:
            top_re, top_im = re[j : j + 1] * scale, im[j : j + 1] * scale
            new_re = re - (m_re * top_re - m_im * top_im)
            new_im = im - (m_re * top_im + m_im * top_re)
            here = row_id == j
            done.append((jnp.where(here, top_re, new_re), jnp.where(here, top_im, new_im)))
        pairs = done
    return pairs


def first_kernel(v_ref, q_ref, s_ref):
    u_re, u_im = project(halves(v_ref), split3(q_ref[...]))
    s_ref[...] = jnp.concatenate([u_re, u_im], axis=0)


def step_kernel(step, v_ref, z_ref, s0, s1, s2, s3, *outs):
    s = (s0[...] + s2[...]) + (s1[...] + s3[...])
    w = (s[0:KDIM, 0:SPECTRA], s[KDIM:, 0:SPECTRA])
    q = (z_ref[0:KDIM], z_ref[KDIM:])
    if step > 0:
        gram = (s[0:KDIM, SPECTRA:], s[KDIM:, SPECTRA:])
        _, w, q = eliminate(gram, [w, q])
    v = halves(v_ref)
    i_re, i_im = expand(v, split3(jnp.concatenate(w, axis=0)))
    z_re = i_re * (1.0 / SPECTRA) + LOADING * q[0]
    z_im = i_im * (1.0 / SPECTRA) + LOADING * q[1]
    z = jnp.concatenate([z_re, z_im], axis=0)
    if step == 2:
        (many_ref,) = outs
        for d in range(NY * NZ):
            many_ref[d] = z
        return
    new_z, new_s = outs
    new_z[...] = z
    pieces = split3(z)
    u_re, u_im = project(v, pieces)
    padded = jnp.concatenate([pieces, jnp.zeros((80, HELD), BF16)], axis=0)
    g_re, g_im = gram_from(dot_nt(pieces, padded))
    new_s[0:KDIM, 0:SPECTRA] = u_re
    new_s[KDIM:, 0:SPECTRA] = u_im
    new_s[0:KDIM, SPECTRA:] = g_re
    new_s[KDIM:, SPECTRA:] = g_im


def first(v, q):
    return pl.pallas_call(
        first_kernel,
        out_shape=jax.ShapeDtypeStruct((2 * KDIM, SPECTRA), F32),
        in_specs=[in_vmem] * 2,
        out_specs=in_vmem,
        compiler_params=params,
    )(v, q)


def step(at, v, z, sums):
    if at == 2:
        shapes = [jax.ShapeDtypeStruct((NY * NZ, 2 * KDIM, HELD), F32)]
    else:
        shapes = [
            jax.ShapeDtypeStruct((2 * KDIM, HELD), F32),
            jax.ShapeDtypeStruct((2 * KDIM, SPECTRA + 128), F32),
        ]
    return pl.pallas_call(
        functools.partial(step_kernel, at),
        out_shape=shapes,
        in_specs=[in_vmem] * 6,
        out_specs=[in_vmem] * len(shapes),
        compiler_params=params,
    )(v, z, *sums)


def final_kernel(v_ref, own_ref, far_ref, core_ref, o_ref, flat, basis):
    row = lax.broadcasted_iota(jnp.int32, (256, 256), 0)
    col = lax.broadcasted_iota(jnp.int32, (256, 256), 1)
    source = ((col // 32) % 2) * 128 + (col // 64) * 32 + col % 32
    place = jnp.where(row == source, 1.0, 0.0).astype(BF16)
    lane = lax.broadcasted_iota(jnp.int32, (2 * KDIM, 128), 1) // 32
    is_zero = core_ref[0] == 0
    for x in range(NX):
        lanes = slice(x * 128, (x + 1) * 128)
        rows = []
        for y in range(NY):
            for z in range(GROUP):
                at = (y * NZ + z) * NC
                rows.append(
                    jnp.concatenate([v_ref[at, :, lanes], v_ref[at + 1, :, lanes]], axis=1)
                )
        got = dot_nn(jnp.concatenate(rows, axis=0), place)
        flat[x] = got.reshape(NY, GROUP, 2 * SHARE, 256)
        for y in range(NY):
            for z in range(GROUP):
                own, far = own_ref[y * NZ + z, :, lanes], far_ref[y * NZ + z, :, lanes]
                a, b = jnp.where(is_zero, own, far), jnp.where(is_zero, far, own)
                left = jnp.where(
                    lane < 2,
                    jnp.where(lane == 0, a, pltpu.roll(b, 32, 1)),
                    jnp.where(lane == 2, pltpu.roll(a, 32, 1), pltpu.roll(b, 64, 1)),
                )
                right = jnp.where(
                    lane < 2,
                    jnp.where(lane == 0, pltpu.roll(a, 64, 1), pltpu.roll(b, 96, 1)),
                    jnp.where(lane == 2, pltpu.roll(a, 96, 1), b),
                )
                at = (x * NY + y) * 256
                basis[z, :, at : at + 128] = left
                basis[z, :, at + 128 : at + 256] = right

    lane = lax.broadcasted_iota(jnp.int32, (KDIM, 128), 1)
    unit = lane == lax.broadcasted_iota(jnp.int32, (KDIM, 128), 0) + KDIM
    unit_lanes = (lane >= KDIM) & (lane < 2 * KDIM)
    u_lanes = (lane >= 48) & (lane < 72)
    wide = NY * 256
    for z in range(GROUP):
        products = jnp.zeros((48, 128), F32)
        for x in range(NX):
            pieces = split3(basis[z, :, x * wide : (x + 1) * wide])
            block = jnp.concatenate([flat[x, y, z] for y in range(NY)], axis=1).astype(BF16)
            right = jnp.concatenate([pieces, block, jnp.zeros((32, wide), BF16)], axis=0)
            products = products + dot_nt(pieces, right)
        g_re, g_im = gram_from(products)
        up_down = sum3(products)
        up, down = up_down[0:KDIM], up_down[KDIM:]
        u_re = up + pltpu.roll(down, 104, 1)
        u_im = down - pltpu.roll(up, 104, 1)
        x_re = jnp.where(u_lanes, u_re, jnp.where(unit_lanes, jnp.where(unit, 1.0, 0.0), g_re))
        x_im = jnp.where(u_lanes, u_im, jnp.where(unit_lanes, 0.0, g_im))
        used = lane < 72
        x_re, x_im = jnp.where(used, x_re, 0.0), jnp.where(used, x_im, 0.0)
        ((x_re, x_im),) = eliminate((x_re, x_im), [])
        both = jnp.concatenate([x_re, x_im], axis=0)
        cross = jnp.concatenate([x_im, -x_re], axis=0)
        t_re = dot_tn(both, both, lax.Precision.HIGHEST)[KDIM : 2 * KDIM]
        t_im = dot_tn(cross, both, lax.Precision.HIGHEST)[KDIM : 2 * KDIM]

        def sides(a, b):
            near, away = pltpu.roll(a, 80, 1), pltpu.roll(b, 104, 1)
            return jnp.where(lane < SHARE, near, jnp.where(lane < 2 * SHARE, away, 0.0))

        t = split3(jnp.concatenate([sides(t_re, t_im), sides(-t_im, t_re)], axis=0))
        hi, mid, lo = t[0:16], t[16:32], t[32:48]
        left = jnp.concatenate([hi, hi, hi, mid, mid, lo], axis=0)
        for x in range(NX):
            pieces = split3(basis[z, :, x * wide : (x + 1) * wide])
            right = jnp.concatenate([pieces, pieces[0:32], pieces[0:16]], axis=0)
            fitted = dot_tn(left, right)[0 : 2 * SHARE]
            for y in range(NY):
                rest = flat[x, y, z] - fitted[:, y * 256 : (y + 1) * 256]
                at = x * wide + y * 256
                o_ref[0, z, :, at : at + 256] = rest[0:SHARE]
                o_ref[1, z, :, at : at + 256] = rest[SHARE:]


def finish(v, own, far, core):
    return pl.pallas_call(
        final_kernel,
        out_shape=jax.ShapeDtypeStruct((2, GROUP, SHARE, INPUTS), F32),
        in_specs=[in_vmem] * 3 + [pl.BlockSpec(memory_space=pltpu.SMEM)],
        out_specs=in_vmem,
        scratch_shapes=[
            pltpu.VMEM((NX, NY, GROUP, 2 * SHARE, 256), F32),
            pltpu.VMEM((GROUP, 2 * KDIM, INPUTS), F32),
        ],
        compiler_params=params,
    )(v, own, far, core)


def turned_by(count, distance):
    return [(i, (i + distance) % count) for i in range(count)]


def sums_over(s):
    s = s + lax.ppermute(s, "core", turned_by(NC, 1))
    return [s] + [lax.ppermute(s, "y", turned_by(NY, d)) for d in range(1, NY)]


def body(voltages, channel_ids, start_basis):
    y, core = lax.axis_index("y"), lax.axis_index("core")
    parcels = channelize(voltages, banded_table(channel_ids))
    v = lax.all_to_all(parcels, ("x", "z"), 0, 0, tiled=True)
    split = start_basis.reshape(2 * KDIM, NX, NY, NZ, NC, LOCAL)
    split = lax.dynamic_index_in_dim(split, y, 2, keepdims=False)
    z = lax.dynamic_index_in_dim(split, core, 3, keepdims=False).reshape(2 * KDIM, HELD)
    s = first(v, z)
    sums = sums_over(s)
    blocks = lax.all_to_all(turn(v), ("y", "z", "core"), 0, 0, tiled=True)
    z, s = step(0, v, z, sums)
    z, s = step(1, v, z, sums_over(s))
    (many,) = step(2, v, z, sums_over(s))
    own = lax.all_to_all(many, ("y", "z"), 0, 0, tiled=True)
    far = lax.ppermute(own, "core", turned_by(NC, 1))
    return finish(blocks, own, far, core.reshape(1).astype(jnp.int32))


def solution(mesh):
    fine = Mesh(mesh.devices.reshape(NX, NY, NZ, NC), ("x", "y", "z", "core"))
    in_specs = (P(("x", "y", "z", "core"), None), P(), P())
    out_specs = P(None, "x", ("y", "z", "core"), None)
    return jax.shard_map(body, mesh=fine, in_specs=in_specs, out_specs=out_specs, check_vma=False)
```

```python
import functools
import math

import jax
import jax.numpy as jnp
from jax import lax
from jax.experimental import pallas as pl
from jax.experimental.pallas import tpu as pltpu
from jax.sharding import Mesh, PartitionSpec as P

TAPS = 4
P_SIZE = 128
INPUTS = 4096
KDIM = 8
CHANNELS = 12
SPECTRA = 768
LOADING = 0.5

NX, NY, NZ, NC = 4, 4, 4, 2
LOCAL = INPUTS // (NX * NY * NZ * NC)
GROUP = CHANNELS // NX
HELD = LOCAL * NX * NZ
PHASES = 6
ROWS = SPECTRA // PHASES
SPAN = (PHASES + TAPS - 1) * P_SIZE
SHARE = SPECTRA // (NY * NZ * NC)
RC = 2 * CHANNELS

F32, BF16 = jnp.float32, jnp.bfloat16


def params(mib):
    return pltpu.CompilerParams(vmem_limit_bytes=mib * 1024 * 1024)


def cost(microseconds):
    return pl.CostEstimate(flops=0, bytes_accessed=int(microseconds * 3e6), transcendentals=0)


in_vmem = pl.BlockSpec(memory_space=pltpu.VMEM)


def dot_nn(a, b):
    return lax.dot_general(a, b, (((1,), (0,)), ((), ())), preferred_element_type=F32)


def dot_nt(a, b):
    return lax.dot_general(a, b, (((1,), (1,)), ((), ())), preferred_element_type=F32)


def dot_tn(a, b, precision=None):
    return lax.dot_general(
        a, b, (((0,), (0,)), ((), ())), preferred_element_type=F32, precision=precision
    )


def split3(x):
    hi = x.astype(BF16)
    rest = x - hi.astype(F32)
    mid = rest.astype(BF16)
    lo = (rest - mid.astype(F32)).astype(BF16)
    return jnp.concatenate([hi, mid, lo], axis=0)


def sum3(x):
    n = x.shape[0] // 3
    return x[:n] + (x[n : 2 * n] + x[2 * n :])


def make_table(channel_ids):
    length = TAPS * P_SIZE
    offsets = jnp.arange(length, dtype=F32)
    shifted = (offsets + 0.5 - length / 2.0) / P_SIZE
    window = jnp.sinc(shifted) * (0.5 - 0.5 * jnp.cos(2.0 * math.pi * (offsets + 0.5) / length))
    window = window / jnp.sqrt(jnp.sum(window * window))
    window = window.reshape(TAPS, P_SIZE)
    phases = channel_ids[:, None] * jnp.arange(P_SIZE, dtype=jnp.int32)[None, :] % P_SIZE
    angles = 2.0 * math.pi / P_SIZE * phases.astype(F32)
    rotors = jnp.stack([jnp.cos(angles), -jnp.sin(angles)])
    return (window[:, None, None, :] * rotors[None]).astype(BF16)


def banded_table(channel_ids):
    columns = jnp.transpose(make_table(channel_ids), (0, 3, 1, 2)).reshape(TAPS * P_SIZE, RC)
    parts = [
        jnp.pad(columns, ((q * P_SIZE, (PHASES - 1 - q) * P_SIZE), (0, 0))) for q in range(PHASES)
    ]
    parts.append(jnp.zeros((SPAN, 256 - PHASES * RC), BF16))
    return jnp.concatenate(parts, axis=1)


STEP_ROWS = 8


def channelize_kernel(x_ref, c_ref, o_ref, wide, tall):
    def filter_rows(at, carry):
        rows = []
        for k in range(STEP_ROWS):
            start = pl.multiple_of((at * STEP_ROWS + k) * (PHASES * P_SIZE), 128)
            rows.append(x_ref[:, pl.ds(start, SPAN)])
        got = dot_nn(jnp.concatenate(rows, axis=0), c_ref[...])
        wide[pl.ds(at * STEP_ROWS, STEP_ROWS)] = got.reshape(STEP_ROWS, LOCAL, 256)
        return carry

    lax.fori_loop(0, ROWS // STEP_ROWS, filter_rows, 0)

    for n in range(LOCAL):
        turned = jnp.concatenate(
            [wide[:, n, 0:128].T, wide[:, n, 128:256].T[0 : PHASES * RC - 128]], axis=0
        )
        for q in range(PHASES):
            tall[:, n, q * 128 : (q + 1) * 128] = turned[q * RC : (q + 1) * RC]

    for x in range(NX):
        for z in range(NZ):
            for r in range(2):
                if z < GROUP:
                    o_ref[x * NZ + z, r] = tall[r * CHANNELS + x * GROUP + z].astype(BF16)
                else:
                    o_ref[x * NZ + z, r] = jnp.zeros((LOCAL, SPECTRA), BF16)


def channelize(x, table):
    return pl.pallas_call(
        channelize_kernel,
        out_shape=jax.ShapeDtypeStruct((NX * NZ, 2, LOCAL, SPECTRA), BF16),
        in_specs=[in_vmem] * 2,
        out_specs=in_vmem,
        scratch_shapes=[
            pltpu.VMEM((ROWS, LOCAL, 256), F32),
            pltpu.VMEM((RC, LOCAL, SPECTRA), F32),
        ],
        compiler_params=params(28),
        cost_estimate=cost(8),
    )(x, table)


def halves(v_ref):
    return v_ref[:, 0].reshape(HELD, SPECTRA), v_ref[:, 1].reshape(HELD, SPECTRA)


def turn_kernel(v_ref, o_ref):
    row = lax.broadcasted_iota(jnp.int32, (SPECTRA, SPECTRA), 0)
    col = lax.broadcasted_iota(jnp.int32, (SPECTRA, SPECTRA), 1)
    pick = jnp.where(row == (col % ROWS) * PHASES + col // ROWS, 1.0, 0.0).astype(BF16)
    real_v, imag_v = halves(v_ref)
    real_t, imag_t = dot_nt(pick, real_v), dot_nt(pick, imag_v)
    for t in range(NY * NZ * NC):
        rows = slice(t * SHARE, (t + 1) * SHARE)
        o_ref[t] = jnp.concatenate([real_t[rows], imag_t[rows]], axis=0).astype(BF16)


def turn(v):
    return pl.pallas_call(
        turn_kernel,
        out_shape=jax.ShapeDtypeStruct((NY * NZ * NC, 2 * SHARE, HELD), BF16),
        in_specs=[in_vmem],
        out_specs=in_vmem,
        compiler_params=params(14),
        cost_estimate=cost(4),
    )(v)


def project(v_halves, pieces):
    a, b = sum3(dot_nn(pieces, v_halves[0])), sum3(dot_nn(pieces, v_halves[1]))
    return a[0:KDIM] + b[KDIM:], a[KDIM:] - b[0:KDIM]


def expand(v_halves, pieces):
    a, b = sum3(dot_nt(pieces, v_halves[0])), sum3(dot_nt(pieces, v_halves[1]))
    return a[0:KDIM] - b[KDIM:], a[KDIM:] + b[0:KDIM]


def gram_from(products):
    p0, p1, p2 = products[0:16], products[16:32], products[32:48]
    m = (p0 + (p1 + p2)) + pltpu.roll(p0 + p1, 112, 1) + pltpu.roll(p0, 96, 1)
    up, down = m[0:KDIM], m[KDIM:]
    return up + pltpu.roll(down, 120, 1), down - pltpu.roll(up, 120, 1)


def eliminate(gram, others):
    row_id = lax.broadcasted_iota(jnp.int32, (KDIM, 1), 0)
    gram_re, gram_im = gram
    pairs = [(gram_re, gram_im)] + list(others)
    for j in range(KDIM):
        gram_re, gram_im = pairs[0]
        scale = 1.0 / jnp.sqrt(gram_re[j : j + 1, j : j + 1])
        below = jnp.where(row_id > j, scale, 0.0)
        m_re, m_im = gram_re[:, j : j + 1] * below, gram_im[:, j : j + 1] * below
        done = []
        for re, im in pairs:
            top_re, top_im = re[j : j + 1] * scale, im[j : j + 1] * scale
            new_re = re - (m_re * top_re - m_im * top_im)
            new_im = im - (m_re * top_im + m_im * top_re)
            here = row_id == j
            done.append((jnp.where(here, top_re, new_re), jnp.where(here, top_im, new_im)))
        pairs = done
    return pairs


def first_kernel(v_ref, q_ref, s_ref):
    u_re, u_im = project(halves(v_ref), split3(q_ref[...]))
    s_ref[...] = jnp.concatenate([u_re, u_im], axis=0)


def step_kernel(step, v_ref, z_ref, s0, s1, s2, s3, *outs):
    s = (s0[...] + s2[...]) + (s1[...] + s3[...])
    w = (s[0:KDIM, 0:SPECTRA], s[KDIM:, 0:SPECTRA])
    q = (z_ref[0:KDIM], z_ref[KDIM:])
    if step > 0:
        gram = (s[0:KDIM, SPECTRA:], s[KDIM:, SPECTRA:])
        _, w, q = eliminate(gram, [w, q])
    v = halves(v_ref)
    i_re, i_im = expand(v, split3(jnp.concatenate(w, axis=0)))
    z_re = i_re * (1.0 / SPECTRA) + LOADING * q[0]
    z_im = i_im * (1.0 / SPECTRA) + LOADING * q[1]
    z = jnp.concatenate([z_re, z_im], axis=0)
    if step == 2:
        (many_ref,) = outs
        for d in range(NY * NZ):
            many_ref[d] = z
        return
    new_z, new_s = outs
    new_z[...] = z
    pieces = split3(z)
    u_re, u_im = project(v, pieces)
    padded = jnp.concatenate([pieces, jnp.zeros((80, HELD), BF16)], axis=0)
    g_re, g_im = gram_from(dot_nt(pieces, padded))
    new_s[0:KDIM, 0:SPECTRA] = u_re
    new_s[KDIM:, 0:SPECTRA] = u_im
    new_s[0:KDIM, SPECTRA:] = g_re
    new_s[KDIM:, SPECTRA:] = g_im


def first(v, q):
    return pl.pallas_call(
        first_kernel,
        out_shape=jax.ShapeDtypeStruct((2 * KDIM, SPECTRA), F32),
        in_specs=[in_vmem] * 2,
        out_specs=in_vmem,
        compiler_params=params(12),
        cost_estimate=cost(2),
    )(v, q)


def step(at, v, z, sums):
    if at == 2:
        shapes = [jax.ShapeDtypeStruct((NY * NZ, 2 * KDIM, HELD), F32)]
    else:
        shapes = [
            jax.ShapeDtypeStruct((2 * KDIM, HELD), F32),
            jax.ShapeDtypeStruct((2 * KDIM, SPECTRA + 128), F32),
        ]
    return pl.pallas_call(
        functools.partial(step_kernel, at),
        out_shape=shapes,
        in_specs=[in_vmem] * 6,
        out_specs=[in_vmem] * len(shapes),
        compiler_params=params(12),
        cost_estimate=cost(3),
    )(v, z, *sums)


def final_kernel(v_ref, own_ref, far_ref, core_ref, o_ref, flat, basis):
    row = lax.broadcasted_iota(jnp.int32, (256, 256), 0)
    col = lax.broadcasted_iota(jnp.int32, (256, 256), 1)
    source = ((col // 32) % 2) * 128 + (col // 64) * 32 + col % 32
    place = jnp.where(row == source, 1.0, 0.0).astype(BF16)
    lane = lax.broadcasted_iota(jnp.int32, (2 * KDIM, 128), 1) // 32
    is_zero = core_ref[0] == 0
    for x in range(NX):
        lanes = slice(x * 128, (x + 1) * 128)
        rows = []
        for y in range(NY):
            for z in range(GROUP):
                at = (y * NZ + z) * NC
                rows.append(
                    jnp.concatenate([v_ref[at, :, lanes], v_ref[at + 1, :, lanes]], axis=1)
                )
        got = dot_nn(jnp.concatenate(rows, axis=0), place)
        flat[x] = got.reshape(NY, GROUP, 2 * SHARE, 256)
        for y in range(NY):
            for z in range(GROUP):
                own, far = own_ref[y * NZ + z, :, lanes], far_ref[y * NZ + z, :, lanes]
                a, b = jnp.where(is_zero, own, far), jnp.where(is_zero, far, own)
                left = jnp.where(
                    lane < 2,
                    jnp.where(lane == 0, a, pltpu.roll(b, 32, 1)),
                    jnp.where(lane == 2, pltpu.roll(a, 32, 1), pltpu.roll(b, 64, 1)),
                )
                right = jnp.where(
                    lane < 2,
                    jnp.where(lane == 0, pltpu.roll(a, 64, 1), pltpu.roll(b, 96, 1)),
                    jnp.where(lane == 2, pltpu.roll(a, 96, 1), b),
                )
                at = (x * NY + y) * 256
                basis[z, :, at : at + 128] = left
                basis[z, :, at + 128 : at + 256] = right

    lane = lax.broadcasted_iota(jnp.int32, (KDIM, 128), 1)
    unit = lane == lax.broadcasted_iota(jnp.int32, (KDIM, 128), 0) + KDIM
    unit_lanes = (lane >= KDIM) & (lane < 2 * KDIM)
    u_lanes = (lane >= 48) & (lane < 72)
    wide = NY * 256
    for z in range(GROUP):
        products = jnp.zeros((48, 128), F32)
        for x in range(NX):
            pieces = split3(basis[z, :, x * wide : (x + 1) * wide])
            block = jnp.concatenate([flat[x, y, z] for y in range(NY)], axis=1).astype(BF16)
            right = jnp.concatenate([pieces, block, jnp.zeros((32, wide), BF16)], axis=0)
            products = products + dot_nt(pieces, right)
        g_re, g_im = gram_from(products)
        up_down = sum3(products)
        up, down = up_down[0:KDIM], up_down[KDIM:]
        u_re = up + pltpu.roll(down, 104, 1)
        u_im = down - pltpu.roll(up, 104, 1)
        x_re = jnp.where(u_lanes, u_re, jnp.where(unit_lanes, jnp.where(unit, 1.0, 0.0), g_re))
        x_im = jnp.where(u_lanes, u_im, jnp.where(unit_lanes, 0.0, g_im))
        used = lane < 72
        x_re, x_im = jnp.where(used, x_re, 0.0), jnp.where(used, x_im, 0.0)
        ((x_re, x_im),) = eliminate((x_re, x_im), [])
        both = jnp.concatenate([x_re, x_im], axis=0)
        cross = jnp.concatenate([x_im, -x_re], axis=0)
        t_re = dot_tn(both, both, lax.Precision.HIGHEST)[KDIM : 2 * KDIM]
        t_im = dot_tn(cross, both, lax.Precision.HIGHEST)[KDIM : 2 * KDIM]

        def sides(a, b):
            near, away = pltpu.roll(a, 80, 1), pltpu.roll(b, 104, 1)
            return jnp.where(lane < SHARE, near, jnp.where(lane < 2 * SHARE, away, 0.0))

        t = split3(jnp.concatenate([sides(t_re, t_im), sides(-t_im, t_re)], axis=0))
        hi, mid, lo = t[0:16], t[16:32], t[32:48]
        left = jnp.concatenate([hi, hi, hi, mid, mid, lo], axis=0)
        for x in range(NX):
            pieces = split3(basis[z, :, x * wide : (x + 1) * wide])
            right = jnp.concatenate([pieces, pieces[0:32], pieces[0:16]], axis=0)
            fitted = dot_tn(left, right)[0 : 2 * SHARE]
            for y in range(NY):
                rest = flat[x, y, z] - fitted[:, y * 256 : (y + 1) * 256]
                at = x * wide + y * 256
                o_ref[0, z, :, at : at + 256] = rest[0:SHARE]
                o_ref[1, z, :, at : at + 256] = rest[SHARE:]


def finish(v, own, far, core):
    return pl.pallas_call(
        final_kernel,
        out_shape=jax.ShapeDtypeStruct((2, GROUP, SHARE, INPUTS), F32),
        in_specs=[in_vmem] * 3 + [pl.BlockSpec(memory_space=pltpu.SMEM)],
        out_specs=in_vmem,
        scratch_shapes=[
            pltpu.VMEM((NX, NY, GROUP, 2 * SHARE, 256), F32),
            pltpu.VMEM((GROUP, 2 * KDIM, INPUTS), F32),
        ],
        compiler_params=params(24),
        cost_estimate=cost(6),
    )(v, own, far, core)


def turned_by(count, distance):
    return [(i, (i + distance) % count) for i in range(count)]


def sums_over(s):
    return [s] + [lax.ppermute(s, "y", turned_by(NY, d)) for d in range(1, NY)]


def core_sum(s):
    return s + lax.ppermute(s, "core", turned_by(NC, 1))


def body(voltages, channel_ids, start_basis):
    y, core = lax.axis_index("y"), lax.axis_index("core")
    parcels = channelize(voltages, banded_table(channel_ids))
    v = lax.all_to_all(parcels, ("x", "z"), 0, 0, tiled=True)
    split = start_basis.reshape(2 * KDIM, NX, NY, NZ, NC, LOCAL)
    split = lax.dynamic_index_in_dim(split, y, 2, keepdims=False)
    z = lax.dynamic_index_in_dim(split, core, 3, keepdims=False).reshape(2 * KDIM, HELD)
    s = core_sum(first(v, z))
    sums = sums_over(s)
    turned = turn(lax.optimization_barrier((v, s))[0])
    blocks = lax.all_to_all(turned, ("y", "z", "core"), 0, 0, tiled=True)
    z, s = step(0, v, z, sums)
    z, s = step(1, v, z, sums_over(core_sum(s)))
    (many,) = step(2, v, z, sums_over(core_sum(s)))
    many, blocks = lax.optimization_barrier((many, blocks))
    own = lax.all_to_all(many, ("y", "z"), 0, 0, tiled=True)
    far = lax.ppermute(own, "core", turned_by(NC, 1))
    return finish(blocks, own, far, core.reshape(1).astype(jnp.int32))


def solution(mesh):
    fine = Mesh(mesh.devices.reshape(NX, NY, NZ, NC), ("x", "y", "z", "core"))
    in_specs = (P(("x", "y", "z", "core"), None), P(), P())
    out_specs = P(None, "x", ("y", "z", "core"), None)
    return jax.shard_map(body, mesh=fine, in_specs=in_specs, out_specs=out_specs, check_vma=False)
```

```python
import functools
import math

import jax
import jax.numpy as jnp
from jax import lax
from jax.experimental import pallas as pl
from jax.experimental.pallas import tpu as pltpu
from jax.sharding import Mesh, PartitionSpec as P

TAPS = 4
P_SIZE = 128
INPUTS = 4096
KDIM = 8
CHANNELS = 12
SPECTRA = 768
LOADING = 0.5

NX, NY, NZ, NC = 4, 4, 4, 2
LOCAL = INPUTS // (NX * NY * NZ * NC)
GROUP = CHANNELS // NX
HELD = LOCAL * NX * NZ
PHASES = 6
ROWS = SPECTRA // PHASES
SPAN = (PHASES + TAPS - 1) * P_SIZE
SHARE = SPECTRA // (NY * NZ * NC)
RC = 2 * CHANNELS

F32, BF16 = jnp.float32, jnp.bfloat16


def params(mib):
    return pltpu.CompilerParams(vmem_limit_bytes=mib * 1024 * 1024)


def cost(microseconds):
    return pl.CostEstimate(flops=0, bytes_accessed=int(microseconds * 3e6), transcendentals=0)


in_vmem = pl.BlockSpec(memory_space=pltpu.VMEM)


def dot_nn(a, b):
    return lax.dot_general(a, b, (((1,), (0,)), ((), ())), preferred_element_type=F32)


def dot_nt(a, b):
    return lax.dot_general(a, b, (((1,), (1,)), ((), ())), preferred_element_type=F32)


def dot_tn(a, b, precision=None):
    return lax.dot_general(
        a, b, (((0,), (0,)), ((), ())), preferred_element_type=F32, precision=precision
    )


def split3(x):
    hi = x.astype(BF16)
    rest = x - hi.astype(F32)
    mid = rest.astype(BF16)
    lo = (rest - mid.astype(F32)).astype(BF16)
    return jnp.concatenate([hi, mid, lo], axis=0)


def sum3(x):
    n = x.shape[0] // 3
    return x[:n] + (x[n : 2 * n] + x[2 * n :])


STEP_ROWS = 8
CHUNKS = 4


def fill_table(ids_ref, turned):
    length = TAPS * P_SIZE
    shape = (TAPS, P_SIZE)
    at = (
        lax.broadcasted_iota(jnp.int32, shape, 0) * P_SIZE
        + lax.broadcasted_iota(jnp.int32, shape, 1)
    ).astype(F32)
    angle = math.pi * ((at + 0.5 - length / 2.0) / P_SIZE)
    window = jnp.sin(angle) / angle * (0.5 - 0.5 * jnp.cos(2.0 * math.pi * (at + 0.5) / length))
    window = window / jnp.sqrt(jnp.sum(window * window))
    row = lax.broadcasted_iota(jnp.int32, (RC, P_SIZE), 0)
    point = lax.broadcasted_iota(jnp.int32, (RC, P_SIZE), 1)
    channel = jnp.where(row >= CHANNELS, row - CHANNELS, row)
    ids = jnp.zeros((RC, P_SIZE), jnp.int32)
    for c in range(CHANNELS):
        ids = jnp.where(channel == c, ids_ref[c], ids)
    angles = 2.0 * math.pi / P_SIZE * ((ids * point) % P_SIZE).astype(F32)
    rotors = jnp.where(row < CHANNELS, jnp.cos(angles), -jnp.sin(angles))
    turned[...] = jnp.zeros((256, SPAN), F32)
    for m in range(TAPS):
        taps = window[m : m + 1] * rotors
        for q in range(PHASES):
            turned[q * RC : (q + 1) * RC, (q + m) * P_SIZE : (q + m + 1) * P_SIZE] = taps


def channelize_kernel(ids_ref, x_hbm, o_ref, x_ref, turned, table, wide, tall, sems):
    step = ROWS // CHUNKS * PHASES * P_SIZE
    halo = (TAPS - 1) * P_SIZE
    copies = []
    for k in range(CHUNKS):
        low = k * step + (halo if k else 0)
        lanes = pl.ds(low, (k + 1) * step + halo - low)
        copies.append(
            pltpu.make_async_copy(x_hbm.at[:, lanes], x_ref.at[:, lanes], sems.at[k])
        )
        copies[-1].start()
    fill_table(ids_ref, turned)
    for k in range(SPAN // P_SIZE):
        lanes = slice(k * P_SIZE, (k + 1) * P_SIZE)
        table[lanes] = turned[:, lanes].T.astype(BF16)

    def filter_rows(at, carry):
        rows = []
        for k in range(STEP_ROWS):
            start = pl.multiple_of((at * STEP_ROWS + k) * (PHASES * P_SIZE), 128)
            rows.append(x_ref[:, pl.ds(start, SPAN)])
        got = dot_nn(jnp.concatenate(rows, axis=0), table[...])
        got = got.reshape(NC, STEP_ROWS // NC, LOCAL, 256)
        y, z = at // NZ, at % NZ
        for core in range(NC):
            wide[pl.ds((y * NC + core) * 16 + z * 4, STEP_ROWS // NC)] = got[core]
        return carry

    for k in range(CHUNKS):
        copies[k].wait()
        each = ROWS // STEP_ROWS // CHUNKS
        lax.fori_loop(k * each, (k + 1) * each, filter_rows, 0)

    for n in range(LOCAL):
        turned_n = jnp.concatenate(
            [wide[:, n, 0:128].T, wide[:, n, 128:256].T[0 : PHASES * RC - 128]], axis=0
        )
        for q in range(PHASES):
            tall[:, n, q * 128 : (q + 1) * 128] = turned_n[q * RC : (q + 1) * RC]

    for x in range(NX):
        for z in range(NZ):
            for r in range(2):
                if z < GROUP:
                    o_ref[x * NZ + z, r] = tall[r * CHANNELS + x * GROUP + z].astype(BF16)
                else:
                    o_ref[x * NZ + z, r] = jnp.zeros((LOCAL, SPECTRA), BF16)


def channelize(ids, x):
    return pl.pallas_call(
        channelize_kernel,
        out_shape=jax.ShapeDtypeStruct((NX * NZ, 2, LOCAL, SPECTRA), BF16),
        in_specs=[pl.BlockSpec(memory_space=pltpu.SMEM), pl.BlockSpec(memory_space=pltpu.HBM)],
        out_specs=in_vmem,
        scratch_shapes=[
            pltpu.VMEM(x.shape, BF16),
            pltpu.VMEM((256, SPAN), F32),
            pltpu.VMEM((SPAN, 256), BF16),
            pltpu.VMEM((ROWS, LOCAL, 256), F32),
            pltpu.VMEM((RC, LOCAL, SPECTRA), F32),
            pltpu.SemaphoreType.DMA((CHUNKS,)),
        ],
        compiler_params=params(32),
        cost_estimate=cost(8),
    )(ids, x)


PAD = 128
TURN_ROWS = GROUP * 2 * SHARE


def spread_kernel(y_ref, v_ref, *outs):
    row = lax.broadcasted_iota(jnp.int32, (SPECTRA, NC * PAD), 0)
    col = lax.broadcasted_iota(jnp.int32, (SPECTRA, NC * PAD), 1)
    inside = col % PAD
    wanted = (inside // 16) * ROWS + (col // PAD) * 16 + inside % 16
    for d in range(NY):
        y = (y_ref[0] + d) % NY
        hit = (row == wanted + y * (NC * 16)) & (inside < PHASES * 16)
        pick = jnp.where(hit, 1.0, 0.0).astype(BF16)
        for c in range(CHANNELS):
            at = c // GROUP * NZ + c % GROUP
            got = dot_nn(v_ref[at].reshape(2 * LOCAL, SPECTRA), pick)
            got = got.astype(BF16).reshape(2, LOCAL, NC * PAD)
            for core in range(NC):
                lanes = slice(core * PAD, (core + 1) * PAD)
                for r in range(2):
                    outs[d][core, c * 2 + r] = got[r, :, lanes]


def spread(y, v):
    return pl.pallas_call(
        spread_kernel,
        out_shape=[jax.ShapeDtypeStruct((NC, RC, LOCAL, PAD), BF16)] * NY,
        in_specs=[pl.BlockSpec(memory_space=pltpu.SMEM), in_vmem],
        out_specs=[in_vmem] * NY,
        compiler_params=params(16),
        cost_estimate=cost(4),
    )(y, v)


def turn_kernel(at_ref, *refs):
    parts, o_ref = refs[:-1], refs[-1]
    core = at_ref[1]
    row = lax.broadcasted_iota(jnp.int32, (NZ * SHARE, PAD), 0)
    col = lax.broadcasted_iota(jnp.int32, (NZ * SHARE, PAD), 1)
    z, s = row // SHARE, row % SHARE
    pick = (col == (s % PHASES) * 16 + z * 4 + s // PHASES)
    pick = jnp.where(pick, 1.0, 0.0).astype(BF16)
    for other in range(NC):
        side = core if other == 0 else 1 - core
        for x in range(NX):
            blocks = []
            for rc in range(2 * GROUP):
                stack = jnp.concatenate(
                    [parts[d][side, x * 2 * GROUP + rc] for d in range(NY)], axis=0
                )
                blocks.append(dot_nt(pick, stack))
            for z_to in range(NZ):
                rows = slice(z_to * SHARE, (z_to + 1) * SHARE)
                o_ref[x * NZ + z_to, other] = jnp.concatenate(
                    [g[rows] for g in blocks], axis=0
                ).astype(BF16)


def turn(at, parts):
    return pl.pallas_call(
        turn_kernel,
        out_shape=jax.ShapeDtypeStruct((NX * NZ, NC, TURN_ROWS, NY * LOCAL), BF16),
        in_specs=[pl.BlockSpec(memory_space=pltpu.SMEM)] + [in_vmem] * NY,
        out_specs=in_vmem,
        compiler_params=params(16),
        cost_estimate=cost(3),
    )(at, *parts)


def halves(v_ref):
    return v_ref[:, 0].reshape(HELD, SPECTRA), v_ref[:, 1].reshape(HELD, SPECTRA)


def project(v_halves, pieces):
    a, b = sum3(dot_nn(pieces, v_halves[0])), sum3(dot_nn(pieces, v_halves[1]))
    return a[0:KDIM] + b[KDIM:], a[KDIM:] - b[0:KDIM]


def expand(v_halves, pieces):
    a, b = sum3(dot_nt(pieces, v_halves[0])), sum3(dot_nt(pieces, v_halves[1]))
    return a[0:KDIM] - b[KDIM:], a[KDIM:] + b[0:KDIM]


def gram_from(products):
    p0, p1, p2 = products[0:16], products[16:32], products[32:48]
    m = (p0 + (p1 + p2)) + pltpu.roll(p0 + p1, 112, 1) + pltpu.roll(p0, 96, 1)
    up, down = m[0:KDIM], m[KDIM:]
    return up + pltpu.roll(down, 120, 1), down - pltpu.roll(up, 120, 1)


def eliminate(gram, others):
    row_id = lax.broadcasted_iota(jnp.int32, (KDIM, 1), 0)
    gram_re, gram_im = gram
    pairs = [(gram_re, gram_im)] + list(others)
    for j in range(KDIM):
        gram_re, gram_im = pairs[0]
        scale = 1.0 / jnp.sqrt(gram_re[j : j + 1, j : j + 1])
        below = jnp.where(row_id > j, scale, 0.0)
        m_re, m_im = gram_re[:, j : j + 1] * below, gram_im[:, j : j + 1] * below
        done = []
        for re, im in pairs:
            top_re, top_im = re[j : j + 1] * scale, im[j : j + 1] * scale
            new_re = re - (m_re * top_re - m_im * top_im)
            new_im = im - (m_re * top_im + m_im * top_re)
            here = row_id == j
            done.append((jnp.where(here, top_re, new_re), jnp.where(here, top_im, new_im)))
        pairs = done
    return pairs


def first_kernel(v_ref, q_ref, s_ref):
    u_re, u_im = project(halves(v_ref), split3(q_ref[...]))
    s_ref[...] = jnp.concatenate([u_re, u_im], axis=0)


def step_kernel(step, v_ref, z_ref, s0, s1, s2, s3, *outs):
    s = (s0[...] + s2[...]) + (s1[...] + s3[...])
    w = (s[0:KDIM, 0:SPECTRA], s[KDIM:, 0:SPECTRA])
    q = (z_ref[0:KDIM], z_ref[KDIM:])
    if step > 0:
        gram = (s[0:KDIM, SPECTRA:], s[KDIM:, SPECTRA:])
        _, w, q = eliminate(gram, [w, q])
    v = halves(v_ref)
    i_re, i_im = expand(v, split3(jnp.concatenate(w, axis=0)))
    z_re = i_re * (1.0 / SPECTRA) + LOADING * q[0]
    z_im = i_im * (1.0 / SPECTRA) + LOADING * q[1]
    z = jnp.concatenate([z_re, z_im], axis=0)
    if step == 2:
        (many_ref,) = outs
        for d in range(NY * NZ):
            many_ref[d] = z
        return
    new_z, new_s = outs
    new_z[...] = z
    pieces = split3(z)
    u_re, u_im = project(v, pieces)
    padded = jnp.concatenate([pieces, jnp.zeros((80, HELD), BF16)], axis=0)
    g_re, g_im = gram_from(dot_nt(pieces, padded))
    new_s[0:KDIM, 0:SPECTRA] = u_re
    new_s[KDIM:, 0:SPECTRA] = u_im
    new_s[0:KDIM, SPECTRA:] = g_re
    new_s[KDIM:, SPECTRA:] = g_im


def first(v, q):
    return pl.pallas_call(
        first_kernel,
        out_shape=jax.ShapeDtypeStruct((2 * KDIM, SPECTRA), F32),
        in_specs=[in_vmem] * 2,
        out_specs=in_vmem,
        compiler_params=params(12),
        cost_estimate=cost(2),
    )(v, q)


def step(at, v, z, sums):
    if at == 2:
        shapes = [jax.ShapeDtypeStruct((NY * NZ, 2 * KDIM, HELD), F32)]
    else:
        shapes = [
            jax.ShapeDtypeStruct((2 * KDIM, HELD), F32),
            jax.ShapeDtypeStruct((2 * KDIM, SPECTRA + 128), F32),
        ]
    return pl.pallas_call(
        functools.partial(step_kernel, at),
        out_shape=shapes,
        in_specs=[in_vmem] * 6,
        out_specs=[in_vmem] * len(shapes),
        compiler_params=params(12),
        cost_estimate=cost(3),
    )(v, z, *sums)


def placing(y, core):
    side = NY * NZ * NC * LOCAL
    row = lax.broadcasted_iota(jnp.int32, (side, side), 0)
    col = lax.broadcasted_iota(jnp.int32, (side, side), 1)
    to_y, to_z, to_core, i = col // 256, (col // 64) % 4, (col // 32) % 2, col % 32
    source = to_z * 256 + ((to_core + core) % 2) * 128 + ((y - to_y) % 4) * 32 + i
    return jnp.where(row == source, 1.0, 0.0).astype(BF16)


def final_kernel(mine_ref, theirs_ref, own_ref, far_ref, core_ref, place_ref, o_ref, flat, basis):
    lane = lax.broadcasted_iota(jnp.int32, (2 * KDIM, 128), 1) // 32
    is_zero = core_ref[1] == 0
    rows = []
    for x in range(NX):
        parts = []
        for z in range(NZ):
            parts += [mine_ref[x * NZ + z], theirs_ref[x * NZ + z]]
        rows.append(jnp.concatenate(parts, axis=1))
    got = dot_nn(jnp.concatenate(rows, axis=0), place_ref[...])
    flat[...] = got.reshape(NX, GROUP, 2 * SHARE, NY * 256)
    for x in range(NX):
        lanes = slice(x * 128, (x + 1) * 128)
        for y in range(NY):
            for z in range(GROUP):
                own, far = own_ref[y * NZ + z, :, lanes], far_ref[y * NZ + z, :, lanes]
                a, b = jnp.where(is_zero, own, far), jnp.where(is_zero, far, own)
                left = jnp.where(
                    lane < 2,
                    jnp.where(lane == 0, a, pltpu.roll(b, 32, 1)),
                    jnp.where(lane == 2, pltpu.roll(a, 32, 1), pltpu.roll(b, 64, 1)),
                )
                right = jnp.where(
                    lane < 2,
                    jnp.where(lane == 0, pltpu.roll(a, 64, 1), pltpu.roll(b, 96, 1)),
                    jnp.where(lane == 2, pltpu.roll(a, 96, 1), b),
                )
                at = (x * NY + y) * 256
                basis[z, :, at : at + 128] = left
                basis[z, :, at + 128 : at + 256] = right

    lane = lax.broadcasted_iota(jnp.int32, (KDIM, 128), 1)
    unit = lane == lax.broadcasted_iota(jnp.int32, (KDIM, 128), 0) + KDIM
    unit_lanes = (lane >= KDIM) & (lane < 2 * KDIM)
    u_lanes = (lane >= 48) & (lane < 72)
    wide = NY * 256
    for z in range(GROUP):
        products = jnp.zeros((48, 128), F32)
        for x in range(NX):
            pieces = split3(basis[z, :, x * wide : (x + 1) * wide])
            block = flat[x, z].astype(BF16)
            right = jnp.concatenate([pieces, block, jnp.zeros((32, wide), BF16)], axis=0)
            products = products + dot_nt(pieces, right)
        g_re, g_im = gram_from(products)
        up_down = sum3(products)
        up, down = up_down[0:KDIM], up_down[KDIM:]
        u_re = up + pltpu.roll(down, 104, 1)
        u_im = down - pltpu.roll(up, 104, 1)
        x_re = jnp.where(u_lanes, u_re, jnp.where(unit_lanes, jnp.where(unit, 1.0, 0.0), g_re))
        x_im = jnp.where(u_lanes, u_im, jnp.where(unit_lanes, 0.0, g_im))
        used = lane < 72
        x_re, x_im = jnp.where(used, x_re, 0.0), jnp.where(used, x_im, 0.0)
        ((x_re, x_im),) = eliminate((x_re, x_im), [])
        both = jnp.concatenate([x_re, x_im], axis=0)
        cross = jnp.concatenate([x_im, -x_re], axis=0)
        t_re = dot_tn(both, both, lax.Precision.HIGHEST)[KDIM : 2 * KDIM]
        t_im = dot_tn(cross, both, lax.Precision.HIGHEST)[KDIM : 2 * KDIM]

        def sides(a, b):
            near, away = pltpu.roll(a, 80, 1), pltpu.roll(b, 104, 1)
            return jnp.where(lane < SHARE, near, jnp.where(lane < 2 * SHARE, away, 0.0))

        t = split3(jnp.concatenate([sides(t_re, t_im), sides(-t_im, t_re)], axis=0))
        hi, mid, lo = t[0:16], t[16:32], t[32:48]
        left = jnp.concatenate([hi, hi, hi, mid, mid, lo], axis=0)
        for x in range(NX):
            pieces = split3(basis[z, :, x * wide : (x + 1) * wide])
            right = jnp.concatenate([pieces, pieces[0:32], pieces[0:16]], axis=0)
            fitted = dot_tn(left, right)[0 : 2 * SHARE]
            rest = flat[x, z] - fitted
            o_ref[0, z, :, x * wide : (x + 1) * wide] = rest[0:SHARE]
            o_ref[1, z, :, x * wide : (x + 1) * wide] = rest[SHARE:]


def finish(mine, theirs, own, far, at, place):
    return pl.pallas_call(
        final_kernel,
        out_shape=jax.ShapeDtypeStruct((2, GROUP, SHARE, INPUTS), F32),
        in_specs=[in_vmem] * 4 + [pl.BlockSpec(memory_space=pltpu.SMEM), in_vmem],
        out_specs=in_vmem,
        scratch_shapes=[
            pltpu.VMEM((NX, GROUP, 2 * SHARE, NY * 256), F32),
            pltpu.VMEM((GROUP, 2 * KDIM, INPUTS), F32),
        ],
        compiler_params=params(24),
        cost_estimate=cost(6),
    )(mine, theirs, own, far, at, place)


def turned_by(count, distance):
    return [(i, (i + distance) % count) for i in range(count)]


def sums_over(s):
    return [s] + [lax.ppermute(s, "y", turned_by(NY, d)) for d in range(1, NY)]


def core_sum(s):
    return s + lax.ppermute(s, "core", turned_by(NC, 1))


def body(voltages, channel_ids, start_basis):
    y, core = lax.axis_index("y"), lax.axis_index("core")
    at = jnp.stack([y, core]).astype(jnp.int32)
    parcels = channelize(channel_ids, voltages)
    v = lax.all_to_all(parcels, ("x", "z"), 0, 0, tiled=True)
    parts = spread(at, parcels)
    parts = [parts[0]] + [lax.ppermute(parts[d], "y", turned_by(NY, d)) for d in range(1, NY)]
    turned = turn(at, parts)
    split = start_basis.reshape(2 * KDIM, NX, NY, NZ, NC, LOCAL)
    split = lax.dynamic_index_in_dim(split, y, 2, keepdims=False)
    z = lax.dynamic_index_in_dim(split, core, 3, keepdims=False).reshape(2 * KDIM, HELD)
    s = core_sum(first(v, z))
    sums = sums_over(s)
    turned = lax.optimization_barrier((turned, s))[0]
    blocks = lax.all_to_all(turned, ("x", "z"), 0, 0, tiled=True)
    place = placing(y, core)
    z, s = step(0, v, z, sums)
    z, s = step(1, v, z, sums_over(core_sum(s)))
    (many,) = step(2, v, z, sums_over(core_sum(s)))
    many, blocks = lax.optimization_barrier((many, blocks))
    mine, theirs = blocks[:, 0], lax.ppermute(blocks[:, 1], "core", turned_by(NC, 1))
    own = lax.all_to_all(many, ("y", "z"), 0, 0, tiled=True)
    far = lax.ppermute(own, "core", turned_by(NC, 1))
    return finish(mine, theirs, own, far, at, place)


def solution(mesh):
    fine = Mesh(mesh.devices.reshape(NX, NY, NZ, NC), ("x", "y", "z", "core"))
    in_specs = (P(("x", "y", "z", "core"), None), P(), P())
    out_specs = P(None, "x", ("y", "z", "core"), None)
    return jax.shard_map(body, mesh=fine, in_specs=in_specs, out_specs=out_specs, check_vma=False)
```

```python
import functools
import math

import jax
import jax.numpy as jnp
from jax import lax
from jax.experimental import pallas as pl
from jax.experimental.pallas import tpu as pltpu
from jax.sharding import Mesh, PartitionSpec as P

TAPS = 4
P_SIZE = 128
INPUTS = 4096
KDIM = 8
CHANNELS = 12
SPECTRA = 768
LOADING = 0.5

NX, NY, NZ, NC = 4, 4, 4, 2
LOCAL = INPUTS // (NX * NY * NZ * NC)
GROUP = CHANNELS // NX
HELD = LOCAL * NX * NZ
PHASES = 6
ROWS = SPECTRA // PHASES
SPAN = (PHASES + TAPS - 1) * P_SIZE
SHARE = SPECTRA // (NY * NZ * NC)
RC = 2 * CHANNELS

F32, BF16 = jnp.float32, jnp.bfloat16


def params(mib):
    return pltpu.CompilerParams(vmem_limit_bytes=mib * 1024 * 1024)


def cost(microseconds):
    return pl.CostEstimate(flops=0, bytes_accessed=int(microseconds * 3e6), transcendentals=0)


in_vmem = pl.BlockSpec(memory_space=pltpu.VMEM)


def dot_nn(a, b):
    return lax.dot_general(a, b, (((1,), (0,)), ((), ())), preferred_element_type=F32)


def dot_nt(a, b):
    return lax.dot_general(a, b, (((1,), (1,)), ((), ())), preferred_element_type=F32)


def dot_tn(a, b, precision=None):
    return lax.dot_general(
        a, b, (((0,), (0,)), ((), ())), preferred_element_type=F32, precision=precision
    )


def split3(x):
    hi = x.astype(BF16)
    rest = x - hi.astype(F32)
    mid = rest.astype(BF16)
    lo = (rest - mid.astype(F32)).astype(BF16)
    return jnp.concatenate([hi, mid, lo], axis=0)


def sum3(x):
    n = x.shape[0] // 3
    return x[:n] + (x[n : 2 * n] + x[2 * n :])


STEP_ROWS = 8
CHUNKS = 4


def fill_table(ids_ref, turned):
    length = TAPS * P_SIZE
    shape = (TAPS, P_SIZE)
    at = (
        lax.broadcasted_iota(jnp.int32, shape, 0) * P_SIZE
        + lax.broadcasted_iota(jnp.int32, shape, 1)
    ).astype(F32)
    angle = math.pi * ((at + 0.5 - length / 2.0) / P_SIZE)
    window = jnp.sin(angle) / angle * (0.5 - 0.5 * jnp.cos(2.0 * math.pi * (at + 0.5) / length))
    window = window / jnp.sqrt(jnp.sum(window * window))
    row = lax.broadcasted_iota(jnp.int32, (RC, P_SIZE), 0)
    point = lax.broadcasted_iota(jnp.int32, (RC, P_SIZE), 1)
    channel = jnp.where(row >= CHANNELS, row - CHANNELS, row)
    ids = jnp.zeros((RC, P_SIZE), jnp.int32)
    for c in range(CHANNELS):
        ids = jnp.where(channel == c, ids_ref[c], ids)
    angles = 2.0 * math.pi / P_SIZE * ((ids * point) % P_SIZE).astype(F32)
    rotors = jnp.where(row < CHANNELS, jnp.cos(angles), -jnp.sin(angles))
    turned[...] = jnp.zeros((256, SPAN), F32)
    for m in range(TAPS):
        taps = window[m : m + 1] * rotors
        for q in range(PHASES):
            turned[q * RC : (q + 1) * RC, (q + m) * P_SIZE : (q + m + 1) * P_SIZE] = taps


def channelize_kernel(ids_ref, x_hbm, o_ref, x_ref, turned, table, wide, tall, sems):
    step = ROWS // CHUNKS * PHASES * P_SIZE
    halo = (TAPS - 1) * P_SIZE
    copies = []
    for k in range(CHUNKS):
        low = k * step + (halo if k else 0)
        lanes = pl.ds(low, (k + 1) * step + halo - low)
        copies.append(
            pltpu.make_async_copy(x_hbm.at[:, lanes], x_ref.at[:, lanes], sems.at[k])
        )
        copies[-1].start()
    fill_table(ids_ref, turned)
    for k in range(SPAN // P_SIZE):
        lanes = slice(k * P_SIZE, (k + 1) * P_SIZE)
        table[lanes] = turned[:, lanes].T.astype(BF16)

    def filter_rows(at, carry):
        rows = []
        for k in range(STEP_ROWS):
            start = pl.multiple_of((at * STEP_ROWS + k) * (PHASES * P_SIZE), 128)
            rows.append(x_ref[:, pl.ds(start, SPAN)])
        got = dot_nn(jnp.concatenate(rows, axis=0), table[...])
        got = got.reshape(NC, STEP_ROWS // NC, LOCAL, 256)
        y, z = at // NZ, at % NZ
        for core in range(NC):
            wide[pl.ds((y * NC + core) * 16 + z * 4, STEP_ROWS // NC)] = got[core]
        return carry

    for k in range(CHUNKS):
        copies[k].wait()
        each = ROWS // STEP_ROWS // CHUNKS
        lax.fori_loop(k * each, (k + 1) * each, filter_rows, 0)

    for n in range(LOCAL):
        turned_n = jnp.concatenate(
            [wide[:, n, 0:128].T, wide[:, n, 128:256].T[0 : PHASES * RC - 128]], axis=0
        )
        for q in range(PHASES):
            tall[:, n, q * 128 : (q + 1) * 128] = turned_n[q * RC : (q + 1) * RC]

    for x in range(NX):
        for z in range(NZ):
            for r in range(2):
                if z < GROUP:
                    o_ref[x * NZ + z, r] = tall[r * CHANNELS + x * GROUP + z].astype(BF16)
                else:
                    o_ref[x * NZ + z, r] = jnp.zeros((LOCAL, SPECTRA), BF16)


def channelize(ids, x):
    return pl.pallas_call(
        channelize_kernel,
        out_shape=jax.ShapeDtypeStruct((NX * NZ, 2, LOCAL, SPECTRA), BF16),
        in_specs=[pl.BlockSpec(memory_space=pltpu.SMEM), pl.BlockSpec(memory_space=pltpu.HBM)],
        out_specs=in_vmem,
        scratch_shapes=[
            pltpu.VMEM(x.shape, BF16),
            pltpu.VMEM((256, SPAN), F32),
            pltpu.VMEM((SPAN, 256), BF16),
            pltpu.VMEM((ROWS, LOCAL, 256), F32),
            pltpu.VMEM((RC, LOCAL, SPECTRA), F32),
            pltpu.SemaphoreType.DMA((CHUNKS,)),
        ],
        compiler_params=params(58),
        cost_estimate=cost(8),
    )(ids, x)


PAD = 128
TURN_ROWS = GROUP * 2 * SHARE


def spread_kernel(y_ref, v_ref, *outs):
    row = lax.broadcasted_iota(jnp.int32, (SPECTRA, NC * PAD), 0)
    col = lax.broadcasted_iota(jnp.int32, (1, NC * PAD), 1)
    inside = col % PAD
    wanted = (inside // 16) * ROWS + (col // PAD) * 16 + inside % 16
    wanted = jnp.where(inside < PHASES * 16, wanted, -SPECTRA)
    rows = [v_ref[c // GROUP * NZ + c % GROUP].reshape(2 * LOCAL, SPECTRA) for c in range(CHANNELS)]
    rows = jnp.concatenate(rows, axis=0)
    for d in range(NY):
        y = (y_ref[0] + d) % NY
        pick = jnp.where(row == wanted + y * (NC * 16), 1.0, 0.0).astype(BF16)
        got = dot_nn(rows, pick).astype(BF16).reshape(RC, LOCAL, NC * PAD)
        for core in range(NC):
            outs[d][core] = got[:, :, core * PAD : (core + 1) * PAD]


def spread(y, v):
    return pl.pallas_call(
        spread_kernel,
        out_shape=[jax.ShapeDtypeStruct((NC, RC, LOCAL, PAD), BF16)] * NY,
        in_specs=[pl.BlockSpec(memory_space=pltpu.SMEM), in_vmem],
        out_specs=[in_vmem] * NY,
        compiler_params=params(16),
        cost_estimate=cost(4),
    )(y, v)


def turn_kernel(at_ref, *refs):
    parts, o_ref = refs[:-1], refs[-1]
    core = at_ref[1]
    row = lax.broadcasted_iota(jnp.int32, (NZ * SHARE, PAD), 0)
    col = lax.broadcasted_iota(jnp.int32, (NZ * SHARE, PAD), 1)
    z, s = row // SHARE, row % SHARE
    pick = (col == (s % PHASES) * 16 + z * 4 + s // PHASES)
    pick = jnp.where(pick, 1.0, 0.0).astype(BF16)
    for other in range(NC):
        side = core if other == 0 else 1 - core
        for x in range(NX):
            blocks = []
            for rc in range(0, 2 * GROUP, 2):
                at = x * 2 * GROUP + rc
                stack = jnp.concatenate(
                    [parts[d][side, at + k] for k in range(2) for d in range(NY)], axis=0
                )
                got = dot_nt(pick, stack)
                blocks += [got[:, 0 : NY * LOCAL], got[:, NY * LOCAL :]]
            for z_to in range(NZ):
                rows = slice(z_to * SHARE, (z_to + 1) * SHARE)
                o_ref[x * NZ + z_to, other] = jnp.concatenate(
                    [g[rows] for g in blocks], axis=0
                ).astype(BF16)


def turn(at, parts):
    return pl.pallas_call(
        turn_kernel,
        out_shape=jax.ShapeDtypeStruct((NX * NZ, NC, TURN_ROWS, NY * LOCAL), BF16),
        in_specs=[pl.BlockSpec(memory_space=pltpu.SMEM)] + [in_vmem] * NY,
        out_specs=in_vmem,
        compiler_params=params(16),
        cost_estimate=cost(3),
    )(at, *parts)


def halves(v_ref):
    return v_ref[:, 0].reshape(HELD, SPECTRA), v_ref[:, 1].reshape(HELD, SPECTRA)


def project(v_halves, pieces):
    a, b = sum3(dot_nn(pieces, v_halves[0])), sum3(dot_nn(pieces, v_halves[1]))
    return a[0:KDIM] + b[KDIM:], a[KDIM:] - b[0:KDIM]


def expand(v_halves, pieces):
    a, b = sum3(dot_nt(pieces, v_halves[0])), sum3(dot_nt(pieces, v_halves[1]))
    return a[0:KDIM] - b[KDIM:], a[KDIM:] + b[0:KDIM]


def gram_from(products):
    p0, p1, p2 = products[0:16], products[16:32], products[32:48]
    m = (p0 + (p1 + p2)) + pltpu.roll(p0 + p1, 112, 1) + pltpu.roll(p0, 96, 1)
    up, down = m[0:KDIM], m[KDIM:]
    return up + pltpu.roll(down, 120, 1), down - pltpu.roll(up, 120, 1)


def eliminate(gram, others):
    row_id = lax.broadcasted_iota(jnp.int32, (KDIM, 1), 0)
    gram_re, gram_im = gram
    pairs = [(gram_re, gram_im)] + list(others)
    for j in range(KDIM):
        gram_re, gram_im = pairs[0]
        scale = 1.0 / jnp.sqrt(gram_re[j : j + 1, j : j + 1])
        below = jnp.where(row_id > j, scale, 0.0)
        m_re, m_im = gram_re[:, j : j + 1] * below, gram_im[:, j : j + 1] * below
        done = []
        for re, im in pairs:
            top_re, top_im = re[j : j + 1] * scale, im[j : j + 1] * scale
            new_re = re - (m_re * top_re - m_im * top_im)
            new_im = im - (m_re * top_im + m_im * top_re)
            here = row_id == j
            done.append((jnp.where(here, top_re, new_re), jnp.where(here, top_im, new_im)))
        pairs = done
    return pairs


def first_kernel(v_ref, q_ref, s_ref):
    u_re, u_im = project(halves(v_ref), split3(q_ref[...]))
    s_ref[...] = jnp.concatenate([u_re, u_im], axis=0)


def step_kernel(step, v_ref, z_ref, s0, s1, s2, s3, *outs):
    s = (s0[...] + s2[...]) + (s1[...] + s3[...])
    w = (s[0:KDIM, 0:SPECTRA], s[KDIM:, 0:SPECTRA])
    q = (z_ref[0:KDIM], z_ref[KDIM:])
    if step > 0:
        gram = (s[0:KDIM, SPECTRA:], s[KDIM:, SPECTRA:])
        _, w, q = eliminate(gram, [w, q])
    v = halves(v_ref)
    i_re, i_im = expand(v, split3(jnp.concatenate(w, axis=0)))
    z_re = i_re * (1.0 / SPECTRA) + LOADING * q[0]
    z_im = i_im * (1.0 / SPECTRA) + LOADING * q[1]
    z = jnp.concatenate([z_re, z_im], axis=0)
    if step == 2:
        (many_ref,) = outs
        for d in range(NY * NZ):
            many_ref[d] = z
        return
    new_z, new_s = outs
    new_z[...] = z
    pieces = split3(z)
    u_re, u_im = project(v, pieces)
    padded = jnp.concatenate([pieces, jnp.zeros((80, HELD), BF16)], axis=0)
    g_re, g_im = gram_from(dot_nt(pieces, padded))
    new_s[0:KDIM, 0:SPECTRA] = u_re
    new_s[KDIM:, 0:SPECTRA] = u_im
    new_s[0:KDIM, SPECTRA:] = g_re
    new_s[KDIM:, SPECTRA:] = g_im


def first(v, q):
    return pl.pallas_call(
        first_kernel,
        out_shape=jax.ShapeDtypeStruct((2 * KDIM, SPECTRA), F32),
        in_specs=[in_vmem] * 2,
        out_specs=in_vmem,
        compiler_params=params(12),
        cost_estimate=cost(2),
    )(v, q)


def step(at, v, z, sums):
    if at == 2:
        shapes = [jax.ShapeDtypeStruct((NY * NZ, 2 * KDIM, HELD), F32)]
    else:
        shapes = [
            jax.ShapeDtypeStruct((2 * KDIM, HELD), F32),
            jax.ShapeDtypeStruct((2 * KDIM, SPECTRA + 128), F32),
        ]
    return pl.pallas_call(
        functools.partial(step_kernel, at),
        out_shape=shapes,
        in_specs=[in_vmem] * 6,
        out_specs=[in_vmem] * len(shapes),
        compiler_params=params(12),
        cost_estimate=cost(3),
    )(v, z, *sums)


def placing(y, core):
    side = NY * NZ * NC * LOCAL
    row = lax.broadcasted_iota(jnp.int32, (side, side), 0)
    col = lax.broadcasted_iota(jnp.int32, (side, side), 1)
    to_y, to_z, to_core, i = col // 256, (col // 64) % 4, (col // 32) % 2, col % 32
    source = to_z * 256 + ((to_core + core) % 2) * 128 + ((y - to_y) % 4) * 32 + i
    return jnp.where(row == source, 1.0, 0.0).astype(BF16)


def arrange_kernel(mine_ref, theirs_ref, place_ref, flat):
    rows = []
    for x in range(NX):
        parts = []
        for z in range(NZ):
            parts += [mine_ref[x * NZ + z], theirs_ref[x * NZ + z]]
        rows.append(jnp.concatenate(parts, axis=1))
    got = dot_nn(jnp.concatenate(rows, axis=0), place_ref[...])
    flat[...] = got.reshape(NX, GROUP, 2 * SHARE, NY * 256)


def arrange(mine, theirs, place):
    return pl.pallas_call(
        arrange_kernel,
        out_shape=jax.ShapeDtypeStruct((NX, GROUP, 2 * SHARE, NY * 256), F32),
        in_specs=[in_vmem] * 3,
        out_specs=in_vmem,
        compiler_params=params(16),
        cost_estimate=cost(4),
    )(mine, theirs, place)


def final_kernel(flat, own_ref, far_ref, core_ref, o_ref, basis):
    z = pl.program_id(0)
    lane = lax.broadcasted_iota(jnp.int32, (2 * KDIM, 128), 1) // 32
    is_zero = core_ref[1] == 0
    for x in range(NX):
        lanes = slice(x * 128, (x + 1) * 128)
        for y in range(NY):
            own, far = own_ref[y * NZ + z, :, lanes], far_ref[y * NZ + z, :, lanes]
            a, b = jnp.where(is_zero, own, far), jnp.where(is_zero, far, own)
            left = jnp.where(
                lane < 2,
                jnp.where(lane == 0, a, pltpu.roll(b, 32, 1)),
                jnp.where(lane == 2, pltpu.roll(a, 32, 1), pltpu.roll(b, 64, 1)),
            )
            right = jnp.where(
                lane < 2,
                jnp.where(lane == 0, pltpu.roll(a, 64, 1), pltpu.roll(b, 96, 1)),
                jnp.where(lane == 2, pltpu.roll(a, 96, 1), b),
            )
            at = (x * NY + y) * 256
            for k, part in enumerate((left, right)):
                basis[:, at + k * 128 : at + (k + 1) * 128] = split3(part)

    lane = lax.broadcasted_iota(jnp.int32, (KDIM, 128), 1)
    unit = lane == lax.broadcasted_iota(jnp.int32, (KDIM, 128), 0) + KDIM
    unit_lanes = (lane >= KDIM) & (lane < 2 * KDIM)
    u_lanes = (lane >= 48) & (lane < 72)
    wide = NY * 256
    products = jnp.zeros((48, 128), F32)
    for x in range(NX):
        pieces = basis[:, x * wide : (x + 1) * wide]
        block = flat[x, z].astype(BF16)
        right = jnp.concatenate([pieces, block, jnp.zeros((32, wide), BF16)], axis=0)
        products = products + dot_nt(pieces, right)
    g_re, g_im = gram_from(products)
    up_down = sum3(products)
    up, down = up_down[0:KDIM], up_down[KDIM:]
    u_re = up + pltpu.roll(down, 104, 1)
    u_im = down - pltpu.roll(up, 104, 1)
    x_re = jnp.where(u_lanes, u_re, jnp.where(unit_lanes, jnp.where(unit, 1.0, 0.0), g_re))
    x_im = jnp.where(u_lanes, u_im, jnp.where(unit_lanes, 0.0, g_im))
    used = lane < 72
    x_re, x_im = jnp.where(used, x_re, 0.0), jnp.where(used, x_im, 0.0)
    ((x_re, x_im),) = eliminate((x_re, x_im), [])
    both = jnp.concatenate([x_re, x_im], axis=0)
    cross = jnp.concatenate([x_im, -x_re], axis=0)
    t_re = dot_tn(both, both, lax.Precision.HIGHEST)[KDIM : 2 * KDIM]
    t_im = dot_tn(cross, both, lax.Precision.HIGHEST)[KDIM : 2 * KDIM]

    def sides(a, b):
        near, away = pltpu.roll(a, 80, 1), pltpu.roll(b, 104, 1)
        return jnp.where(lane < SHARE, near, jnp.where(lane < 2 * SHARE, away, 0.0))

    t = split3(jnp.concatenate([sides(t_re, t_im), sides(-t_im, t_re)], axis=0))
    hi, mid, lo = t[0:16], t[16:32], t[32:48]
    left = jnp.concatenate([hi, hi, hi, mid, mid, lo], axis=0)
    for x in range(NX):
        pieces = basis[:, x * wide : (x + 1) * wide]
        right = jnp.concatenate([pieces, pieces[0:32], pieces[0:16]], axis=0)
        rest = flat[x, z] - dot_tn(left, right)[0 : 2 * SHARE]
        o_ref[0, 0, :, x * wide : (x + 1) * wide] = rest[0:SHARE]
        o_ref[1, 0, :, x * wide : (x + 1) * wide] = rest[SHARE:]


def finish(flat, own, far, at):
    return pl.pallas_call(
        final_kernel,
        grid=(GROUP,),
        out_shape=jax.ShapeDtypeStruct((2, GROUP, SHARE, INPUTS), F32),
        in_specs=[in_vmem] * 3 + [pl.BlockSpec(memory_space=pltpu.SMEM)],
        out_specs=pl.BlockSpec((2, 1, SHARE, INPUTS), lambda z: (0, z, 0, 0)),
        scratch_shapes=[pltpu.VMEM((6 * KDIM, INPUTS), BF16)],
        compiler_params=params(16),
        cost_estimate=cost(6),
    )(flat, own, far, at)


def turned_by(count, distance):
    return [(i, (i + distance) % count) for i in range(count)]


def sums_over(s):
    return [s] + [lax.ppermute(s, "y", turned_by(NY, d)) for d in range(1, NY)]


def core_sum(s):
    return s + lax.ppermute(s, "core", turned_by(NC, 1))


def body(voltages, channel_ids, start_basis):
    y, core = lax.axis_index("y"), lax.axis_index("core")
    at = jnp.stack([y, core]).astype(jnp.int32)
    parcels = channelize(channel_ids, voltages)
    v = lax.all_to_all(parcels, ("x", "z"), 0, 0, tiled=True)
    parts = spread(at, parcels)
    parts = [parts[0]] + [lax.ppermute(parts[d], "y", turned_by(NY, d)) for d in range(1, NY)]
    turned = turn(at, parts)
    split = start_basis.reshape(2 * KDIM, NX, NY, NZ, NC, LOCAL)
    split = lax.dynamic_index_in_dim(split, y, 2, keepdims=False)
    z = lax.dynamic_index_in_dim(split, core, 3, keepdims=False).reshape(2 * KDIM, HELD)
    s = core_sum(first(v, z))
    sums = sums_over(s)
    turned = lax.optimization_barrier((turned, s))[0]
    blocks = lax.all_to_all(turned, ("x", "z"), 0, 0, tiled=True)
    place = placing(y, core)
    z, s = step(0, v, z, sums)
    z, s = step(1, v, z, sums_over(core_sum(s)))
    s, blocks = lax.optimization_barrier((core_sum(s), blocks))
    sums = sums_over(s)
    mine, theirs = blocks[:, 0], lax.ppermute(blocks[:, 1], "core", turned_by(NC, 1))
    flat = arrange(mine, theirs, place)
    z, flat = lax.optimization_barrier((z, flat))
    (many,) = step(2, v, z, sums)
    own = lax.all_to_all(many, ("y", "z"), 0, 0, tiled=True)
    far = lax.ppermute(own, "core", turned_by(NC, 1))
    return finish(flat, own, far, at)


def solution(mesh):
    fine = Mesh(mesh.devices.reshape(NX, NY, NZ, NC), ("x", "y", "z", "core"))
    in_specs = (P(("x", "y", "z", "core"), None), P(), P())
    out_specs = P(None, "x", ("y", "z", "core"), None)
    return jax.shard_map(body, mesh=fine, in_specs=in_specs, out_specs=out_specs, check_vma=False)
```

```python
import functools
import math

import jax
import jax.numpy as jnp
from jax import lax
from jax.experimental import pallas as pl
from jax.experimental.pallas import tpu as pltpu
from jax.sharding import Mesh, PartitionSpec as P

TAPS = 4
P_SIZE = 128
INPUTS = 4096
KDIM = 8
CHANNELS = 12
SPECTRA = 768
LOADING = 0.5

NX, NY, NZ, NC = 4, 4, 4, 2
LOCAL = INPUTS // (NX * NY * NZ * NC)
GROUP = CHANNELS // NX
HELD = LOCAL * NX * NZ
PHASES = 6
ROWS = SPECTRA // PHASES
SPAN = (PHASES + TAPS - 1) * P_SIZE
SHARE = SPECTRA // (NY * NZ * NC)
RC = 2 * CHANNELS

F32, BF16 = jnp.float32, jnp.bfloat16


def params(mib):
    return pltpu.CompilerParams(vmem_limit_bytes=mib * 1024 * 1024)


def cost(microseconds):
    return pl.CostEstimate(flops=int(microseconds * 9e8), bytes_accessed=int(microseconds * 3e6), transcendentals=0)


in_vmem = pl.BlockSpec(memory_space=pltpu.VMEM)


def dot_nn(a, b):
    return lax.dot_general(a, b, (((1,), (0,)), ((), ())), preferred_element_type=F32)


def dot_nt(a, b):
    return lax.dot_general(a, b, (((1,), (1,)), ((), ())), preferred_element_type=F32)


def dot_tn(a, b, precision=None):
    return lax.dot_general(
        a, b, (((0,), (0,)), ((), ())), preferred_element_type=F32, precision=precision
    )


def split3(x):
    hi = x.astype(BF16)
    rest = x - hi.astype(F32)
    mid = rest.astype(BF16)
    lo = (rest - mid.astype(F32)).astype(BF16)
    return jnp.concatenate([hi, mid, lo], axis=0)


def sum3(x):
    n = x.shape[0] // 3
    return x[:n] + (x[n : 2 * n] + x[2 * n :])


STEP_ROWS = 16
CHUNKS = 4


def fill_table(ids_ref, turned):
    length = TAPS * P_SIZE
    shape = (TAPS, P_SIZE)
    at = (
        lax.broadcasted_iota(jnp.int32, shape, 0) * P_SIZE
        + lax.broadcasted_iota(jnp.int32, shape, 1)
    ).astype(F32)
    angle = math.pi * ((at + 0.5 - length / 2.0) / P_SIZE)
    window = jnp.sin(angle) / angle * (0.5 - 0.5 * jnp.cos(2.0 * math.pi * (at + 0.5) / length))
    window = window / jnp.sqrt(jnp.sum(window * window))
    row = lax.broadcasted_iota(jnp.int32, (RC, P_SIZE), 0)
    point = lax.broadcasted_iota(jnp.int32, (RC, P_SIZE), 1)
    channel = jnp.where(row >= CHANNELS, row - CHANNELS, row)
    ids = jnp.zeros((RC, P_SIZE), jnp.int32)
    for c in range(CHANNELS):
        ids = jnp.where(channel == c, ids_ref[c], ids)
    angles = 2.0 * math.pi / P_SIZE * ((ids * point) % P_SIZE).astype(F32)
    rotors = jnp.where(row < CHANNELS, jnp.cos(angles), -jnp.sin(angles))
    turned[...] = jnp.zeros((256, SPAN), F32)
    for m in range(TAPS):
        taps = window[m : m + 1] * rotors
        for q in range(PHASES):
            turned[q * RC : (q + 1) * RC, (q + m) * P_SIZE : (q + m + 1) * P_SIZE] = taps


def channelize_kernel(ids_ref, x_hbm, o_ref, x_ref, turned, table, wide, tall, sems):
    step = ROWS // CHUNKS * PHASES * P_SIZE
    halo = (TAPS - 1) * P_SIZE
    copies = []
    for k in range(CHUNKS):
        low = k * step + (halo if k else 0)
        lanes = pl.ds(low, (k + 1) * step + halo - low)
        copies.append(
            pltpu.make_async_copy(x_hbm.at[:, lanes], x_ref.at[:, lanes], sems.at[k])
        )
        copies[-1].start()
    fill_table(ids_ref, turned)
    for k in range(SPAN // P_SIZE):
        lanes = slice(k * P_SIZE, (k + 1) * P_SIZE)
        table[lanes] = turned[:, lanes].T.astype(BF16)

    def filter_rows(at, carry):
        rows = []
        for k in range(STEP_ROWS):
            start = pl.multiple_of((at * STEP_ROWS + k) * (PHASES * P_SIZE), 128)
            rows.append(x_ref[:, pl.ds(start, SPAN)])
        got = dot_nn(jnp.concatenate(rows, axis=0), table[...])
        got = got.reshape(STEP_ROWS // 4, 4, LOCAL, 256)
        for k in range(STEP_ROWS // 4):
            owner = at * (STEP_ROWS // 4) + k
            y, z, core = owner // (NZ * NC), owner // NC % NZ, owner % NC
            wide[pl.ds((y * NC + core) * 16 + z * 4, 4)] = got[k]
        return carry

    for k in range(CHUNKS):
        copies[k].wait()
        each = ROWS // STEP_ROWS // CHUNKS
        lax.fori_loop(k * each, (k + 1) * each, filter_rows, 0)

    for n in range(LOCAL):
        turned_n = jnp.concatenate(
            [wide[:, n, 0:128].T, wide[:, n, 128:256].T[0 : PHASES * RC - 128]], axis=0
        )
        for q in range(PHASES):
            tall[:, n, q * 128 : (q + 1) * 128] = turned_n[q * RC : (q + 1) * RC]

    for x in range(NX):
        for z in range(NZ):
            for r in range(2):
                if z < GROUP:
                    o_ref[x * NZ + z, r] = tall[r * CHANNELS + x * GROUP + z].astype(BF16)
                else:
                    o_ref[x * NZ + z, r] = jnp.zeros((LOCAL, SPECTRA), BF16)


def channelize(ids, x):
    return pl.pallas_call(
        channelize_kernel,
        out_shape=jax.ShapeDtypeStruct((NX * NZ, 2, LOCAL, SPECTRA), BF16),
        in_specs=[pl.BlockSpec(memory_space=pltpu.SMEM), pl.BlockSpec(memory_space=pltpu.HBM)],
        out_specs=in_vmem,
        scratch_shapes=[
            pltpu.VMEM(x.shape, BF16),
            pltpu.VMEM((256, SPAN), F32),
            pltpu.VMEM((SPAN, 256), BF16),
            pltpu.VMEM((ROWS, LOCAL, 256), F32),
            pltpu.VMEM((RC, LOCAL, SPECTRA), F32),
            pltpu.SemaphoreType.DMA((CHUNKS,)),
        ],
        compiler_params=params(58),
        cost_estimate=cost(8),
    )(ids, x)


PAD = 128
TURN_ROWS = GROUP * 2 * SHARE


def spread_kernel(y_ref, v_ref, *outs):
    row = lax.broadcasted_iota(jnp.int32, (SPECTRA, NC * PAD), 0)
    col = lax.broadcasted_iota(jnp.int32, (1, NC * PAD), 1)
    inside = col % PAD
    wanted = (inside // 16) * ROWS + (col // PAD) * 16 + inside % 16
    wanted = jnp.where(inside < PHASES * 16, wanted, -SPECTRA)
    rows = [v_ref[c // GROUP * NZ + c % GROUP].reshape(2 * LOCAL, SPECTRA) for c in range(CHANNELS)]
    rows = jnp.concatenate(rows, axis=0)
    for d in range(NY):
        y = (y_ref[0] + d) % NY
        pick = jnp.where(row == wanted + y * (NC * 16), 1.0, 0.0).astype(BF16)
        got = dot_nn(rows, pick).astype(BF16).reshape(RC, LOCAL, NC * PAD)
        for core in range(NC):
            outs[d][core] = got[:, :, core * PAD : (core + 1) * PAD]


def spread(y, v):
    return pl.pallas_call(
        spread_kernel,
        out_shape=[jax.ShapeDtypeStruct((NC, RC, LOCAL, PAD), BF16)] * NY,
        in_specs=[pl.BlockSpec(memory_space=pltpu.SMEM), in_vmem],
        out_specs=[in_vmem] * NY,
        compiler_params=params(16),
        cost_estimate=cost(4),
    )(y, v)


def turn_kernel(at_ref, *refs):
    parts, o_ref = refs[:-1], refs[-1]
    core = at_ref[1]
    row = lax.broadcasted_iota(jnp.int32, (NZ * SHARE, PAD), 0)
    col = lax.broadcasted_iota(jnp.int32, (NZ * SHARE, PAD), 1)
    z, s = row // SHARE, row % SHARE
    pick = (col == (s % PHASES) * 16 + z * 4 + s // PHASES)
    pick = jnp.where(pick, 1.0, 0.0).astype(BF16)
    for other in range(NC):
        side = core if other == 0 else 1 - core
        for x in range(NX):
            blocks = []
            for rc in range(0, 2 * GROUP, 2):
                at = x * 2 * GROUP + rc
                stack = jnp.concatenate(
                    [parts[d][side, at + k] for k in range(2) for d in range(NY)], axis=0
                )
                got = dot_nt(pick, stack)
                blocks += [got[:, 0 : NY * LOCAL], got[:, NY * LOCAL :]]
            for z_to in range(NZ):
                rows = slice(z_to * SHARE, (z_to + 1) * SHARE)
                o_ref[x * NZ + z_to, other] = jnp.concatenate(
                    [g[rows] for g in blocks], axis=0
                ).astype(BF16)


def turn(at, parts):
    return pl.pallas_call(
        turn_kernel,
        out_shape=jax.ShapeDtypeStruct((NX * NZ, NC, TURN_ROWS, NY * LOCAL), BF16),
        in_specs=[pl.BlockSpec(memory_space=pltpu.SMEM)] + [in_vmem] * NY,
        out_specs=in_vmem,
        compiler_params=params(16),
        cost_estimate=cost(3),
    )(at, *parts)


def halves(v_ref):
    return v_ref[:, 0].reshape(HELD, SPECTRA), v_ref[:, 1].reshape(HELD, SPECTRA)


def project(v_halves, pieces):
    a, b = sum3(dot_nn(pieces, v_halves[0])), sum3(dot_nn(pieces, v_halves[1]))
    return a[0:KDIM] + b[KDIM:], a[KDIM:] - b[0:KDIM]


def expand(v_halves, pieces):
    a, b = sum3(dot_nt(pieces, v_halves[0])), sum3(dot_nt(pieces, v_halves[1]))
    return a[0:KDIM] - b[KDIM:], a[KDIM:] + b[0:KDIM]


def gram_from(products):
    p0, p1, p2 = products[0:16], products[16:32], products[32:48]
    m = (p0 + (p1 + p2)) + pltpu.roll(p0 + p1, 112, 1) + pltpu.roll(p0, 96, 1)
    up, down = m[0:KDIM], m[KDIM:]
    return up + pltpu.roll(down, 120, 1), down - pltpu.roll(up, 120, 1)


def eliminate(gram, others):
    row_id = lax.broadcasted_iota(jnp.int32, gram[0].shape[:-1] + (1,), gram[0].ndim - 2)
    pairs = [gram] + list(others)
    for j in range(KDIM):
        gram_re, gram_im = pairs[0]
        scale = 1.0 / jnp.sqrt(gram_re[..., j : j + 1, j : j + 1])
        below = jnp.where(row_id > j, scale, 0.0)
        m_re, m_im = gram_re[..., j : j + 1] * below, gram_im[..., j : j + 1] * below
        done = []
        for re, im in pairs:
            top_re, top_im = re[..., j : j + 1, :] * scale, im[..., j : j + 1, :] * scale
            new_re = re - (m_re * top_re - m_im * top_im)
            new_im = im - (m_re * top_im + m_im * top_re)
            here = row_id == j
            done.append((jnp.where(here, top_re, new_re), jnp.where(here, top_im, new_im)))
        pairs = done
    return pairs


def first_kernel(v_ref, q_ref, s_ref):
    u_re, u_im = project(halves(v_ref), split3(q_ref[...]))
    s_ref[...] = jnp.concatenate([u_re, u_im], axis=0)


def step_kernel(step, v_ref, z_ref, s0, s1, s2, s3, *outs):
    s = (s0[...] + s2[...]) + (s1[...] + s3[...])
    w = (s[0:KDIM, 0:SPECTRA], s[KDIM:, 0:SPECTRA])
    q = (z_ref[0:KDIM], z_ref[KDIM:])
    if step > 0:
        gram = (s[0:KDIM, SPECTRA:], s[KDIM:, SPECTRA:])
        _, w, q = eliminate(gram, [w, q])
    v = halves(v_ref)
    i_re, i_im = expand(v, split3(jnp.concatenate(w, axis=0)))
    z_re = i_re * (1.0 / SPECTRA) + LOADING * q[0]
    z_im = i_im * (1.0 / SPECTRA) + LOADING * q[1]
    z = jnp.concatenate([z_re, z_im], axis=0)
    if step == 2:
        (many_ref,) = outs
        for d in range(NY * NZ):
            many_ref[d] = z
        return
    new_z, new_s = outs
    new_z[...] = z
    pieces = split3(z)
    u_re, u_im = project(v, pieces)
    padded = jnp.concatenate([pieces, jnp.zeros((80, HELD), BF16)], axis=0)
    g_re, g_im = gram_from(dot_nt(pieces, padded))
    new_s[0:KDIM, 0:SPECTRA] = u_re
    new_s[KDIM:, 0:SPECTRA] = u_im
    new_s[0:KDIM, SPECTRA:] = g_re
    new_s[KDIM:, SPECTRA:] = g_im


def first(v, q):
    return pl.pallas_call(
        first_kernel,
        out_shape=jax.ShapeDtypeStruct((2 * KDIM, SPECTRA), F32),
        in_specs=[in_vmem] * 2,
        out_specs=in_vmem,
        compiler_params=params(12),
        cost_estimate=cost(2),
    )(v, q)


def step(at, v, z, sums):
    if at == 2:
        shapes = [jax.ShapeDtypeStruct((NY * NZ, 2 * KDIM, HELD), F32)]
    else:
        shapes = [
            jax.ShapeDtypeStruct((2 * KDIM, HELD), F32),
            jax.ShapeDtypeStruct((2 * KDIM, SPECTRA + 128), F32),
        ]
    return pl.pallas_call(
        functools.partial(step_kernel, at),
        out_shape=shapes,
        in_specs=[in_vmem] * 6,
        out_specs=[in_vmem] * len(shapes),
        compiler_params=params(12),
        cost_estimate=cost(5),
    )(v, z, *sums)


def placing(y, core):
    side = NY * NZ * NC * LOCAL
    row = lax.broadcasted_iota(jnp.int32, (side, side), 0)
    col = lax.broadcasted_iota(jnp.int32, (side, side), 1)
    to_y, to_z, to_core, i = col // 256, (col // 64) % 4, (col // 32) % 2, col % 32
    source = to_z * 256 + ((to_core + core) % 2) * 128 + ((y - to_y) % 4) * 32 + i
    return jnp.where(row == source, 1.0, 0.0).astype(BF16)


def arrange_kernel(mine_ref, theirs_ref, place_ref, flat):
    rows = []
    for x in range(NX):
        parts = []
        for z in range(NZ):
            parts += [mine_ref[x * NZ + z], theirs_ref[x * NZ + z]]
        rows.append(jnp.concatenate(parts, axis=1))
    got = dot_nn(jnp.concatenate(rows, axis=0), place_ref[...])
    flat[...] = got.reshape(NX, GROUP, 2 * SHARE, NY * 256)


def arrange(mine, theirs, place):
    return pl.pallas_call(
        arrange_kernel,
        out_shape=jax.ShapeDtypeStruct((NX, GROUP, 2 * SHARE, NY * 256), F32),
        in_specs=[in_vmem] * 3,
        out_specs=in_vmem,
        compiler_params=params(16),
        cost_estimate=cost(4),
    )(mine, theirs, place)


def final_kernel(flat, own_ref, far_ref, core_ref, o_hbm, basis, result, sems):
    lane = lax.broadcasted_iota(jnp.int32, (2 * KDIM, 128), 1) // 32
    is_zero = core_ref[1] == 0
    wide = NY * 256
    solved = []
    for z in range(GROUP):
        products = jnp.zeros((48, 128), F32)
        for x in range(NX):
            lanes = slice(x * 128, (x + 1) * 128)
            for y in range(NY):
                own, far = own_ref[y * NZ + z, :, lanes], far_ref[y * NZ + z, :, lanes]
                a, b = jnp.where(is_zero, own, far), jnp.where(is_zero, far, own)
                left = jnp.where(
                    lane < 2,
                    jnp.where(lane == 0, a, pltpu.roll(b, 32, 1)),
                    jnp.where(lane == 2, pltpu.roll(a, 32, 1), pltpu.roll(b, 64, 1)),
                )
                right = jnp.where(
                    lane < 2,
                    jnp.where(lane == 0, pltpu.roll(a, 64, 1), pltpu.roll(b, 96, 1)),
                    jnp.where(lane == 2, pltpu.roll(a, 96, 1), b),
                )
                at = (x * NY + y) * 256
                for k, part in enumerate((left, right)):
                    basis[z, :, at + k * 128 : at + (k + 1) * 128] = split3(part)
            pieces = basis[z, :, x * wide : (x + 1) * wide]
            block = flat[x, z].astype(BF16)
            right = jnp.concatenate([pieces, block, jnp.zeros((32, wide), BF16)], axis=0)
            products = products + dot_nt(pieces, right)
        g_re, g_im = gram_from(products)
        up_down = sum3(products)
        up, down = up_down[0:KDIM], up_down[KDIM:]
        u_re = up + pltpu.roll(down, 104, 1)
        u_im = down - pltpu.roll(up, 104, 1)
        solved.append((g_re, g_im, u_re, u_im))

    lane = lax.broadcasted_iota(jnp.int32, (KDIM, 128), 1)
    unit = lane == lax.broadcasted_iota(jnp.int32, (KDIM, 128), 0) + KDIM
    unit_lanes = (lane >= KDIM) & (lane < 2 * KDIM)
    u_lanes = (lane >= 48) & (lane < 72)
    used = lane < 72
    all_re, all_im = [], []
    for g_re, g_im, u_re, u_im in solved:
        x_re = jnp.where(u_lanes, u_re, jnp.where(unit_lanes, jnp.where(unit, 1.0, 0.0), g_re))
        x_im = jnp.where(u_lanes, u_im, jnp.where(unit_lanes, 0.0, g_im))
        all_re.append(jnp.where(used, x_re, 0.0))
        all_im.append(jnp.where(used, x_im, 0.0))
    ((all_re, all_im),) = eliminate((jnp.stack(all_re), jnp.stack(all_im)), [])

    def sides(a, b):
        near, away = pltpu.roll(a, 80, 1), pltpu.roll(b, 104, 1)
        return jnp.where(lane < SHARE, near, jnp.where(lane < 2 * SHARE, away, 0.0))

    lefts = []
    for z in range(GROUP):
        x_re, x_im = all_re[z], all_im[z]
        both = jnp.concatenate([x_re, x_im], axis=0)
        cross = jnp.concatenate([x_im, -x_re], axis=0)
        t_re = dot_tn(both, both, lax.Precision.HIGHEST)[KDIM : 2 * KDIM]
        t_im = dot_tn(cross, both, lax.Precision.HIGHEST)[KDIM : 2 * KDIM]
        t = split3(jnp.concatenate([sides(t_re, t_im), sides(-t_im, t_re)], axis=0))
        hi, mid, lo = t[0:16], t[16:32], t[32:48]
        lefts.append(jnp.concatenate([hi, hi, hi, mid, mid, lo], axis=0))
    copies = []
    for z in range(GROUP):
        for x in range(NX):
            lanes = slice(x * wide, (x + 1) * wide)
            pieces = basis[z, :, lanes]
            right = jnp.concatenate([pieces, pieces[0:32], pieces[0:16]], axis=0)
            rest = flat[x, z] - dot_tn(lefts[z], right)[0 : 2 * SHARE]
            result[0, z, :, lanes] = rest[0:SHARE]
            result[1, z, :, lanes] = rest[SHARE:]
        for r in range(2):
            copies.append(
                pltpu.make_async_copy(result.at[r, z], o_hbm.at[r, z], sems.at[r, z])
            )
            copies[-1].start()
    for copy in copies:
        copy.wait()


def finish(flat, own, far, at):
    return pl.pallas_call(
        final_kernel,
        out_shape=jax.ShapeDtypeStruct((2, GROUP, SHARE, INPUTS), F32),
        in_specs=[in_vmem] * 3 + [pl.BlockSpec(memory_space=pltpu.SMEM)],
        out_specs=pl.BlockSpec(memory_space=pltpu.HBM),
        scratch_shapes=[
            pltpu.VMEM((GROUP, 6 * KDIM, INPUTS), BF16),
            pltpu.VMEM((2, GROUP, SHARE, INPUTS), F32),
            pltpu.SemaphoreType.DMA((2, GROUP)),
        ],
        compiler_params=params(16),
        cost_estimate=cost(6),
    )(flat, own, far, at)


def turned_by(count, distance):
    return [(i, (i + distance) % count) for i in range(count)]


def sums_over(s):
    return [s] + [lax.ppermute(s, "y", turned_by(NY, d)) for d in range(1, NY)]


def core_sum(s):
    return s + lax.ppermute(s, "core", turned_by(NC, 1))


def body(voltages, channel_ids, start_basis):
    y, core = lax.axis_index("y"), lax.axis_index("core")
    at = jnp.stack([y, core]).astype(jnp.int32)
    parcels = channelize(channel_ids, voltages)
    v = lax.all_to_all(parcels, ("x", "z"), 0, 0, tiled=True)
    parts = spread(at, parcels)
    parts = [parts[0]] + [lax.ppermute(parts[d], "y", turned_by(NY, d)) for d in range(1, NY)]
    turned = turn(at, parts)
    split = start_basis.reshape(2 * KDIM, NX, NY, NZ, NC, LOCAL)
    split = lax.dynamic_index_in_dim(split, y, 2, keepdims=False)
    z = lax.dynamic_index_in_dim(split, core, 3, keepdims=False).reshape(2 * KDIM, HELD)
    s = core_sum(first(v, z))
    sums = sums_over(s)
    turned = lax.optimization_barrier((turned, s))[0]
    blocks = lax.all_to_all(turned, ("x", "z"), 0, 0, tiled=True)
    place = placing(y, core)
    z, s = step(0, v, z, sums)
    z, s = step(1, v, z, sums_over(core_sum(s)))
    s, blocks = lax.optimization_barrier((core_sum(s), blocks))
    sums = sums_over(s)
    mine, theirs = blocks[:, 0], lax.ppermute(blocks[:, 1], "core", turned_by(NC, 1))
    flat = arrange(mine, theirs, place)
    z, flat = lax.optimization_barrier((z, flat))
    (many,) = step(2, v, z, sums)
    own = lax.all_to_all(many, ("y", "z"), 0, 0, tiled=True)
    far = lax.ppermute(own, "core", turned_by(NC, 1))
    return finish(flat, own, far, at)


def solution(mesh):
    fine = Mesh(mesh.devices.reshape(NX, NY, NZ, NC), ("x", "y", "z", "core"))
    in_specs = (P(("x", "y", "z", "core"), None), P(), P())
    out_specs = P(None, "x", ("y", "z", "core"), None)
    return jax.shard_map(body, mesh=fine, in_specs=in_specs, out_specs=out_specs, check_vma=False)
```

```python
import functools
import math

import jax
import jax.numpy as jnp
from jax import lax
from jax.experimental import pallas as pl
from jax.experimental.pallas import tpu as pltpu
from jax.sharding import Mesh, PartitionSpec as P

TAPS = 4
P_SIZE = 128
INPUTS = 4096
KDIM = 8
CHANNELS = 12
SPECTRA = 768
LOADING = 0.5

NX, NY, NZ, NC = 4, 4, 4, 2
LOCAL = INPUTS // (NX * NY * NZ * NC)
GROUP = CHANNELS // NX
HELD = LOCAL * NX * NZ
PHASES = 6
ROWS = SPECTRA // PHASES
SPAN = (PHASES + TAPS - 1) * P_SIZE
SHARE = SPECTRA // (NY * NZ * NC)
RC = 2 * CHANNELS

F32, BF16 = jnp.float32, jnp.bfloat16


def params(mib):
    return pltpu.CompilerParams(vmem_limit_bytes=mib * 1024 * 1024)


def cost(microseconds):
    return pl.CostEstimate(flops=int(microseconds * 9e8), bytes_accessed=int(microseconds * 3e6), transcendentals=0)


in_vmem = pl.BlockSpec(memory_space=pltpu.VMEM)


def dot_nn(a, b):
    return lax.dot_general(a, b, (((1,), (0,)), ((), ())), preferred_element_type=F32)


def dot_nt(a, b):
    return lax.dot_general(a, b, (((1,), (1,)), ((), ())), preferred_element_type=F32)


def dot_tn(a, b, precision=None):
    return lax.dot_general(
        a, b, (((0,), (0,)), ((), ())), preferred_element_type=F32, precision=precision
    )


def split3(x):
    hi = x.astype(BF16)
    rest = x - hi.astype(F32)
    mid = rest.astype(BF16)
    lo = (rest - mid.astype(F32)).astype(BF16)
    return jnp.concatenate([hi, mid, lo], axis=0)


def sum3(x):
    n = x.shape[0] // 3
    return x[:n] + (x[n : 2 * n] + x[2 * n :])


STEP_ROWS = 16
CHUNKS = 4


def fill_table(ids_ref, turned):
    length = TAPS * P_SIZE
    shape = (TAPS, P_SIZE)
    at = (
        lax.broadcasted_iota(jnp.int32, shape, 0) * P_SIZE
        + lax.broadcasted_iota(jnp.int32, shape, 1)
    ).astype(F32)
    angle = math.pi * ((at + 0.5 - length / 2.0) / P_SIZE)
    window = jnp.sin(angle) / angle * (0.5 - 0.5 * jnp.cos(2.0 * math.pi * (at + 0.5) / length))
    window = window / jnp.sqrt(jnp.sum(window * window))
    row = lax.broadcasted_iota(jnp.int32, (RC, P_SIZE), 0)
    point = lax.broadcasted_iota(jnp.int32, (RC, P_SIZE), 1)
    channel = jnp.where(row >= CHANNELS, row - CHANNELS, row)
    ids = jnp.zeros((RC, P_SIZE), jnp.int32)
    for c in range(CHANNELS):
        ids = jnp.where(channel == c, ids_ref[c], ids)
    angles = 2.0 * math.pi / P_SIZE * ((ids * point) % P_SIZE).astype(F32)
    rotors = jnp.where(row < CHANNELS, jnp.cos(angles), -jnp.sin(angles))
    turned[...] = jnp.zeros((256, SPAN), F32)
    for m in range(TAPS):
        taps = window[m : m + 1] * rotors
        for q in range(PHASES):
            turned[q * RC : (q + 1) * RC, (q + m) * P_SIZE : (q + m + 1) * P_SIZE] = taps


def channelize_kernel(ids_ref, x_hbm, o_ref, x_ref, turned, table, wide, tall, sems):
    step = ROWS // CHUNKS * PHASES * P_SIZE
    halo = (TAPS - 1) * P_SIZE
    copies = []
    for k in range(CHUNKS):
        low = k * step + (halo if k else 0)
        lanes = pl.ds(low, (k + 1) * step + halo - low)
        copies.append(
            pltpu.make_async_copy(x_hbm.at[:, lanes], x_ref.at[:, lanes], sems.at[k])
        )
        copies[-1].start()
    fill_table(ids_ref, turned)
    for k in range(SPAN // P_SIZE):
        lanes = slice(k * P_SIZE, (k + 1) * P_SIZE)
        table[lanes] = turned[:, lanes].T.astype(BF16)

    def filter_rows(at, carry):
        rows = []
        for k in range(STEP_ROWS):
            start = pl.multiple_of((at * STEP_ROWS + k) * (PHASES * P_SIZE), 128)
            rows.append(x_ref[:, pl.ds(start, SPAN)])
        got = dot_nn(jnp.concatenate(rows, axis=0), table[...])
        got = got.reshape(STEP_ROWS // 4, 4, LOCAL, 256)
        for k in range(STEP_ROWS // 4):
            owner = at * (STEP_ROWS // 4) + k
            y, z, core = owner // (NZ * NC), owner // NC % NZ, owner % NC
            wide[pl.ds((y * NC + core) * 16 + z * 4, 4)] = got[k]
        return carry

    for k in range(CHUNKS):
        copies[k].wait()
        each = ROWS // STEP_ROWS // CHUNKS
        lax.fori_loop(k * each, (k + 1) * each, filter_rows, 0)

    for n in range(LOCAL):
        turned_n = jnp.concatenate(
            [wide[:, n, 0:128].T, wide[:, n, 128:256].T[0 : PHASES * RC - 128]], axis=0
        )
        for q in range(PHASES):
            tall[:, n, q * 128 : (q + 1) * 128] = turned_n[q * RC : (q + 1) * RC]

    for x in range(NX):
        for z in range(NZ):
            for r in range(2):
                if z < GROUP:
                    o_ref[x * NZ + z, r] = tall[r * CHANNELS + x * GROUP + z].astype(BF16)
                else:
                    o_ref[x * NZ + z, r] = jnp.zeros((LOCAL, SPECTRA), BF16)


def channelize(ids, x):
    return pl.pallas_call(
        channelize_kernel,
        out_shape=jax.ShapeDtypeStruct((NX * NZ, 2, LOCAL, SPECTRA), BF16),
        in_specs=[pl.BlockSpec(memory_space=pltpu.SMEM), pl.BlockSpec(memory_space=pltpu.HBM)],
        out_specs=in_vmem,
        scratch_shapes=[
            pltpu.VMEM(x.shape, BF16),
            pltpu.VMEM((256, SPAN), F32),
            pltpu.VMEM((SPAN, 256), BF16),
            pltpu.VMEM((ROWS, LOCAL, 256), F32),
            pltpu.VMEM((RC, LOCAL, SPECTRA), F32),
            pltpu.SemaphoreType.DMA((CHUNKS,)),
        ],
        compiler_params=params(58),
        cost_estimate=cost(8),
    )(ids, x)


PAD = 128
TURN_ROWS = GROUP * 2 * SHARE


def spread_kernel(y_ref, v_ref, *outs):
    row = lax.broadcasted_iota(jnp.int32, (SPECTRA, NC * PAD), 0)
    col = lax.broadcasted_iota(jnp.int32, (1, NC * PAD), 1)
    inside = col % PAD
    wanted = (inside // 16) * ROWS + (col // PAD) * 16 + inside % 16
    wanted = jnp.where(inside < PHASES * 16, wanted, -SPECTRA)
    rows = [v_ref[c // GROUP * NZ + c % GROUP].reshape(2 * LOCAL, SPECTRA) for c in range(CHANNELS)]
    rows = jnp.concatenate(rows, axis=0)
    for d in range(NY):
        y = (y_ref[0] + d) % NY
        pick = jnp.where(row == wanted + y * (NC * 16), 1.0, 0.0).astype(BF16)
        got = dot_nn(rows, pick).astype(BF16).reshape(RC, LOCAL, NC * PAD)
        for core in range(NC):
            outs[d][core] = got[:, :, core * PAD : (core + 1) * PAD]


def spread(y, v):
    return pl.pallas_call(
        spread_kernel,
        out_shape=[jax.ShapeDtypeStruct((NC, RC, LOCAL, PAD), BF16)] * NY,
        in_specs=[pl.BlockSpec(memory_space=pltpu.SMEM), in_vmem],
        out_specs=[in_vmem] * NY,
        compiler_params=params(16),
        cost_estimate=cost(4),
    )(y, v)


def turn_kernel(at_ref, *refs):
    parts, o_ref = refs[:-1], refs[-1]
    core = at_ref[1]
    row = lax.broadcasted_iota(jnp.int32, (NZ * SHARE, PAD), 0)
    col = lax.broadcasted_iota(jnp.int32, (NZ * SHARE, PAD), 1)
    z, s = row // SHARE, row % SHARE
    pick = (col == (s % PHASES) * 16 + z * 4 + s // PHASES)
    pick = jnp.where(pick, 1.0, 0.0).astype(BF16)
    for other in range(NC):
        side = core if other == 0 else 1 - core
        for x in range(NX):
            blocks = []
            for rc in range(0, 2 * GROUP, 2):
                at = x * 2 * GROUP + rc
                stack = jnp.concatenate(
                    [parts[d][side, at + k] for k in range(2) for d in range(NY)], axis=0
                )
                got = dot_nt(pick, stack)
                blocks += [got[:, 0 : NY * LOCAL], got[:, NY * LOCAL :]]
            for z_to in range(NZ):
                rows = slice(z_to * SHARE, (z_to + 1) * SHARE)
                o_ref[x * NZ + z_to, other] = jnp.concatenate(
                    [g[rows] for g in blocks], axis=0
                ).astype(BF16)


def turn(at, parts):
    return pl.pallas_call(
        turn_kernel,
        out_shape=jax.ShapeDtypeStruct((NX * NZ, NC, TURN_ROWS, NY * LOCAL), BF16),
        in_specs=[pl.BlockSpec(memory_space=pltpu.SMEM)] + [in_vmem] * NY,
        out_specs=in_vmem,
        compiler_params=params(16),
        cost_estimate=cost(3),
    )(at, *parts)


def halves(v_ref):
    return v_ref[:, 0].reshape(HELD, SPECTRA), v_ref[:, 1].reshape(HELD, SPECTRA)


def project(v_halves, pieces):
    a, b = sum3(dot_nn(pieces, v_halves[0])), sum3(dot_nn(pieces, v_halves[1]))
    return a[0:KDIM] + b[KDIM:], a[KDIM:] - b[0:KDIM]


def expand(v_halves, pieces):
    a, b = sum3(dot_nt(pieces, v_halves[0])), sum3(dot_nt(pieces, v_halves[1]))
    return a[0:KDIM] - b[KDIM:], a[KDIM:] + b[0:KDIM]


def gram_from(products):
    p0, p1, p2 = products[0:16], products[16:32], products[32:48]
    m = (p0 + (p1 + p2)) + pltpu.roll(p0 + p1, 112, 1) + pltpu.roll(p0, 96, 1)
    up, down = m[0:KDIM], m[KDIM:]
    return up + pltpu.roll(down, 120, 1), down - pltpu.roll(up, 120, 1)


def eliminate(gram, others):
    row_id = lax.broadcasted_iota(jnp.int32, gram[0].shape[:-1] + (1,), gram[0].ndim - 2)
    pairs = [gram] + list(others)
    for j in range(KDIM):
        gram_re, gram_im = pairs[0]
        scale = 1.0 / jnp.sqrt(gram_re[..., j : j + 1, j : j + 1])
        below = jnp.where(row_id > j, scale, 0.0)
        m_re, m_im = gram_re[..., j : j + 1] * below, gram_im[..., j : j + 1] * below
        done = []
        for re, im in pairs:
            top_re, top_im = re[..., j : j + 1, :] * scale, im[..., j : j + 1, :] * scale
            new_re = re - (m_re * top_re - m_im * top_im)
            new_im = im - (m_re * top_im + m_im * top_re)
            here = row_id == j
            done.append((jnp.where(here, top_re, new_re), jnp.where(here, top_im, new_im)))
        pairs = done
    return pairs


def first_kernel(v_ref, q_ref, s_ref):
    u_re, u_im = project(halves(v_ref), split3(q_ref[...]))
    s_ref[...] = jnp.concatenate([u_re, u_im], axis=0)


def step_kernel(step, v_ref, z_ref, s0, s1, s2, s3, *outs):
    s = (s0[...] + s2[...]) + (s1[...] + s3[...])
    w = (s[0:KDIM, 0:SPECTRA], s[KDIM:, 0:SPECTRA])
    q = (z_ref[0:KDIM], z_ref[KDIM:])
    if step > 0:
        gram = (s[0:KDIM, SPECTRA:], s[KDIM:, SPECTRA:])
        _, w, q = eliminate(gram, [w, q])
    v = halves(v_ref)
    i_re, i_im = expand(v, split3(jnp.concatenate(w, axis=0)))
    z_re = i_re * (1.0 / SPECTRA) + LOADING * q[0]
    z_im = i_im * (1.0 / SPECTRA) + LOADING * q[1]
    z = jnp.concatenate([z_re, z_im], axis=0)
    if step == 2:
        (many_ref,) = outs
        for d in range(NY * NZ):
            many_ref[d] = z
        return
    new_z, new_s = outs
    new_z[...] = z
    pieces = split3(z)
    u_re, u_im = project(v, pieces)
    padded = jnp.concatenate([pieces, jnp.zeros((80, HELD), BF16)], axis=0)
    g_re, g_im = gram_from(dot_nt(pieces, padded))
    new_s[0:KDIM, 0:SPECTRA] = u_re
    new_s[KDIM:, 0:SPECTRA] = u_im
    new_s[0:KDIM, SPECTRA:] = g_re
    new_s[KDIM:, SPECTRA:] = g_im


def first(v, q):
    return pl.pallas_call(
        first_kernel,
        out_shape=jax.ShapeDtypeStruct((2 * KDIM, SPECTRA), F32),
        in_specs=[in_vmem] * 2,
        out_specs=in_vmem,
        compiler_params=params(12),
        cost_estimate=cost(2),
    )(v, q)


def step(at, v, z, sums):
    if at == 2:
        shapes = [jax.ShapeDtypeStruct((NY * NZ, 2 * KDIM, HELD), F32)]
    else:
        shapes = [
            jax.ShapeDtypeStruct((2 * KDIM, HELD), F32),
            jax.ShapeDtypeStruct((2 * KDIM, SPECTRA + 128), F32),
        ]
    return pl.pallas_call(
        functools.partial(step_kernel, at),
        out_shape=shapes,
        in_specs=[in_vmem] * 6,
        out_specs=[in_vmem] * len(shapes),
        compiler_params=params(12),
        cost_estimate=cost(5),
    )(v, z, *sums)


def placing(y, core):
    side = NY * NZ * NC * LOCAL
    row = lax.broadcasted_iota(jnp.int32, (side, side), 0)
    col = lax.broadcasted_iota(jnp.int32, (side, side), 1)
    to_y, to_z, to_core, i = col // 256, (col // 64) % 4, (col // 32) % 2, col % 32
    source = to_z * 256 + ((to_core + core) % 2) * 128 + ((y - to_y) % 4) * 32 + i
    return jnp.where(row == source, 1.0, 0.0).astype(BF16)


def arrange_kernel(mine_ref, theirs_ref, place_ref, flat):
    rows = []
    for x in range(NX):
        parts = []
        for z in range(NZ):
            parts += [mine_ref[x * NZ + z], theirs_ref[x * NZ + z]]
        rows.append(jnp.concatenate(parts, axis=1))
    got = dot_nn(jnp.concatenate(rows, axis=0), place_ref[...])
    flat[...] = got.reshape(NX, GROUP, 2 * SHARE, NY * 256)


def arrange(mine, theirs, place):
    return pl.pallas_call(
        arrange_kernel,
        out_shape=jax.ShapeDtypeStruct((NX, GROUP, 2 * SHARE, NY * 256), F32),
        in_specs=[in_vmem] * 3,
        out_specs=in_vmem,
        compiler_params=params(16),
        cost_estimate=cost(4),
    )(mine, theirs, place)


def final_kernel(flat, own_ref, far_ref, core_ref, o_hbm, basis, result, sems):
    lane = lax.broadcasted_iota(jnp.int32, (2 * KDIM, 128), 1) // 32
    is_zero = core_ref[1] == 0
    wide = NY * 256
    solved = []
    for z in range(GROUP):
        products = jnp.zeros((48, 128), F32)
        for x in range(NX):
            lanes = slice(x * 128, (x + 1) * 128)
            for y in range(NY):
                own, far = own_ref[y * NZ + z, :, lanes], far_ref[y * NZ + z, :, lanes]
                a, b = jnp.where(is_zero, own, far), jnp.where(is_zero, far, own)
                left = jnp.where(
                    lane < 2,
                    jnp.where(lane == 0, a, pltpu.roll(b, 32, 1)),
                    jnp.where(lane == 2, pltpu.roll(a, 32, 1), pltpu.roll(b, 64, 1)),
                )
                right = jnp.where(
                    lane < 2,
                    jnp.where(lane == 0, pltpu.roll(a, 64, 1), pltpu.roll(b, 96, 1)),
                    jnp.where(lane == 2, pltpu.roll(a, 96, 1), b),
                )
                at = (x * NY + y) * 256
                for k, part in enumerate((left, right)):
                    basis[z, :, at + k * 128 : at + (k + 1) * 128] = split3(part)
            pieces = basis[z, :, x * wide : (x + 1) * wide]
            block = flat[x, z].astype(BF16)
            right = jnp.concatenate([pieces, block, jnp.zeros((32, wide), BF16)], axis=0)
            products = products + dot_nt(pieces, right)
        g_re, g_im = gram_from(products)
        up_down = sum3(products)
        up, down = up_down[0:KDIM], up_down[KDIM:]
        u_re = up + pltpu.roll(down, 104, 1)
        u_im = down - pltpu.roll(up, 104, 1)
        solved.append((g_re, g_im, u_re, u_im))

    lane = lax.broadcasted_iota(jnp.int32, (KDIM, 128), 1)
    unit = lane == lax.broadcasted_iota(jnp.int32, (KDIM, 128), 0) + KDIM
    unit_lanes = (lane >= KDIM) & (lane < 2 * KDIM)
    u_lanes = (lane >= 48) & (lane < 72)
    used = lane < 72
    all_re, all_im = [], []
    for g_re, g_im, u_re, u_im in solved:
        x_re = jnp.where(u_lanes, u_re, jnp.where(unit_lanes, jnp.where(unit, 1.0, 0.0), g_re))
        x_im = jnp.where(u_lanes, u_im, jnp.where(unit_lanes, 0.0, g_im))
        all_re.append(jnp.where(used, x_re, 0.0))
        all_im.append(jnp.where(used, x_im, 0.0))
    ((all_re, all_im),) = eliminate((jnp.stack(all_re), jnp.stack(all_im)), [])

    def sides(a, b):
        near, away = pltpu.roll(a, 80, 1), pltpu.roll(b, 104, 1)
        return jnp.where(lane < SHARE, near, jnp.where(lane < 2 * SHARE, away, 0.0))

    lefts = []
    for z in range(GROUP):
        x_re, x_im = all_re[z], all_im[z]
        both = jnp.concatenate([x_re, x_im], axis=0)
        cross = jnp.concatenate([x_im, -x_re], axis=0)
        t_re = dot_tn(both, both, lax.Precision.HIGHEST)[KDIM : 2 * KDIM]
        t_im = dot_tn(cross, both, lax.Precision.HIGHEST)[KDIM : 2 * KDIM]
        t = split3(jnp.concatenate([sides(t_re, t_im), sides(-t_im, t_re)], axis=0))
        hi, mid, lo = t[0:16], t[16:32], t[32:48]
        lefts.append(jnp.concatenate([hi, hi, hi, mid, mid, lo], axis=0))
    copies = []
    for z in range(GROUP):
        for x in range(NX):
            lanes = slice(x * wide, (x + 1) * wide)
            pieces = basis[z, :, lanes]
            right = jnp.concatenate([pieces, pieces[0:32], pieces[0:16]], axis=0)
            rest = flat[x, z] - dot_tn(lefts[z], right)[0 : 2 * SHARE]
            result[0, z, :, lanes] = rest[0:SHARE]
            result[1, z, :, lanes] = rest[SHARE:]
        for r in range(2):
            copies.append(
                pltpu.make_async_copy(result.at[r, z], o_hbm.at[r, z], sems.at[r, z])
            )
            copies[-1].start()
    for copy in copies:
        copy.wait()


def finish(flat, own, far, at):
    return pl.pallas_call(
        final_kernel,
        out_shape=jax.ShapeDtypeStruct((2, GROUP, SHARE, INPUTS), F32),
        in_specs=[in_vmem] * 3 + [pl.BlockSpec(memory_space=pltpu.SMEM)],
        out_specs=pl.BlockSpec(memory_space=pltpu.HBM),
        scratch_shapes=[
            pltpu.VMEM((GROUP, 6 * KDIM, INPUTS), BF16),
            pltpu.VMEM((2, GROUP, SHARE, INPUTS), F32),
            pltpu.SemaphoreType.DMA((2, GROUP)),
        ],
        compiler_params=params(16),
        cost_estimate=cost(6),
    )(flat, own, far, at)


def turned_by(count, distance):
    return [(i, (i + distance) % count) for i in range(count)]


def sums_over(s):
    return [s] + [lax.ppermute(s, "y", turned_by(NY, d)) for d in range(1, NY)]


def core_sum(s):
    return s + lax.ppermute(s, "core", turned_by(NC, 1))


def body(voltages, channel_ids, start_basis):
    y, core = lax.axis_index("y"), lax.axis_index("core")
    at = jnp.stack([y, core]).astype(jnp.int32)
    parcels = channelize(channel_ids, voltages)
    v = lax.all_to_all(parcels, ("x", "z"), 0, 0, tiled=True)
    parts = spread(at, parcels)
    parts = [parts[0]] + [lax.ppermute(parts[d], "y", turned_by(NY, d)) for d in range(1, NY)]
    turned = turn(at, parts)
    split = start_basis.reshape(2 * KDIM, NX, NY, NZ, NC, LOCAL)
    split = lax.dynamic_index_in_dim(split, y, 2, keepdims=False)
    z = lax.dynamic_index_in_dim(split, core, 3, keepdims=False).reshape(2 * KDIM, HELD)
    s = core_sum(first(v, z))
    sums = sums_over(s)
    turned = lax.optimization_barrier((turned, s))[0]
    blocks = lax.all_to_all(turned, ("x", "z"), 0, 0, tiled=True)
    place = placing(y, core)
    z, s = step(0, v, z, sums)
    z, s = step(1, v, z, sums_over(core_sum(s)))
    sums = sums_over(core_sum(s))
    tail, blocks = lax.optimization_barrier((sums[3], blocks))
    (many,) = step(2, v, z, sums[:3] + [tail])
    own = lax.all_to_all(many, ("y", "z"), 0, 0, tiled=True)
    mine, theirs = blocks[:, 0], lax.ppermute(blocks[:, 1], "core", turned_by(NC, 1))
    flat = arrange(mine, theirs, place)
    far = lax.ppermute(own, "core", turned_by(NC, 1))
    return finish(flat, own, far, at)


def solution(mesh):
    fine = Mesh(mesh.devices.reshape(NX, NY, NZ, NC), ("x", "y", "z", "core"))
    in_specs = (P(("x", "y", "z", "core"), None), P(), P())
    out_specs = P(None, "x", ("y", "z", "core"), None)
    return jax.shard_map(body, mesh=fine, in_specs=in_specs, out_specs=out_specs, check_vma=False)
```

```python
import functools
import math

import jax
import jax.numpy as jnp
from jax import lax
from jax.experimental import pallas as pl
from jax.experimental.pallas import tpu as pltpu
from jax.sharding import Mesh, PartitionSpec as P

TAPS = 4
P_SIZE = 128
INPUTS = 4096
KDIM = 8
CHANNELS = 12
SPECTRA = 768
LOADING = 0.5

NX, NY, NZ, NC = 4, 4, 4, 2
LOCAL = INPUTS // (NX * NY * NZ * NC)
GROUP = CHANNELS // NX
HELD = LOCAL * NX * NZ
PHASES = 6
ROWS = SPECTRA // PHASES
SPAN = (PHASES + TAPS - 1) * P_SIZE
SHARE = SPECTRA // (NY * NZ * NC)
RC = 2 * CHANNELS

F32, BF16 = jnp.float32, jnp.bfloat16


def params(mib):
    return pltpu.CompilerParams(vmem_limit_bytes=mib * 1024 * 1024)


def cost(microseconds):
    return pl.CostEstimate(flops=int(microseconds * 9e8), bytes_accessed=int(microseconds * 3e6), transcendentals=0)


in_vmem = pl.BlockSpec(memory_space=pltpu.VMEM)


def dot_nn(a, b):
    return lax.dot_general(a, b, (((1,), (0,)), ((), ())), preferred_element_type=F32)


def dot_nt(a, b):
    return lax.dot_general(a, b, (((1,), (1,)), ((), ())), preferred_element_type=F32)


def dot_tn(a, b, precision=None):
    return lax.dot_general(
        a, b, (((0,), (0,)), ((), ())), preferred_element_type=F32, precision=precision
    )


def split3(x):
    hi = x.astype(BF16)
    rest = x - hi.astype(F32)
    mid = rest.astype(BF16)
    lo = (rest - mid.astype(F32)).astype(BF16)
    return jnp.concatenate([hi, mid, lo], axis=0)


def sum3(x):
    n = x.shape[0] // 3
    return x[:n] + (x[n : 2 * n] + x[2 * n :])


STEP_ROWS = 32
CHUNKS = 2


def fill_table(ids_ref, turned):
    length = TAPS * P_SIZE
    shape = (TAPS, P_SIZE)
    at = (
        lax.broadcasted_iota(jnp.int32, shape, 0) * P_SIZE
        + lax.broadcasted_iota(jnp.int32, shape, 1)
    ).astype(F32)
    angle = math.pi * ((at + 0.5 - length / 2.0) / P_SIZE)
    window = jnp.sin(angle) / angle * (0.5 - 0.5 * jnp.cos(2.0 * math.pi * (at + 0.5) / length))
    window = window / jnp.sqrt(jnp.sum(window * window))
    row = lax.broadcasted_iota(jnp.int32, (RC, P_SIZE), 0)
    point = lax.broadcasted_iota(jnp.int32, (RC, P_SIZE), 1)
    channel = jnp.where(row >= CHANNELS, row - CHANNELS, row)
    ids = jnp.zeros((RC, P_SIZE), jnp.int32)
    for c in range(CHANNELS):
        ids = jnp.where(channel == c, ids_ref[c], ids)
    angles = 2.0 * math.pi / P_SIZE * ((ids * point) % P_SIZE).astype(F32)
    rotors = jnp.where(row < CHANNELS, jnp.cos(angles), -jnp.sin(angles))
    turned[...] = jnp.zeros((256, SPAN), F32)
    for m in range(TAPS):
        taps = window[m : m + 1] * rotors
        for q in range(PHASES):
            turned[q * RC : (q + 1) * RC, (q + m) * P_SIZE : (q + m + 1) * P_SIZE] = taps


def channelize_kernel(ids_ref, x_hbm, o_hbm, x_ref, o_ref, turned, table, wide, tall, sems, out_sems):
    step = ROWS // CHUNKS * PHASES * P_SIZE
    halo = (TAPS - 1) * P_SIZE
    copies = []
    for k in range(CHUNKS):
        low = k * step + (halo if k else 0)
        lanes = pl.ds(low, (k + 1) * step + halo - low)
        copies.append(
            pltpu.make_async_copy(x_hbm.at[:, lanes], x_ref.at[:, lanes], sems.at[k])
        )
        copies[-1].start()
    fill_table(ids_ref, turned)
    for k in range(SPAN // P_SIZE):
        lanes = slice(k * P_SIZE, (k + 1) * P_SIZE)
        table[lanes] = turned[:, lanes].T.astype(BF16)

    def filter_rows(at, carry):
        rows = []
        for k in range(STEP_ROWS):
            start = pl.multiple_of((at * STEP_ROWS + k) * (PHASES * P_SIZE), 128)
            rows.append(x_ref[:, pl.ds(start, SPAN)])
        got = dot_nn(jnp.concatenate(rows, axis=0), table[...])
        got = got.reshape(STEP_ROWS // 4, 4, LOCAL, 256)
        for k in range(STEP_ROWS // 4):
            owner = at * (STEP_ROWS // 4) + k
            y, z, core = owner // (NZ * NC), owner // NC % NZ, owner % NC
            wide[pl.ds((y * NC + core) * 16 + z * 4, 4)] = got[k]
        return carry

    for k in range(CHUNKS):
        copies[k].wait()
        each = ROWS // STEP_ROWS // CHUNKS
        lax.fori_loop(k * each, (k + 1) * each, filter_rows, 0)

    for n in range(LOCAL):
        turned_n = jnp.concatenate(
            [wide[:, n, 0:128].T, wide[:, n, 128:256].T[0 : PHASES * RC - 128]], axis=0
        )
        for q in range(PHASES):
            tall[:, n, q * 128 : (q + 1) * 128] = turned_n[q * RC : (q + 1) * RC]

    copies = []
    for x in range(NX):
        for z in range(NZ):
            for r in range(2):
                if z < GROUP:
                    o_ref[x * NZ + z, r] = tall[r * CHANNELS + x * GROUP + z].astype(BF16)
                else:
                    o_ref[x * NZ + z, r] = jnp.zeros((LOCAL, SPECTRA), BF16)
        part = pl.ds(x * NZ, NZ)
        copies.append(pltpu.make_async_copy(o_ref.at[part], o_hbm.at[part], out_sems.at[x]))
        copies[-1].start()
    for copy in copies:
        copy.wait()


def channelize(ids, x):
    return pl.pallas_call(
        channelize_kernel,
        out_shape=jax.ShapeDtypeStruct((NX * NZ, 2, LOCAL, SPECTRA), BF16),
        in_specs=[pl.BlockSpec(memory_space=pltpu.SMEM), pl.BlockSpec(memory_space=pltpu.HBM)],
        out_specs=pl.BlockSpec(memory_space=pltpu.HBM),
        scratch_shapes=[
            pltpu.VMEM(x.shape, BF16),
            pltpu.VMEM((NX * NZ, 2, LOCAL, SPECTRA), BF16),
            pltpu.VMEM((256, SPAN), F32),
            pltpu.VMEM((SPAN, 256), BF16),
            pltpu.VMEM((ROWS, LOCAL, 256), F32),
            pltpu.VMEM((RC, LOCAL, SPECTRA), F32),
            pltpu.SemaphoreType.DMA((CHUNKS,)),
            pltpu.SemaphoreType.DMA((NX,)),
        ],
        compiler_params=params(58),
        cost_estimate=cost(8),
    )(ids, x)


PAD = 128
TURN_ROWS = GROUP * 2 * SHARE


def spread_kernel(y_ref, v_ref, *outs):
    row = lax.broadcasted_iota(jnp.int32, (SPECTRA, NC * PAD), 0)
    col = lax.broadcasted_iota(jnp.int32, (1, NC * PAD), 1)
    inside = col % PAD
    wanted = (inside // 16) * ROWS + (col // PAD) * 16 + inside % 16
    wanted = jnp.where(inside < PHASES * 16, wanted, -SPECTRA)
    rows = [v_ref[c // GROUP * NZ + c % GROUP].reshape(2 * LOCAL, SPECTRA) for c in range(CHANNELS)]
    rows = jnp.concatenate(rows, axis=0)
    for d in range(NY):
        y = (y_ref[0] + d) % NY
        pick = jnp.where(row == wanted + y * (NC * 16), 1.0, 0.0).astype(BF16)
        got = dot_nn(rows, pick).astype(BF16).reshape(RC, LOCAL, NC * PAD)
        for core in range(NC):
            outs[d][core] = got[:, :, core * PAD : (core + 1) * PAD]


def spread(y, v):
    return pl.pallas_call(
        spread_kernel,
        out_shape=[jax.ShapeDtypeStruct((NC, RC, LOCAL, PAD), BF16)] * NY,
        in_specs=[pl.BlockSpec(memory_space=pltpu.SMEM), in_vmem],
        out_specs=[in_vmem] * NY,
        compiler_params=params(16),
        cost_estimate=cost(4),
    )(y, v)


def turn_kernel(at_ref, *refs):
    parts, o_ref = refs[:-1], refs[-1]
    core = at_ref[1]
    row = lax.broadcasted_iota(jnp.int32, (NZ * SHARE, PAD), 0)
    col = lax.broadcasted_iota(jnp.int32, (NZ * SHARE, PAD), 1)
    z, s = row // SHARE, row % SHARE
    pick = (col == (s % PHASES) * 16 + z * 4 + s // PHASES)
    pick = jnp.where(pick, 1.0, 0.0).astype(BF16)
    for other in range(NC):
        side = core if other == 0 else 1 - core
        for x in range(NX):
            blocks = []
            for rc in range(0, 2 * GROUP, 2):
                at = x * 2 * GROUP + rc
                stack = jnp.concatenate(
                    [parts[d][side, at + k] for k in range(2) for d in range(NY)], axis=0
                )
                got = dot_nt(pick, stack)
                blocks += [got[:, 0 : NY * LOCAL], got[:, NY * LOCAL :]]
            for z_to in range(NZ):
                rows = slice(z_to * SHARE, (z_to + 1) * SHARE)
                o_ref[x * NZ + z_to, other] = jnp.concatenate(
                    [g[rows] for g in blocks], axis=0
                ).astype(BF16)


def turn(at, parts):
    return pl.pallas_call(
        turn_kernel,
        out_shape=jax.ShapeDtypeStruct((NX * NZ, NC, TURN_ROWS, NY * LOCAL), BF16),
        in_specs=[pl.BlockSpec(memory_space=pltpu.SMEM)] + [in_vmem] * NY,
        out_specs=in_vmem,
        compiler_params=params(16),
        cost_estimate=cost(3),
    )(at, *parts)


def halves(v_ref):
    return v_ref[:, 0].reshape(HELD, SPECTRA), v_ref[:, 1].reshape(HELD, SPECTRA)


def project(v_halves, pieces):
    a, b = sum3(dot_nn(pieces, v_halves[0])), sum3(dot_nn(pieces, v_halves[1]))
    return a[0:KDIM] + b[KDIM:], a[KDIM:] - b[0:KDIM]


def expand(v_halves, pieces):
    a, b = sum3(dot_nt(pieces, v_halves[0])), sum3(dot_nt(pieces, v_halves[1]))
    return a[0:KDIM] - b[KDIM:], a[KDIM:] + b[0:KDIM]


def gram_from(products):
    p0, p1, p2 = products[0:16], products[16:32], products[32:48]
    m = (p0 + (p1 + p2)) + pltpu.roll(p0 + p1, 112, 1) + pltpu.roll(p0, 96, 1)
    up, down = m[0:KDIM], m[KDIM:]
    return up + pltpu.roll(down, 120, 1), down - pltpu.roll(up, 120, 1)


def eliminate(gram, others):
    row_id = lax.broadcasted_iota(jnp.int32, gram[0].shape[:-1] + (1,), gram[0].ndim - 2)
    pairs = [gram] + list(others)
    for j in range(KDIM):
        gram_re, gram_im = pairs[0]
        scale = 1.0 / jnp.sqrt(gram_re[..., j : j + 1, j : j + 1])
        below = jnp.where(row_id > j, scale, 0.0)
        m_re, m_im = gram_re[..., j : j + 1] * below, gram_im[..., j : j + 1] * below
        done = []
        for re, im in pairs:
            top_re, top_im = re[..., j : j + 1, :] * scale, im[..., j : j + 1, :] * scale
            new_re = re - (m_re * top_re - m_im * top_im)
            new_im = im - (m_re * top_im + m_im * top_re)
            here = row_id == j
            done.append((jnp.where(here, top_re, new_re), jnp.where(here, top_im, new_im)))
        pairs = done
    return pairs


def first_kernel(v_ref, q_ref, s_ref):
    u_re, u_im = project(halves(v_ref), split3(q_ref[...]))
    s_ref[...] = jnp.concatenate([u_re, u_im], axis=0)


def step_kernel(step, v_ref, z_ref, s0, s1, s2, s3, *outs):
    s = (s0[...] + s2[...]) + (s1[...] + s3[...])
    w = (s[0:KDIM, 0:SPECTRA], s[KDIM:, 0:SPECTRA])
    q = (z_ref[0:KDIM], z_ref[KDIM:])
    if step > 0:
        gram = (s[0:KDIM, SPECTRA:], s[KDIM:, SPECTRA:])
        _, w, q = eliminate(gram, [w, q])
    v = halves(v_ref)
    i_re, i_im = expand(v, split3(jnp.concatenate(w, axis=0)))
    z_re = i_re * (1.0 / SPECTRA) + LOADING * q[0]
    z_im = i_im * (1.0 / SPECTRA) + LOADING * q[1]
    z = jnp.concatenate([z_re, z_im], axis=0)
    if step == 2:
        (many_ref,) = outs
        for d in range(NY * NZ):
            many_ref[d] = z
        return
    new_z, new_s = outs
    new_z[...] = z
    pieces = split3(z)
    u_re, u_im = project(v, pieces)
    padded = jnp.concatenate([pieces, jnp.zeros((80, HELD), BF16)], axis=0)
    g_re, g_im = gram_from(dot_nt(pieces, padded))
    new_s[0:KDIM, 0:SPECTRA] = u_re
    new_s[KDIM:, 0:SPECTRA] = u_im
    new_s[0:KDIM, SPECTRA:] = g_re
    new_s[KDIM:, SPECTRA:] = g_im


def first(v, q):
    return pl.pallas_call(
        first_kernel,
        out_shape=jax.ShapeDtypeStruct((2 * KDIM, SPECTRA), F32),
        in_specs=[in_vmem] * 2,
        out_specs=in_vmem,
        compiler_params=params(12),
        cost_estimate=cost(2),
    )(v, q)


def step(at, v, z, sums):
    if at == 2:
        shapes = [jax.ShapeDtypeStruct((NY * NZ, 2 * KDIM, HELD), F32)]
    else:
        shapes = [
            jax.ShapeDtypeStruct((2 * KDIM, HELD), F32),
            jax.ShapeDtypeStruct((2 * KDIM, SPECTRA + 128), F32),
        ]
    return pl.pallas_call(
        functools.partial(step_kernel, at),
        out_shape=shapes,
        in_specs=[in_vmem] * 6,
        out_specs=[in_vmem] * len(shapes),
        compiler_params=params(12),
        cost_estimate=cost(5),
    )(v, z, *sums)


def placing(y, core):
    side = NY * NZ * NC * LOCAL
    row = lax.broadcasted_iota(jnp.int32, (side, side), 0)
    col = lax.broadcasted_iota(jnp.int32, (side, side), 1)
    to_y, to_z, to_core, i = col // 256, (col // 64) % 4, (col // 32) % 2, col % 32
    source = to_z * 256 + ((to_core + core) % 2) * 128 + ((y - to_y) % 4) * 32 + i
    return jnp.where(row == source, 1.0, 0.0).astype(BF16)


def arrange_kernel(mine_ref, theirs_ref, place_ref, flat, done):
    done[...] = jnp.zeros((8, 128), F32)
    rows = []
    for x in range(NX):
        parts = []
        for z in range(NZ):
            parts += [mine_ref[x * NZ + z], theirs_ref[x * NZ + z]]
        rows.append(jnp.concatenate(parts, axis=1))
    got = dot_nn(jnp.concatenate(rows, axis=0), place_ref[...])
    flat[...] = got.astype(BF16).reshape(NX, GROUP, 2 * SHARE, NY * 256)


def arrange(mine, theirs, place):
    return pl.pallas_call(
        arrange_kernel,
        out_shape=[
            jax.ShapeDtypeStruct((NX, GROUP, 2 * SHARE, NY * 256), BF16),
            jax.ShapeDtypeStruct((8, 128), F32),
        ],
        in_specs=[in_vmem] * 3,
        out_specs=[in_vmem] * 2,
        compiler_params=params(16),
        cost_estimate=cost(4),
    )(mine, theirs, place)


def final_kernel(flat, own_ref, far_ref, core_ref, done_ref, o_hbm, basis, result, sems):
    lane = lax.broadcasted_iota(jnp.int32, (2 * KDIM, 128), 1) // 32
    is_zero = core_ref[1] == 0
    wide = NY * 256
    solved = []
    for z in range(GROUP):
        products = jnp.zeros((48, 128), F32)
        for x in range(NX):
            lanes = slice(x * 128, (x + 1) * 128)
            for y in range(NY):
                own, far = own_ref[y * NZ + z, :, lanes], far_ref[y * NZ + z, :, lanes]
                a, b = jnp.where(is_zero, own, far), jnp.where(is_zero, far, own)
                left = jnp.where(
                    lane < 2,
                    jnp.where(lane == 0, a, pltpu.roll(b, 32, 1)),
                    jnp.where(lane == 2, pltpu.roll(a, 32, 1), pltpu.roll(b, 64, 1)),
                )
                right = jnp.where(
                    lane < 2,
                    jnp.where(lane == 0, pltpu.roll(a, 64, 1), pltpu.roll(b, 96, 1)),
                    jnp.where(lane == 2, pltpu.roll(a, 96, 1), b),
                )
                at = (x * NY + y) * 256
                for k, part in enumerate((left, right)):
                    basis[z, :, at + k * 128 : at + (k + 1) * 128] = split3(part)
            pieces = basis[z, :, x * wide : (x + 1) * wide]
            block = flat[x, z]
            right = jnp.concatenate([pieces, block, jnp.zeros((32, wide), BF16)], axis=0)
            products = products + dot_nt(pieces, right)
        g_re, g_im = gram_from(products)
        up_down = sum3(products)
        up, down = up_down[0:KDIM], up_down[KDIM:]
        u_re = up + pltpu.roll(down, 104, 1)
        u_im = down - pltpu.roll(up, 104, 1)
        solved.append((g_re, g_im, u_re, u_im))

    lane = lax.broadcasted_iota(jnp.int32, (KDIM, 128), 1)
    unit = lane == lax.broadcasted_iota(jnp.int32, (KDIM, 128), 0) + KDIM
    unit_lanes = (lane >= KDIM) & (lane < 2 * KDIM)
    u_lanes = (lane >= 48) & (lane < 72)
    used = lane < 72
    all_re, all_im = [], []
    for g_re, g_im, u_re, u_im in solved:
        x_re = jnp.where(u_lanes, u_re, jnp.where(unit_lanes, jnp.where(unit, 1.0, 0.0), g_re))
        x_im = jnp.where(u_lanes, u_im, jnp.where(unit_lanes, 0.0, g_im))
        all_re.append(jnp.where(used, x_re, 0.0))
        all_im.append(jnp.where(used, x_im, 0.0))
    ((all_re, all_im),) = eliminate((jnp.stack(all_re), jnp.stack(all_im)), [])

    def sides(a, b):
        near, away = pltpu.roll(a, 80, 1), pltpu.roll(b, 104, 1)
        return jnp.where(lane < SHARE, near, jnp.where(lane < 2 * SHARE, away, 0.0))

    lefts = []
    for z in range(GROUP):
        x_re, x_im = all_re[z], all_im[z]
        both = jnp.concatenate([x_re, x_im], axis=0)
        cross = jnp.concatenate([x_im, -x_re], axis=0)
        t_re = dot_tn(both, both, lax.Precision.HIGHEST)[KDIM : 2 * KDIM]
        t_im = dot_tn(cross, both, lax.Precision.HIGHEST)[KDIM : 2 * KDIM]
        t = split3(jnp.concatenate([sides(t_re, t_im), sides(-t_im, t_re)], axis=0))
        hi, mid, lo = t[0:16], t[16:32], t[32:48]
        lefts.append(jnp.concatenate([hi, hi, hi, mid, mid, lo], axis=0))
    copies = []
    for z in range(GROUP):
        for x in range(NX):
            lanes = slice(x * wide, (x + 1) * wide)
            pieces = basis[z, :, lanes]
            right = jnp.concatenate([pieces, pieces[0:32], pieces[0:16]], axis=0)
            rest = flat[x, z].astype(F32) - dot_tn(lefts[z], right)[0 : 2 * SHARE]
            result[0, z, :, lanes] = rest[0:SHARE]
            result[1, z, :, lanes] = rest[SHARE:]
        for r in range(2):
            copies.append(
                pltpu.make_async_copy(result.at[r, z], o_hbm.at[r, z], sems.at[r, z])
            )
            copies[-1].start()
    for copy in copies:
        copy.wait()


def finish(flat, own, far, at, done):
    return pl.pallas_call(
        final_kernel,
        out_shape=jax.ShapeDtypeStruct((2, GROUP, SHARE, INPUTS), F32),
        in_specs=[in_vmem] * 3 + [pl.BlockSpec(memory_space=pltpu.SMEM), in_vmem],
        out_specs=pl.BlockSpec(memory_space=pltpu.HBM),
        scratch_shapes=[
            pltpu.VMEM((GROUP, 6 * KDIM, INPUTS), BF16),
            pltpu.VMEM((2, GROUP, SHARE, INPUTS), F32),
            pltpu.SemaphoreType.DMA((2, GROUP)),
        ],
        compiler_params=params(16),
        cost_estimate=cost(6),
    )(flat, own, far, at, done)


def turned_by(count, distance):
    return [(i, (i + distance) % count) for i in range(count)]


def sums_over(s):
    return [s] + [lax.ppermute(s, "y", turned_by(NY, d)) for d in range(1, NY)]


def core_sum(s):
    return s + lax.ppermute(s, "core", turned_by(NC, 1))


def body(voltages, channel_ids, start_basis):
    y, core = lax.axis_index("y"), lax.axis_index("core")
    at = jnp.stack([y, core]).astype(jnp.int32)
    parcels = channelize(channel_ids, voltages)
    v = lax.all_to_all(parcels, ("x", "z"), 0, 0, tiled=True)
    parts = spread(at, parcels)
    parts = [parts[0]] + [lax.ppermute(parts[d], "y", turned_by(NY, d)) for d in range(1, NY)]
    turned = turn(at, parts)
    split = start_basis.reshape(2 * KDIM, NX, NY, NZ, NC, LOCAL)
    split = lax.dynamic_index_in_dim(split, y, 2, keepdims=False)
    z = lax.dynamic_index_in_dim(split, core, 3, keepdims=False).reshape(2 * KDIM, HELD)
    s = core_sum(first(v, z))
    sums = sums_over(s)
    turned = lax.optimization_barrier((turned, s))[0]
    blocks = lax.all_to_all(turned, ("x", "z"), 0, 0, tiled=True)
    place = placing(y, core)
    z, s = step(0, v, z, sums)
    z, s = step(1, v, z, sums_over(core_sum(s)))
    sums = sums_over(core_sum(s))
    tail, blocks = lax.optimization_barrier((sums[3], blocks))
    (many,) = step(2, v, z, sums[:3] + [tail])
    own = lax.all_to_all(many, ("y", "z"), 0, 0, tiled=True)
    mine, theirs = blocks[:, 0], lax.ppermute(blocks[:, 1], "core", turned_by(NC, 1))
    flat, done = arrange(mine, theirs, place)
    own, done = lax.optimization_barrier((own, done))
    far = lax.ppermute(own, "core", turned_by(NC, 1))
    return finish(flat, own, far, at, done)


def solution(mesh):
    fine = Mesh(mesh.devices.reshape(NX, NY, NZ, NC), ("x", "y", "z", "core"))
    in_specs = (P(("x", "y", "z", "core"), None), P(), P())
    out_specs = P(None, "x", ("y", "z", "core"), None)
    return jax.shard_map(body, mesh=fine, in_specs=in_specs, out_specs=out_specs, check_vma=False)
```

```python
import functools
import math

import jax
import jax.numpy as jnp
from jax import lax
from jax.experimental import pallas as pl
from jax.experimental.pallas import tpu as pltpu
from jax.sharding import Mesh, PartitionSpec as P

TAPS = 4
P_SIZE = 128
INPUTS = 4096
KDIM = 8
CHANNELS = 12
SPECTRA = 768
LOADING = 0.5

NX, NY, NZ, NC = 4, 4, 4, 2
LOCAL = INPUTS // (NX * NY * NZ * NC)
GROUP = CHANNELS // NX
HELD = LOCAL * NX * NZ
PHASES = 6
ROWS = SPECTRA // PHASES
SPAN = (PHASES + TAPS - 1) * P_SIZE
SHARE = SPECTRA // (NY * NZ * NC)
RC = 2 * CHANNELS

F32, BF16 = jnp.float32, jnp.bfloat16


def params(mib):
    return pltpu.CompilerParams(vmem_limit_bytes=mib * 1024 * 1024)


def cost(microseconds):
    return pl.CostEstimate(flops=int(microseconds * 9e8), bytes_accessed=int(microseconds * 3e6), transcendentals=0)


in_vmem = pl.BlockSpec(memory_space=pltpu.VMEM)


def dot_nn(a, b):
    return lax.dot_general(a, b, (((1,), (0,)), ((), ())), preferred_element_type=F32)


def dot_nt(a, b):
    return lax.dot_general(a, b, (((1,), (1,)), ((), ())), preferred_element_type=F32)


def dot_tn(a, b, precision=None):
    return lax.dot_general(
        a, b, (((0,), (0,)), ((), ())), preferred_element_type=F32, precision=precision
    )


def split3(x):
    hi = x.astype(BF16)
    rest = x - hi.astype(F32)
    mid = rest.astype(BF16)
    lo = (rest - mid.astype(F32)).astype(BF16)
    return jnp.concatenate([hi, mid, lo], axis=0)


def sum3(x):
    n = x.shape[0] // 3
    return x[:n] + (x[n : 2 * n] + x[2 * n :])


STEP_ROWS = 32
CHUNKS = 2


def fill_table(ids_ref, turned):
    length = TAPS * P_SIZE
    shape = (TAPS, P_SIZE)
    at = (
        lax.broadcasted_iota(jnp.int32, shape, 0) * P_SIZE
        + lax.broadcasted_iota(jnp.int32, shape, 1)
    ).astype(F32)
    angle = math.pi * ((at + 0.5 - length / 2.0) / P_SIZE)
    window = jnp.sin(angle) / angle * (0.5 - 0.5 * jnp.cos(2.0 * math.pi * (at + 0.5) / length))
    window = window / jnp.sqrt(jnp.sum(window * window))
    row = lax.broadcasted_iota(jnp.int32, (RC, P_SIZE), 0)
    point = lax.broadcasted_iota(jnp.int32, (RC, P_SIZE), 1)
    channel = jnp.where(row >= CHANNELS, row - CHANNELS, row)
    ids = jnp.zeros((RC, P_SIZE), jnp.int32)
    for c in range(CHANNELS):
        ids = jnp.where(channel == c, ids_ref[c], ids)
    angles = 2.0 * math.pi / P_SIZE * ((ids * point) % P_SIZE).astype(F32)
    rotors = jnp.where(row < CHANNELS, jnp.cos(angles), -jnp.sin(angles))
    turned[...] = jnp.zeros((256, SPAN), F32)
    for m in range(TAPS):
        taps = window[m : m + 1] * rotors
        for q in range(PHASES):
            turned[q * RC : (q + 1) * RC, (q + m) * P_SIZE : (q + m + 1) * P_SIZE] = taps


def channelize_kernel(ids_ref, x_hbm, o_hbm, x_ref, o_ref, turned, table, wide, tall, sems, out_sems):
    step = ROWS // CHUNKS * PHASES * P_SIZE
    halo = (TAPS - 1) * P_SIZE
    copies = []
    for k in range(CHUNKS):
        low = k * step + (halo if k else 0)
        lanes = pl.ds(low, (k + 1) * step + halo - low)
        copies.append(
            pltpu.make_async_copy(x_hbm.at[:, lanes], x_ref.at[:, lanes], sems.at[k])
        )
        copies[-1].start()
    fill_table(ids_ref, turned)
    for k in range(SPAN // P_SIZE):
        lanes = slice(k * P_SIZE, (k + 1) * P_SIZE)
        table[lanes] = turned[:, lanes].T.astype(BF16)

    def filter_rows(at, carry):
        rows = []
        for k in range(STEP_ROWS):
            start = pl.multiple_of((at * STEP_ROWS + k) * (PHASES * P_SIZE), 128)
            rows.append(x_ref[:, pl.ds(start, SPAN)])
        got = dot_nn(jnp.concatenate(rows, axis=0), table[...])
        got = got.reshape(STEP_ROWS // 4, 4, LOCAL, 256)
        for k in range(STEP_ROWS // 4):
            owner = at * (STEP_ROWS // 4) + k
            y, z, core = owner // (NZ * NC), owner // NC % NZ, owner % NC
            wide[pl.ds((y * NC + core) * 16 + z * 4, 4)] = got[k]
        return carry

    for k in range(CHUNKS):
        copies[k].wait()
        each = ROWS // STEP_ROWS // CHUNKS
        lax.fori_loop(k * each, (k + 1) * each, filter_rows, 0)

    for n in range(LOCAL):
        turned_n = jnp.concatenate(
            [wide[:, n, 0:128].T, wide[:, n, 128:256].T[0 : PHASES * RC - 128]], axis=0
        )
        for q in range(PHASES):
            tall[:, n, q * 128 : (q + 1) * 128] = turned_n[q * RC : (q + 1) * RC]

    copies = []
    for x in range(NX):
        for z in range(NZ):
            for r in range(2):
                if z < GROUP:
                    o_ref[x * NZ + z, r] = tall[r * CHANNELS + x * GROUP + z].astype(BF16)
                else:
                    o_ref[x * NZ + z, r] = jnp.zeros((LOCAL, SPECTRA), BF16)
        part = pl.ds(x * NZ, NZ)
        copies.append(pltpu.make_async_copy(o_ref.at[part], o_hbm.at[part], out_sems.at[x]))
        copies[-1].start()
    for copy in copies:
        copy.wait()


def channelize(ids, x):
    return pl.pallas_call(
        channelize_kernel,
        out_shape=jax.ShapeDtypeStruct((NX * NZ, 2, LOCAL, SPECTRA), BF16),
        in_specs=[pl.BlockSpec(memory_space=pltpu.SMEM), pl.BlockSpec(memory_space=pltpu.HBM)],
        out_specs=pl.BlockSpec(memory_space=pltpu.HBM),
        scratch_shapes=[
            pltpu.VMEM(x.shape, BF16),
            pltpu.VMEM((NX * NZ, 2, LOCAL, SPECTRA), BF16),
            pltpu.VMEM((256, SPAN), F32),
            pltpu.VMEM((SPAN, 256), BF16),
            pltpu.VMEM((ROWS, LOCAL, 256), F32),
            pltpu.VMEM((RC, LOCAL, SPECTRA), F32),
            pltpu.SemaphoreType.DMA((CHUNKS,)),
            pltpu.SemaphoreType.DMA((NX,)),
        ],
        compiler_params=params(58),
        cost_estimate=cost(8),
    )(ids, x)


PAD = 128
TURN_ROWS = GROUP * 2 * SHARE


def spread_kernel(y_ref, v_ref, *outs):
    row = lax.broadcasted_iota(jnp.int32, (SPECTRA, NC * PAD), 0)
    col = lax.broadcasted_iota(jnp.int32, (1, NC * PAD), 1)
    inside = col % PAD
    wanted = (inside // 16) * ROWS + (col // PAD) * 16 + inside % 16
    wanted = jnp.where(inside < PHASES * 16, wanted, -SPECTRA)
    rows = [v_ref[c // GROUP * NZ + c % GROUP].reshape(2 * LOCAL, SPECTRA) for c in range(CHANNELS)]
    rows = jnp.concatenate(rows, axis=0)
    for d in range(NY):
        y = (y_ref[0] + d) % NY
        pick = jnp.where(row == wanted + y * (NC * 16), 1.0, 0.0).astype(BF16)
        got = dot_nn(rows, pick).astype(BF16).reshape(RC, LOCAL, NC * PAD)
        for core in range(NC):
            outs[d][core] = got[:, :, core * PAD : (core + 1) * PAD]


def spread(y, v):
    return pl.pallas_call(
        spread_kernel,
        out_shape=[jax.ShapeDtypeStruct((NC, RC, LOCAL, PAD), BF16)] * NY,
        in_specs=[pl.BlockSpec(memory_space=pltpu.SMEM), in_vmem],
        out_specs=[in_vmem] * NY,
        compiler_params=params(16),
        cost_estimate=cost(4),
    )(y, v)


def turn_kernel(at_ref, *refs):
    parts, o_ref = refs[:-1], refs[-1]
    core = at_ref[1]
    row = lax.broadcasted_iota(jnp.int32, (NZ * SHARE, PAD), 0)
    col = lax.broadcasted_iota(jnp.int32, (NZ * SHARE, PAD), 1)
    z, s = row // SHARE, row % SHARE
    pick = (col == (s % PHASES) * 16 + z * 4 + s // PHASES)
    pick = jnp.where(pick, 1.0, 0.0).astype(BF16)
    for other in range(NC):
        side = core if other == 0 else 1 - core
        for x in range(NX):
            blocks = []
            for rc in range(0, 2 * GROUP, 2):
                at = x * 2 * GROUP + rc
                stack = jnp.concatenate(
                    [parts[d][side, at + k] for k in range(2) for d in range(NY)], axis=0
                )
                got = dot_nt(pick, stack)
                blocks += [got[:, 0 : NY * LOCAL], got[:, NY * LOCAL :]]
            for z_to in range(NZ):
                rows = slice(z_to * SHARE, (z_to + 1) * SHARE)
                o_ref[x * NZ + z_to, other] = jnp.concatenate(
                    [g[rows] for g in blocks], axis=0
                ).astype(BF16)


def turn(at, parts):
    return pl.pallas_call(
        turn_kernel,
        out_shape=jax.ShapeDtypeStruct((NX * NZ, NC, TURN_ROWS, NY * LOCAL), BF16),
        in_specs=[pl.BlockSpec(memory_space=pltpu.SMEM)] + [in_vmem] * NY,
        out_specs=in_vmem,
        compiler_params=params(16),
        cost_estimate=cost(3),
    )(at, *parts)


def halves(v_ref):
    return v_ref[:, 0].reshape(HELD, SPECTRA), v_ref[:, 1].reshape(HELD, SPECTRA)


def project(v_halves, pieces):
    a, b = sum3(dot_nn(pieces, v_halves[0])), sum3(dot_nn(pieces, v_halves[1]))
    return a[0:KDIM] + b[KDIM:], a[KDIM:] - b[0:KDIM]


def expand(v_halves, pieces):
    a, b = sum3(dot_nt(pieces, v_halves[0])), sum3(dot_nt(pieces, v_halves[1]))
    return a[0:KDIM] - b[KDIM:], a[KDIM:] + b[0:KDIM]


def gram_from(products):
    p0, p1, p2 = products[0:16], products[16:32], products[32:48]
    m = (p0 + (p1 + p2)) + pltpu.roll(p0 + p1, 112, 1) + pltpu.roll(p0, 96, 1)
    up, down = m[0:KDIM], m[KDIM:]
    return up + pltpu.roll(down, 120, 1), down - pltpu.roll(up, 120, 1)


def eliminate(gram, others):
    row_id = lax.broadcasted_iota(jnp.int32, gram[0].shape[:-1] + (1,), gram[0].ndim - 2)
    pairs = [gram] + list(others)
    for j in range(KDIM):
        gram_re, gram_im = pairs[0]
        scale = 1.0 / jnp.sqrt(gram_re[..., j : j + 1, j : j + 1])
        below = jnp.where(row_id > j, scale, 0.0)
        m_re, m_im = gram_re[..., j : j + 1] * below, gram_im[..., j : j + 1] * below
        done = []
        for re, im in pairs:
            top_re, top_im = re[..., j : j + 1, :] * scale, im[..., j : j + 1, :] * scale
            new_re = re - (m_re * top_re - m_im * top_im)
            new_im = im - (m_re * top_im + m_im * top_re)
            here = row_id == j
            done.append((jnp.where(here, top_re, new_re), jnp.where(here, top_im, new_im)))
        pairs = done
    return pairs


def first_kernel(v_ref, q_ref, s_ref):
    u_re, u_im = project(halves(v_ref), split3(q_ref[...]))
    s_ref[...] = jnp.concatenate([u_re, u_im], axis=0)


def step_kernel(step, v_ref, z_ref, s0, s1, s2, s3, *outs):
    s = (s0[...] + s2[...]) + (s1[...] + s3[...])
    w = (s[0:KDIM, 0:SPECTRA], s[KDIM:, 0:SPECTRA])
    q = (z_ref[0:KDIM], z_ref[KDIM:])
    if step > 0:
        gram = (s[0:KDIM, SPECTRA:], s[KDIM:, SPECTRA:])
        _, w, q = eliminate(gram, [w, q])
    v = halves(v_ref)
    i_re, i_im = expand(v, split3(jnp.concatenate(w, axis=0)))
    z_re = i_re * (1.0 / SPECTRA) + LOADING * q[0]
    z_im = i_im * (1.0 / SPECTRA) + LOADING * q[1]
    z = jnp.concatenate([z_re, z_im], axis=0)
    outs[0][...] = z
    if step == 2:
        return
    new_s = outs[1]
    pieces = split3(z)
    u_re, u_im = project(v, pieces)
    padded = jnp.concatenate([pieces, jnp.zeros((80, HELD), BF16)], axis=0)
    g_re, g_im = gram_from(dot_nt(pieces, padded))
    new_s[0:KDIM, 0:SPECTRA] = u_re
    new_s[KDIM:, 0:SPECTRA] = u_im
    new_s[0:KDIM, SPECTRA:] = g_re
    new_s[KDIM:, SPECTRA:] = g_im


def first(v, q):
    return pl.pallas_call(
        first_kernel,
        out_shape=jax.ShapeDtypeStruct((2 * KDIM, SPECTRA), F32),
        in_specs=[in_vmem] * 2,
        out_specs=in_vmem,
        compiler_params=params(12),
        cost_estimate=cost(2),
    )(v, q)


def step(at, v, z, sums):
    shapes = [jax.ShapeDtypeStruct((2 * KDIM, HELD), F32)]
    if at < 2:
        shapes.append(jax.ShapeDtypeStruct((2 * KDIM, SPECTRA + 128), F32))
    return pl.pallas_call(
        functools.partial(step_kernel, at),
        out_shape=shapes,
        in_specs=[in_vmem] * 6,
        out_specs=[in_vmem] * len(shapes),
        compiler_params=params(12),
        cost_estimate=cost(5),
    )(v, z, *sums)


def placing(y, core):
    side = NY * NZ * NC * LOCAL
    row = lax.broadcasted_iota(jnp.int32, (side, side), 0)
    col = lax.broadcasted_iota(jnp.int32, (side, side), 1)
    to_y, to_z, to_core, i = col // 256, (col // 64) % 4, (col // 32) % 2, col % 32
    source = to_z * 256 + ((to_core + core) % 2) * 128 + ((y - to_y) % 4) * 32 + i
    return jnp.where(row == source, 1.0, 0.0).astype(BF16)


def arrange_kernel(mine_ref, theirs_ref, place_ref, flat, done):
    done[...] = jnp.zeros((8, 128), F32)
    rows = []
    for x in range(NX):
        parts = []
        for z in range(NZ):
            parts += [mine_ref[x * NZ + z], theirs_ref[x * NZ + z]]
        rows.append(jnp.concatenate(parts, axis=1))
    got = dot_nn(jnp.concatenate(rows, axis=0), place_ref[...])
    flat[...] = got.astype(BF16).reshape(NX, GROUP, 2 * SHARE, NY * 256)


def arrange(mine, theirs, place):
    return pl.pallas_call(
        arrange_kernel,
        out_shape=[
            jax.ShapeDtypeStruct((NX, GROUP, 2 * SHARE, NY * 256), BF16),
            jax.ShapeDtypeStruct((8, 128), F32),
        ],
        in_specs=[in_vmem] * 3,
        out_specs=[in_vmem] * 2,
        compiler_params=params(16),
        cost_estimate=cost(4),
    )(mine, theirs, place)


def final_kernel(flat, *refs):
    own_refs, far_refs = refs[0:NY], refs[NY : 2 * NY]
    at_ref, _, o_hbm, basis, result, sems = refs[2 * NY :]
    lane = lax.broadcasted_iota(jnp.int32, (2 * KDIM, 128), 1) // 32
    is_zero = at_ref[1] == 0
    wide = NY * 256
    for d in range(NY):
        y = (at_ref[0] + NY - d) % NY
        for z in range(GROUP):
            from_z = (at_ref[2] + NZ - z) % NZ
            for x in range(NX):
                lanes = slice(x * 128, (x + 1) * 128)
                own, far = own_refs[d][from_z, :, lanes], far_refs[d][from_z, :, lanes]
                a, b = jnp.where(is_zero, own, far), jnp.where(is_zero, far, own)
                left = jnp.where(
                    lane < 2,
                    jnp.where(lane == 0, a, pltpu.roll(b, 32, 1)),
                    jnp.where(lane == 2, pltpu.roll(a, 32, 1), pltpu.roll(b, 64, 1)),
                )
                right = jnp.where(
                    lane < 2,
                    jnp.where(lane == 0, pltpu.roll(a, 64, 1), pltpu.roll(b, 96, 1)),
                    jnp.where(lane == 2, pltpu.roll(a, 96, 1), b),
                )
                for k, part in enumerate((left, right)):
                    start = pl.multiple_of(x * wide + y * 256 + k * 128, 128)
                    basis[z, :, pl.ds(start, 128)] = split3(part)
    solved = []
    for z in range(GROUP):
        products = jnp.zeros((48, 128), F32)
        for x in range(NX):
            pieces = basis[z, :, x * wide : (x + 1) * wide]
            block = flat[x, z]
            right = jnp.concatenate([pieces, block, jnp.zeros((32, wide), BF16)], axis=0)
            products = products + dot_nt(pieces, right)
        g_re, g_im = gram_from(products)
        up_down = sum3(products)
        up, down = up_down[0:KDIM], up_down[KDIM:]
        u_re = up + pltpu.roll(down, 104, 1)
        u_im = down - pltpu.roll(up, 104, 1)
        solved.append((g_re, g_im, u_re, u_im))

    lane = lax.broadcasted_iota(jnp.int32, (KDIM, 128), 1)
    unit = lane == lax.broadcasted_iota(jnp.int32, (KDIM, 128), 0) + KDIM
    unit_lanes = (lane >= KDIM) & (lane < 2 * KDIM)
    u_lanes = (lane >= 48) & (lane < 72)
    used = lane < 72
    all_re, all_im = [], []
    for g_re, g_im, u_re, u_im in solved:
        x_re = jnp.where(u_lanes, u_re, jnp.where(unit_lanes, jnp.where(unit, 1.0, 0.0), g_re))
        x_im = jnp.where(u_lanes, u_im, jnp.where(unit_lanes, 0.0, g_im))
        all_re.append(jnp.where(used, x_re, 0.0))
        all_im.append(jnp.where(used, x_im, 0.0))
    ((all_re, all_im),) = eliminate((jnp.stack(all_re), jnp.stack(all_im)), [])

    def sides(a, b):
        near, away = pltpu.roll(a, 80, 1), pltpu.roll(b, 104, 1)
        return jnp.where(lane < SHARE, near, jnp.where(lane < 2 * SHARE, away, 0.0))

    lefts = []
    for z in range(GROUP):
        x_re, x_im = all_re[z], all_im[z]
        both = jnp.concatenate([x_re, x_im], axis=0)
        cross = jnp.concatenate([x_im, -x_re], axis=0)
        t_re = dot_tn(both, both, lax.Precision.HIGHEST)[KDIM : 2 * KDIM]
        t_im = dot_tn(cross, both, lax.Precision.HIGHEST)[KDIM : 2 * KDIM]
        t = split3(jnp.concatenate([sides(t_re, t_im), sides(-t_im, t_re)], axis=0))
        hi, mid, lo = t[0:16], t[16:32], t[32:48]
        lefts.append(jnp.concatenate([hi, hi, hi, mid, mid, lo], axis=0))
    copies = []
    for z in range(GROUP):
        for x in range(NX):
            lanes = slice(x * wide, (x + 1) * wide)
            pieces = basis[z, :, lanes]
            right = jnp.concatenate([pieces, pieces[0:32], pieces[0:16]], axis=0)
            rest = flat[x, z].astype(F32) - dot_tn(lefts[z], right)[0 : 2 * SHARE]
            result[0, z, :, lanes] = rest[0:SHARE]
            result[1, z, :, lanes] = rest[SHARE:]
        for r in range(2):
            copies.append(
                pltpu.make_async_copy(result.at[r, z], o_hbm.at[r, z], sems.at[r, z])
            )
            copies[-1].start()
    for copy in copies:
        copy.wait()


def finish(flat, own, far, at, done):
    return pl.pallas_call(
        final_kernel,
        out_shape=jax.ShapeDtypeStruct((2, GROUP, SHARE, INPUTS), F32),
        in_specs=[in_vmem] * (1 + 2 * NY) + [pl.BlockSpec(memory_space=pltpu.SMEM), in_vmem],
        out_specs=pl.BlockSpec(memory_space=pltpu.HBM),
        scratch_shapes=[
            pltpu.VMEM((GROUP, 6 * KDIM, INPUTS), BF16),
            pltpu.VMEM((2, GROUP, SHARE, INPUTS), F32),
            pltpu.SemaphoreType.DMA((2, GROUP)),
        ],
        compiler_params=params(16),
        cost_estimate=cost(6),
    )(flat, *own, *far, at, done)


def turned_by(count, distance):
    return [(i, (i + distance) % count) for i in range(count)]


def sums_over(s):
    return [s] + [lax.ppermute(s, "y", turned_by(NY, d)) for d in range(1, NY)]


def core_sum(s):
    return s + lax.ppermute(s, "core", turned_by(NC, 1))


def body(voltages, channel_ids, start_basis):
    y, core = lax.axis_index("y"), lax.axis_index("core")
    at = jnp.stack([y, core, lax.axis_index("z")]).astype(jnp.int32)
    parcels = channelize(channel_ids, voltages)
    v = lax.all_to_all(parcels, ("x", "z"), 0, 0, tiled=True)
    parts = spread(at, parcels)
    parts = [parts[0]] + [lax.ppermute(parts[d], "y", turned_by(NY, d)) for d in range(1, NY)]
    split = start_basis.reshape(2 * KDIM, NX, NY, NZ, NC, LOCAL)
    split = lax.dynamic_index_in_dim(split, y, 2, keepdims=False)
    z = lax.dynamic_index_in_dim(split, core, 3, keepdims=False).reshape(2 * KDIM, HELD)
    place = placing(y, core)
    s = core_sum(first(v, z))
    sums = sums_over(s)
    *parts, tail = lax.optimization_barrier((*parts, sums[3]))
    z, s = step(0, v, z, sums[:3] + [tail])
    turned = turn(at, parts)
    s = core_sum(s)
    sums = sums_over(s)
    turned = lax.optimization_barrier((turned, s))[0]
    blocks = lax.all_to_all(turned, ("x", "z"), 0, 0, tiled=True)
    z, s = step(1, v, z, sums)
    (z,) = step(2, v, z, sums_over(core_sum(s)))
    mine, theirs = blocks[:, 0], lax.ppermute(blocks[:, 1], "core", turned_by(NC, 1))
    flat, done = arrange(mine, theirs, place)
    along_z = [z] + [lax.ppermute(z, "z", turned_by(NZ, d)) for d in range(1, NZ)]
    column = jnp.stack(along_z)
    own = [column] + [lax.ppermute(column, "y", turned_by(NY, d)) for d in range(1, NY)]
    *late, done = lax.optimization_barrier((*own[1:], done))
    own = own[:1] + late
    far = [lax.ppermute(part, "core", turned_by(NC, 1)) for part in own]
    return finish(flat, own, far, at, done)


def solution(mesh):
    fine = Mesh(mesh.devices.reshape(NX, NY, NZ, NC), ("x", "y", "z", "core"))
    in_specs = (P(("x", "y", "z", "core"), None), P(), P())
    out_specs = P(None, "x", ("y", "z", "core"), None)
    return jax.shard_map(body, mesh=fine, in_specs=in_specs, out_specs=out_specs, check_vma=False)
```

```python
import functools
import math

import jax
import jax.numpy as jnp
from jax import lax
from jax.experimental import pallas as pl
from jax.experimental.pallas import tpu as pltpu
from jax.sharding import Mesh, PartitionSpec as P

TAPS = 4
P_SIZE = 128
INPUTS = 4096
KDIM = 8
CHANNELS = 12
SPECTRA = 768
LOADING = 0.5

NX, NY, NZ, NC = 4, 4, 4, 2
LOCAL = INPUTS // (NX * NY * NZ * NC)
GROUP = CHANNELS // NX
HELD = LOCAL * NX * NZ
PHASES = 6
ROWS = SPECTRA // PHASES
SPAN = (PHASES + TAPS - 1) * P_SIZE
SHARE = SPECTRA // (NY * NZ * NC)
RC = 2 * CHANNELS

F32, BF16 = jnp.float32, jnp.bfloat16


def params(mib):
    return pltpu.CompilerParams(vmem_limit_bytes=mib * 1024 * 1024)


def cost(microseconds):
    return pl.CostEstimate(flops=int(microseconds * 9e8), bytes_accessed=int(microseconds * 3e6), transcendentals=0)


in_vmem = pl.BlockSpec(memory_space=pltpu.VMEM)


def dot_nn(a, b):
    return lax.dot_general(a, b, (((1,), (0,)), ((), ())), preferred_element_type=F32)


def dot_nt(a, b):
    return lax.dot_general(a, b, (((1,), (1,)), ((), ())), preferred_element_type=F32)


def dot_tn(a, b, precision=None):
    return lax.dot_general(
        a, b, (((0,), (0,)), ((), ())), preferred_element_type=F32, precision=precision
    )


def split3(x):
    hi = x.astype(BF16)
    rest = x - hi.astype(F32)
    mid = rest.astype(BF16)
    lo = (rest - mid.astype(F32)).astype(BF16)
    return jnp.concatenate([hi, mid, lo], axis=0)


def sum3(x):
    n = x.shape[0] // 3
    return x[:n] + (x[n : 2 * n] + x[2 * n :])


STEP_ROWS = 32
CHUNKS = 2


def fill_table(ids_ref, turned):
    length = TAPS * P_SIZE
    shape = (TAPS, P_SIZE)
    at = (
        lax.broadcasted_iota(jnp.int32, shape, 0) * P_SIZE
        + lax.broadcasted_iota(jnp.int32, shape, 1)
    ).astype(F32)
    angle = math.pi * ((at + 0.5 - length / 2.0) / P_SIZE)
    window = jnp.sin(angle) / angle * (0.5 - 0.5 * jnp.cos(2.0 * math.pi * (at + 0.5) / length))
    window = window / jnp.sqrt(jnp.sum(window * window))
    row = lax.broadcasted_iota(jnp.int32, (RC, P_SIZE), 0)
    point = lax.broadcasted_iota(jnp.int32, (RC, P_SIZE), 1)
    channel = jnp.where(row >= CHANNELS, row - CHANNELS, row)
    ids = jnp.zeros((RC, P_SIZE), jnp.int32)
    for c in range(CHANNELS):
        ids = jnp.where(channel == c, ids_ref[c], ids)
    angles = 2.0 * math.pi / P_SIZE * ((ids * point) % P_SIZE).astype(F32)
    rotors = jnp.where(row < CHANNELS, jnp.cos(angles), -jnp.sin(angles))
    turned[...] = jnp.zeros((256, SPAN), F32)
    for m in range(TAPS):
        taps = window[m : m + 1] * rotors
        for q in range(PHASES):
            turned[q * RC : (q + 1) * RC, (q + m) * P_SIZE : (q + m + 1) * P_SIZE] = taps


def channelize_kernel(ids_ref, x_hbm, o_hbm, x_ref, o_ref, turned, table, wide, tall, sems, out_sems):
    step = ROWS // CHUNKS * PHASES * P_SIZE
    halo = (TAPS - 1) * P_SIZE
    copies = []
    for k in range(CHUNKS):
        low = k * step + (halo if k else 0)
        lanes = pl.ds(low, (k + 1) * step + halo - low)
        copies.append(
            pltpu.make_async_copy(x_hbm.at[:, lanes], x_ref.at[:, lanes], sems.at[k])
        )
        copies[-1].start()
    fill_table(ids_ref, turned)
    for k in range(SPAN // P_SIZE):
        lanes = slice(k * P_SIZE, (k + 1) * P_SIZE)
        table[lanes] = turned[:, lanes].T.astype(BF16)

    def filter_rows(at, carry):
        rows = []
        for k in range(STEP_ROWS):
            start = pl.multiple_of((at * STEP_ROWS + k) * (PHASES * P_SIZE), 128)
            rows.append(x_ref[:, pl.ds(start, SPAN)])
        got = dot_nn(jnp.concatenate(rows, axis=0), table[...])
        got = got.reshape(STEP_ROWS // 4, 4, LOCAL, 256)
        for k in range(STEP_ROWS // 4):
            owner = at * (STEP_ROWS // 4) + k
            y, z, core = owner // (NZ * NC), owner // NC % NZ, owner % NC
            wide[pl.ds((y * NC + core) * 16 + z * 4, 4)] = got[k]
        return carry

    for k in range(CHUNKS):
        copies[k].wait()
        each = ROWS // STEP_ROWS // CHUNKS
        lax.fori_loop(k * each, (k + 1) * each, filter_rows, 0)

    for n in range(LOCAL):
        turned_n = jnp.concatenate(
            [wide[:, n, 0:128].T, wide[:, n, 128:256].T[0 : PHASES * RC - 128]], axis=0
        )
        for q in range(PHASES):
            tall[:, n, q * 128 : (q + 1) * 128] = turned_n[q * RC : (q + 1) * RC]

    copies = []
    for x in range(NX):
        for z in range(NZ):
            for r in range(2):
                if z < GROUP:
                    o_ref[x * NZ + z, r] = tall[r * CHANNELS + x * GROUP + z].astype(BF16)
                else:
                    o_ref[x * NZ + z, r] = jnp.zeros((LOCAL, SPECTRA), BF16)
        part = pl.ds(x * NZ, NZ)
        copies.append(pltpu.make_async_copy(o_ref.at[part], o_hbm.at[part], out_sems.at[x]))
        copies[-1].start()
    for copy in copies:
        copy.wait()


def channelize(ids, x):
    return pl.pallas_call(
        channelize_kernel,
        out_shape=jax.ShapeDtypeStruct((NX * NZ, 2, LOCAL, SPECTRA), BF16),
        in_specs=[pl.BlockSpec(memory_space=pltpu.SMEM), pl.BlockSpec(memory_space=pltpu.HBM)],
        out_specs=pl.BlockSpec(memory_space=pltpu.HBM),
        scratch_shapes=[
            pltpu.VMEM(x.shape, BF16),
            pltpu.VMEM((NX * NZ, 2, LOCAL, SPECTRA), BF16),
            pltpu.VMEM((256, SPAN), F32),
            pltpu.VMEM((SPAN, 256), BF16),
            pltpu.VMEM((ROWS, LOCAL, 256), F32),
            pltpu.VMEM((RC, LOCAL, SPECTRA), F32),
            pltpu.SemaphoreType.DMA((CHUNKS,)),
            pltpu.SemaphoreType.DMA((NX,)),
        ],
        compiler_params=params(58),
        cost_estimate=cost(8),
    )(ids, x)


PAD = 128
TURN_ROWS = GROUP * 2 * SHARE


def spread_kernel(y_ref, v_ref, *outs):
    row = lax.broadcasted_iota(jnp.int32, (SPECTRA, NC * PAD), 0)
    col = lax.broadcasted_iota(jnp.int32, (1, NC * PAD), 1)
    inside = col % PAD
    wanted = (inside // 16) * ROWS + (col // PAD) * 16 + inside % 16
    wanted = jnp.where(inside < PHASES * 16, wanted, -SPECTRA)
    rows = [v_ref[c // GROUP * NZ + c % GROUP].reshape(2 * LOCAL, SPECTRA) for c in range(CHANNELS)]
    rows = jnp.concatenate(rows, axis=0)
    for d in range(NY):
        y = (y_ref[0] + d) % NY
        pick = jnp.where(row == wanted + y * (NC * 16), 1.0, 0.0).astype(BF16)
        got = dot_nn(rows, pick).astype(BF16).reshape(RC, LOCAL, NC * PAD)
        for core in range(NC):
            outs[d][core] = got[:, :, core * PAD : (core + 1) * PAD]


def spread(y, v):
    return pl.pallas_call(
        spread_kernel,
        out_shape=[jax.ShapeDtypeStruct((NC, RC, LOCAL, PAD), BF16)] * NY,
        in_specs=[pl.BlockSpec(memory_space=pltpu.SMEM), in_vmem],
        out_specs=[in_vmem] * NY,
        compiler_params=params(16),
        cost_estimate=cost(4),
    )(y, v)


def turn_kernel(at_ref, *refs):
    parts, o_ref = refs[:-1], refs[-1]
    core = at_ref[1]
    row = lax.broadcasted_iota(jnp.int32, (NZ * SHARE, PAD), 0)
    col = lax.broadcasted_iota(jnp.int32, (NZ * SHARE, PAD), 1)
    z, s = row // SHARE, row % SHARE
    pick = (col == (s % PHASES) * 16 + z * 4 + s // PHASES)
    pick = jnp.where(pick, 1.0, 0.0).astype(BF16)
    for other in range(NC):
        side = core if other == 0 else 1 - core
        for x in range(NX):
            blocks = []
            for rc in range(0, 2 * GROUP, 2):
                at = x * 2 * GROUP + rc
                stack = jnp.concatenate(
                    [parts[d][side, at + k] for k in range(2) for d in range(NY)], axis=0
                )
                got = dot_nt(pick, stack)
                blocks += [got[:, 0 : NY * LOCAL], got[:, NY * LOCAL :]]
            for z_to in range(NZ):
                rows = slice(z_to * SHARE, (z_to + 1) * SHARE)
                o_ref[x * NZ + z_to, other] = jnp.concatenate(
                    [g[rows] for g in blocks], axis=0
                ).astype(BF16)


def turn(at, parts):
    return pl.pallas_call(
        turn_kernel,
        out_shape=jax.ShapeDtypeStruct((NX * NZ, NC, TURN_ROWS, NY * LOCAL), BF16),
        in_specs=[pl.BlockSpec(memory_space=pltpu.SMEM)] + [in_vmem] * NY,
        out_specs=in_vmem,
        compiler_params=params(16),
        cost_estimate=cost(3),
    )(at, *parts)


def halves(v_ref):
    return v_ref[:, 0].reshape(HELD, SPECTRA), v_ref[:, 1].reshape(HELD, SPECTRA)


def project(v_halves, pieces):
    a, b = sum3(dot_nn(pieces, v_halves[0])), sum3(dot_nn(pieces, v_halves[1]))
    return a[0:KDIM] + b[KDIM:], a[KDIM:] - b[0:KDIM]


def expand(v_halves, pieces):
    a, b = sum3(dot_nt(pieces, v_halves[0])), sum3(dot_nt(pieces, v_halves[1]))
    return a[0:KDIM] - b[KDIM:], a[KDIM:] + b[0:KDIM]


def gram_from(products):
    p0, p1, p2 = products[0:16], products[16:32], products[32:48]
    m = (p0 + (p1 + p2)) + pltpu.roll(p0 + p1, 112, 1) + pltpu.roll(p0, 96, 1)
    up, down = m[0:KDIM], m[KDIM:]
    return up + pltpu.roll(down, 120, 1), down - pltpu.roll(up, 120, 1)


def eliminate(gram, others):
    row_id = lax.broadcasted_iota(jnp.int32, gram[0].shape[:-1] + (1,), gram[0].ndim - 2)
    pairs = [gram] + list(others)
    for j in range(KDIM):
        gram_re, gram_im = pairs[0]
        scale = 1.0 / jnp.sqrt(gram_re[..., j : j + 1, j : j + 1])
        below = jnp.where(row_id > j, scale, 0.0)
        m_re, m_im = gram_re[..., j : j + 1] * below, gram_im[..., j : j + 1] * below
        done = []
        for re, im in pairs:
            top_re, top_im = re[..., j : j + 1, :] * scale, im[..., j : j + 1, :] * scale
            new_re = re - (m_re * top_re - m_im * top_im)
            new_im = im - (m_re * top_im + m_im * top_re)
            here = row_id == j
            done.append((jnp.where(here, top_re, new_re), jnp.where(here, top_im, new_im)))
        pairs = done
    return pairs


def first_kernel(v_ref, q_ref, s_ref):
    u_re, u_im = project(halves(v_ref), split3(q_ref[...]))
    s_ref[...] = jnp.concatenate([u_re, u_im], axis=0)


def step_kernel(step, v_ref, z_ref, s0, s1, s2, s3, *outs):
    s = (s0[...] + s2[...]) + (s1[...] + s3[...])
    w = (s[0:KDIM, 0:SPECTRA], s[KDIM:, 0:SPECTRA])
    q = (z_ref[0:KDIM], z_ref[KDIM:])
    if step > 0:
        gram = (s[0:KDIM, SPECTRA:], s[KDIM:, SPECTRA:])
        _, w, q = eliminate(gram, [w, q])
    v = halves(v_ref)
    i_re, i_im = expand(v, split3(jnp.concatenate(w, axis=0)))
    z_re = i_re * (1.0 / SPECTRA) + LOADING * q[0]
    z_im = i_im * (1.0 / SPECTRA) + LOADING * q[1]
    z = jnp.concatenate([z_re, z_im], axis=0)
    outs[0][...] = z
    if step == 2:
        return
    new_s = outs[1]
    pieces = split3(z)
    u_re, u_im = project(v, pieces)
    padded = jnp.concatenate([pieces, jnp.zeros((80, HELD), BF16)], axis=0)
    g_re, g_im = gram_from(dot_nt(pieces, padded))
    new_s[0:KDIM, 0:SPECTRA] = u_re
    new_s[KDIM:, 0:SPECTRA] = u_im
    new_s[0:KDIM, SPECTRA:] = g_re
    new_s[KDIM:, SPECTRA:] = g_im


def first(v, q):
    return pl.pallas_call(
        first_kernel,
        out_shape=jax.ShapeDtypeStruct((2 * KDIM, SPECTRA), F32),
        in_specs=[in_vmem] * 2,
        out_specs=in_vmem,
        compiler_params=params(12),
        cost_estimate=cost(2),
    )(v, q)


def step(at, v, z, sums):
    shapes = [jax.ShapeDtypeStruct((2 * KDIM, HELD), F32)]
    if at < 2:
        shapes.append(jax.ShapeDtypeStruct((2 * KDIM, SPECTRA + 128), F32))
    return pl.pallas_call(
        functools.partial(step_kernel, at),
        out_shape=shapes,
        in_specs=[in_vmem] * 6,
        out_specs=[in_vmem] * len(shapes),
        compiler_params=params(12),
        cost_estimate=cost(5),
    )(v, z, *sums)


def placing(y, core):
    side = NY * NZ * NC * LOCAL
    row = lax.broadcasted_iota(jnp.int32, (side, side), 0)
    col = lax.broadcasted_iota(jnp.int32, (side, side), 1)
    to_y, to_z, to_core, i = col // 256, (col // 64) % 4, (col // 32) % 2, col % 32
    source = to_z * 256 + ((to_core + core) % 2) * 128 + ((y - to_y) % 4) * 32 + i
    return jnp.where(row == source, 1.0, 0.0).astype(BF16)


def arrange_kernel(mine_ref, theirs_ref, place_ref, flat, done):
    done[...] = jnp.zeros((8, 128), F32)
    rows = []
    for x in range(NX):
        parts = []
        for z in range(NZ):
            parts += [mine_ref[x * NZ + z, 0], theirs_ref[x * NZ + z]]
        rows.append(jnp.concatenate(parts, axis=1))
    got = dot_nn(jnp.concatenate(rows, axis=0), place_ref[...])
    flat[...] = got.astype(BF16).reshape(NX, GROUP, 2 * SHARE, NY * 256)


def arrange(mine, theirs, place):
    return pl.pallas_call(
        arrange_kernel,
        out_shape=[
            jax.ShapeDtypeStruct((NX, GROUP, 2 * SHARE, NY * 256), BF16),
            jax.ShapeDtypeStruct((8, 128), F32),
        ],
        in_specs=[in_vmem] * 3,
        out_specs=[in_vmem] * 2,
        compiler_params=params(16),
        cost_estimate=cost(4),
    )(mine, theirs, place)


def final_kernel(flat, *refs):
    own_refs, far_refs = refs[0:NY], refs[NY : 2 * NY]
    at_ref, _, o_hbm, basis, result, sems = refs[2 * NY :]
    lane = lax.broadcasted_iota(jnp.int32, (2 * KDIM, 128), 1) // 32
    is_zero = at_ref[1] == 0
    wide = NY * 256
    for d in range(NY):
        y = (at_ref[0] + NY - d) % NY
        for z in range(GROUP):
            from_z = (at_ref[2] + NZ - z) % NZ
            for x in range(NX):
                lanes = slice(x * 128, (x + 1) * 128)
                own, far = own_refs[d][from_z, :, lanes], far_refs[d][from_z, :, lanes]
                a, b = jnp.where(is_zero, own, far), jnp.where(is_zero, far, own)
                left = jnp.where(
                    lane < 2,
                    jnp.where(lane == 0, a, pltpu.roll(b, 32, 1)),
                    jnp.where(lane == 2, pltpu.roll(a, 32, 1), pltpu.roll(b, 64, 1)),
                )
                right = jnp.where(
                    lane < 2,
                    jnp.where(lane == 0, pltpu.roll(a, 64, 1), pltpu.roll(b, 96, 1)),
                    jnp.where(lane == 2, pltpu.roll(a, 96, 1), b),
                )
                for k, part in enumerate((left, right)):
                    start = pl.multiple_of(x * wide + y * 256 + k * 128, 128)
                    basis[z, :, pl.ds(start, 128)] = split3(part)
    solved = []
    for z in range(GROUP):
        products = jnp.zeros((48, 128), F32)
        for x in range(NX):
            pieces = basis[z, :, x * wide : (x + 1) * wide]
            block = flat[x, z]
            right = jnp.concatenate([pieces, block, jnp.zeros((32, wide), BF16)], axis=0)
            products = products + dot_nt(pieces, right)
        g_re, g_im = gram_from(products)
        up_down = sum3(products)
        up, down = up_down[0:KDIM], up_down[KDIM:]
        u_re = up + pltpu.roll(down, 104, 1)
        u_im = down - pltpu.roll(up, 104, 1)
        solved.append((g_re, g_im, u_re, u_im))

    lane = lax.broadcasted_iota(jnp.int32, (KDIM, 128), 1)
    unit = lane == lax.broadcasted_iota(jnp.int32, (KDIM, 128), 0) + KDIM
    unit_lanes = (lane >= KDIM) & (lane < 2 * KDIM)
    u_lanes = (lane >= 48) & (lane < 72)
    used = lane < 72
    all_re, all_im = [], []
    for g_re, g_im, u_re, u_im in solved:
        x_re = jnp.where(u_lanes, u_re, jnp.where(unit_lanes, jnp.where(unit, 1.0, 0.0), g_re))
        x_im = jnp.where(u_lanes, u_im, jnp.where(unit_lanes, 0.0, g_im))
        all_re.append(jnp.where(used, x_re, 0.0))
        all_im.append(jnp.where(used, x_im, 0.0))
    ((all_re, all_im),) = eliminate((jnp.stack(all_re), jnp.stack(all_im)), [])

    def sides(a, b):
        near, away = pltpu.roll(a, 80, 1), pltpu.roll(b, 104, 1)
        return jnp.where(lane < SHARE, near, jnp.where(lane < 2 * SHARE, away, 0.0))

    lefts = []
    for z in range(GROUP):
        x_re, x_im = all_re[z], all_im[z]
        both = jnp.concatenate([x_re, x_im], axis=0)
        cross = jnp.concatenate([x_im, -x_re], axis=0)
        t_re = dot_tn(both, both, lax.Precision.HIGHEST)[KDIM : 2 * KDIM]
        t_im = dot_tn(cross, both, lax.Precision.HIGHEST)[KDIM : 2 * KDIM]
        t = split3(jnp.concatenate([sides(t_re, t_im), sides(-t_im, t_re)], axis=0))
        hi, mid, lo = t[0:16], t[16:32], t[32:48]
        lefts.append(jnp.concatenate([hi, hi, hi, mid, mid, lo], axis=0))
    copies = []
    for z in range(GROUP):
        for x in range(NX):
            lanes = slice(x * wide, (x + 1) * wide)
            pieces = basis[z, :, lanes]
            right = jnp.concatenate([pieces, pieces[0:32], pieces[0:16]], axis=0)
            rest = flat[x, z].astype(F32) - dot_tn(lefts[z], right)[0 : 2 * SHARE]
            result[0, z, :, lanes] = rest[0:SHARE]
            result[1, z, :, lanes] = rest[SHARE:]
        for r in range(2):
            copies.append(
                pltpu.make_async_copy(result.at[r, z], o_hbm.at[r, z], sems.at[r, z])
            )
            copies[-1].start()
    for copy in copies:
        copy.wait()


def finish(flat, own, far, at, done):
    return pl.pallas_call(
        final_kernel,
        out_shape=jax.ShapeDtypeStruct((2, GROUP, SHARE, INPUTS), F32),
        in_specs=[in_vmem] * (1 + 2 * NY) + [pl.BlockSpec(memory_space=pltpu.SMEM), in_vmem],
        out_specs=pl.BlockSpec(memory_space=pltpu.HBM),
        scratch_shapes=[
            pltpu.VMEM((GROUP, 6 * KDIM, INPUTS), BF16),
            pltpu.VMEM((2, GROUP, SHARE, INPUTS), F32),
            pltpu.SemaphoreType.DMA((2, GROUP)),
        ],
        compiler_params=params(16),
        cost_estimate=cost(6),
    )(flat, *own, *far, at, done)


def turned_by(count, distance):
    return [(i, (i + distance) % count) for i in range(count)]


def sums_over(s):
    return [s] + [lax.ppermute(s, "y", turned_by(NY, d)) for d in range(1, NY)]


def core_sum(s):
    return s + lax.ppermute(s, "core", turned_by(NC, 1))


def body(voltages, channel_ids, start_basis):
    y, core = lax.axis_index("y"), lax.axis_index("core")
    at = jnp.stack([y, core, lax.axis_index("z")]).astype(jnp.int32)
    parcels = channelize(channel_ids, voltages)
    v = lax.all_to_all(parcels, ("x", "z"), 0, 0, tiled=True)
    parts = spread(at, parcels)
    parts = [parts[0]] + [lax.ppermute(parts[d], "y", turned_by(NY, d)) for d in range(1, NY)]
    split = start_basis.reshape(2 * KDIM, NX, NY, NZ, NC, LOCAL)
    split = lax.dynamic_index_in_dim(split, y, 2, keepdims=False)
    z = lax.dynamic_index_in_dim(split, core, 3, keepdims=False).reshape(2 * KDIM, HELD)
    place = placing(y, core)
    s = core_sum(first(v, z))
    sums = sums_over(s)
    *parts, tail = lax.optimization_barrier((*parts, sums[3]))
    z, s = step(0, v, z, sums[:3] + [tail])
    turned = turn(at, parts)
    s = core_sum(s)
    sums = sums_over(s)
    turned = lax.optimization_barrier((turned, s))[0]
    blocks = lax.all_to_all(turned, ("x", "z"), 0, 0, tiled=True)
    z, s = step(1, v, z, sums)
    (z,) = step(2, v, z, sums_over(core_sum(s)))
    theirs = lax.ppermute(blocks[:, 1], "core", turned_by(NC, 1))
    flat, done = arrange(blocks, theirs, place)
    along_z = [z] + [lax.ppermute(z, "z", turned_by(NZ, d)) for d in range(1, NZ)]
    column = jnp.stack(along_z)
    own = [column] + [lax.ppermute(column, "y", turned_by(NY, d)) for d in range(1, NY)]
    *late, done = lax.optimization_barrier((*own[1:], done))
    own = own[:1] + late
    far = [lax.ppermute(part, "core", turned_by(NC, 1)) for part in own]
    return finish(flat, own, far, at, done)


def solution(mesh):
    fine = Mesh(mesh.devices.reshape(NX, NY, NZ, NC), ("x", "y", "z", "core"))
    in_specs = (P(("x", "y", "z", "core"), None), P(), P())
    out_specs = P(None, "x", ("y", "z", "core"), None)
    return jax.shard_map(body, mesh=fine, in_specs=in_specs, out_specs=out_specs, check_vma=False)
```
